32 devices in a mesh: slot: 8 (over z, y), pb: 4 (over x, core).
Axes of the slice: x: 2, y: 2, z: 4, core: 2. Of those that a mesh axis runs over, the one named last changes fastest.
Arguments:
- enc_input: bfloat16 [4, 8, 384, 1024], P('pb', 'slot'), may hold values from -6 to 6
- dec_input: bfloat16 [4, 8, 128, 1024], P('pb', 'slot'), may hold values from -6 to 6
- doc_scores: float32 [4, 8], P('pb', 'slot'), may hold values from -5 to 5
- owner: int32 [4, 8], P('pb', 'slot'), may hold values from 0 to 1, as said below
- targets: int32 [4, 2, 128], P('pb'), may hold values from 0 to 49151
- enc_attn: bfloat16 [4, 1024, 1024], P(None, 'pb'), may hold values from -0.1875 to 0.1875
- enc_up: bfloat16 [1024, 4096], P('pb'), may hold values from -0.1875 to 0.1875
- enc_down: bfloat16 [4096, 1024], P('pb'), may hold values from -0.09375 to 0.09375
- enc_up_bias: bfloat16 [4096], P('pb'), may hold values from -1.5 to 1.5
- enc_bias: bfloat16 [6, 1024], P(None, 'pb'), may hold values from -1.5 to 1.5
- enc_gain: bfloat16 [2, 1024], P(None, 'pb'), may hold values from 0.5 to 1.5
- dec_self: bfloat16 [4, 1024, 1024], P(None, 'pb'), may hold values from -0.1875 to 0.1875
- dec_cross: bfloat16 [4, 1024, 1024], P(None, 'pb'), may hold values from -0.1875 to 0.1875
- dec_up: bfloat16 [1024, 4096], P('pb'), may hold values from -0.1875 to 0.1875
- dec_down: bfloat16 [4096, 1024], P('pb'), may hold values from -0.09375 to 0.09375
- dec_up_bias: bfloat16 [4096], P('pb'), may hold values from -1.5 to 1.5
- dec_bias: bfloat16 [10, 1024], P(None, 'pb'), may hold values from -1.5 to 1.5
- dec_gain: bfloat16 [3, 1024], P(None, 'pb'), may hold values from 0.5 to 1.5
- embed: bfloat16 [49152, 1024], P(('slot', 'pb')), may hold values from -0.375 to 0.375
Outputs:
- loss: float32 [4], P('pb')
- enc_input_grad: float32 [4, 8, 384, 1024], P('pb', 'slot')
- dec_input_grad: float32 [4, 8, 128, 1024], P('pb', 'slot')
- doc_scores_grad: float32 [4, 8], P('pb', 'slot')
- enc_attn_grad: float32 [4, 1024, 1024], P(None, 'pb')
- enc_up_grad: float32 [1024, 4096], P('pb')
- enc_down_grad: float32 [4096, 1024], P('pb')
- enc_up_bias_grad: float32 [4096], P('pb')
- enc_bias_grad: float32 [6, 1024], P(None, 'pb')
- enc_gain_grad: float32 [2, 1024], P(None, 'pb')
- dec_self_grad: float32 [4, 1024, 1024], P(None, 'pb')
- dec_cross_grad: float32 [4, 1024, 1024], P(None, 'pb')
- dec_up_grad: float32 [1024, 4096], P('pb')
- dec_down_grad: float32 [4096, 1024], P('pb')
- dec_up_bias_grad: float32 [4096], P('pb')
- dec_bias_grad: float32 [10, 1024], P(None, 'pb')
- dec_gain_grad: float32 [3, 1024], P(None, 'pb')
- embed_grad: float32 [49152, 1024], P(('slot', 'pb'))
The draws below stay inside these ranges and needn't reach their ends.
Inputs may be any that keep to these rules, and one draw needn't show every extreme that they name: `owner`: in each group every question is served by between 2 and 6 slots, and one question by exactly 6; the slots of a question may lie anywhere along the group.
All inputs are finite; a program needn't handle non-finite values.
Results may differ from the reference program's by a relative error of at most 0.019.
Values may be sent and summed in bfloat16 or wider, within the bound.
A program may use at most 576 MiB of HBM per device.

```python
import math
import jax
import jax.numpy as jnp
import numpy as np
from jax import lax

D = 1024
FF = 4096
HEADS = 16
HEAD_DIM = 64
VOCAB = 49152
SRC_LEN = 384
TGT_LEN = 128
GROUPS = 4
SLOTS = 8
QUESTIONS = 2
MOST_SLOTS = 6


def draw_owner(key, part):
    key = jax.random.fold_in(key, 7)
    spare = SLOTS - MOST_SLOTS - 2 * (QUESTIONS - 1)

    def one_group(group_key):
        pick_key, unit_key, order_key = jax.random.split(group_key, 3)
        busiest = jax.random.randint(pick_key, (), 0, QUESTIONS)
        offsets = jax.random.randint(unit_key, (max(spare, 1),), 1, QUESTIONS)
        receivers = (busiest + offsets) % QUESTIONS
        additions = jnp.sum((receivers[:, None] == jnp.arange(QUESTIONS)[None, :]).astype(jnp.int32), axis=0) * int(spare > 0)
        tallies = jnp.where(jnp.arange(QUESTIONS) == busiest, MOST_SLOTS, 2 + additions)
        bounds = jnp.cumsum(tallies)
        ordered = jnp.sum((jnp.arange(SLOTS)[:, None] >= bounds[None, :]).astype(jnp.int32), axis=1)
        shuffle = jax.random.permutation(order_key, SLOTS)
        return ordered[shuffle]
    return jax.vmap(one_group)(jax.random.split(key, GROUPS)).astype(jnp.int32)


def set_ends(drawn, stream_key, least, top_value):
    shape = drawn.shape
    place = [jax.random.randint(jax.random.fold_in(stream_key, axis), (), 0, shape[axis]) for axis in range(len(shape))]
    drawn = drawn.at[tuple(place)].set(least)
    longest = shape.index(max(shape))
    place[longest] = (place[longest] + 1) % shape[longest]
    return drawn.at[tuple(place)].set(top_value)


def level_of(stream_key, dims, pieces, smallest, high):
    def one(axis_at, parts):
        draws = jax.random.uniform(jax.random.fold_in(jax.random.fold_in(stream_key, 6), axis_at), (parts,), jnp.float32, smallest / len(pieces), high / len(pieces))
        return jnp.repeat(jnp.exp(draws), dims[axis_at] // parts).reshape((-1,) + (1,) * (len(dims) - axis_at - 1))

    level = one(*pieces[0])
    for cut in pieces[1:]:
        level = level * one(*cut)
    return level


def rank_table(count, slope):
    portions = [(1 << 20) // math.isqrt(standing ** slope) + 1 for standing in range(1, count + 1)]
    spread = 1 + sum(portions) // (1 << 30)
    return np.cumsum(np.array([max(1, weight // spread) for weight in portions]))


def ranked_ids(stream_key, shape, count, slope):
    table = rank_table(count, slope)
    lot = jax.random.randint(jax.random.fold_in(stream_key, 1), shape, 0, int(table[count - 1]))
    rank = jnp.searchsorted(jnp.asarray(table, jnp.int32), lot, side="right")
    return jax.random.permutation(jax.random.fold_in(stream_key, 2), count)[rank].astype(jnp.int32)


def centred(rng, shape, width, bound, pieces=(), kind=jnp.bfloat16):
    drawn = jax.random.normal(rng, shape, jnp.float32) * width
    if len(pieces) > 0:
        drawn = level_of(rng, shape, pieces, -0.22, 0.18) * drawn
    return jnp.clip(drawn, min=-bound, max=bound).astype(kind)


def setup_inputs(seed: int = 0) -> dict:
    key_list = jax.random.split(jax.random.key(seed), 20)
    enc_input = centred(key_list[0], (GROUPS, SLOTS, SRC_LEN, D), 1.0, 6.0, ((0, 4), (1, 8)))
    dec_input = centred(key_list[1], (GROUPS, SLOTS, TGT_LEN, D), 1.0, 6.0, ((0, 4), (1, 8)))
    doc_scores = centred(key_list[2], (GROUPS, SLOTS), 1.0, 5.0, ((0, 4), (1, 8)), jnp.float32)
    owner = draw_owner(jax.random.fold_in(key_list[19], 71), 0)
    targets = set_ends(ranked_ids(key_list[4], (GROUPS, QUESTIONS, TGT_LEN), VOCAB, 2), jax.random.fold_in(key_list[4], 3), 0, VOCAB - 1).astype(jnp.int32)
    enc_attn = centred(key_list[5], (4, D, D), D ** -0.5, 0.1875, ((1, 4),))
    enc_up = centred(key_list[6], (D, FF), D ** -0.5, 0.1875, ((0, 4),))
    enc_down = centred(key_list[7], (FF, D), FF ** -0.5, 0.09375, ((0, 4),))
    enc_up_bias = centred(key_list[8], (FF,), 0.3, 1.5, ((0, 4),))
    enc_bias = centred(key_list[9], (6, D), 0.3, 1.5, ((1, 4),))
    enc_gain = jnp.clip(1.0 + 0.1 * jax.random.normal(key_list[10], (2, D), jnp.float32), 0.5, 1.5).astype(jnp.bfloat16)
    dec_self = centred(key_list[11], (4, D, D), D ** -0.5, 0.1875, ((1, 4),))
    dec_cross = centred(key_list[12], (4, D, D), D ** -0.5, 0.1875, ((1, 4),))
    dec_up = centred(key_list[13], (D, FF), D ** -0.5, 0.1875, ((0, 4),))
    dec_down = centred(key_list[14], (FF, D), FF ** -0.5, 0.09375, ((0, 4),))
    dec_up_bias = centred(key_list[15], (FF,), 0.3, 1.5, ((0, 4),))
    dec_bias = centred(key_list[16], (10, D), 0.3, 1.5, ((1, 4),))
    dec_gain = jnp.clip(1.0 + 0.1 * jax.random.normal(key_list[17], (3, D), jnp.float32), 0.5, 1.5).astype(jnp.bfloat16)
    embed = centred(key_list[18], (VOCAB, D), (D // 4) ** -0.5, 0.375, ((0, 32),))
    return dict(enc_input=enc_input, dec_input=dec_input, doc_scores=doc_scores, owner=owner, targets=targets, enc_attn=enc_attn, enc_up=enc_up, enc_down=enc_down, enc_up_bias=enc_up_bias, enc_bias=enc_bias, enc_gain=enc_gain, dec_self=dec_self, dec_cross=dec_cross, dec_up=dec_up, dec_down=dec_down, dec_up_bias=dec_up_bias, dec_bias=dec_bias, dec_gain=dec_gain, embed=embed)


@jax.custom_vjp
def low(v):
    return lax.optimization_barrier(v.astype(jnp.bfloat16)).astype(jnp.float32)

@jax.custom_vjp
def low_back(v):
    return v

def low_keep(v):
    return (low(v), None)

def low_pass(kept, grad):
    return (grad,)

def back_keep(v):
    return (v, None)

def back_low(kept, grad):
    return (low(grad),)
low.defvjp(low_keep, low_pass)
low_back.defvjp(back_keep, back_low)

def product(left, right):
    return jnp.dot(left, right, precision=lax.Precision.HIGHEST)

def project(input_low, weight):
    return low_back(product(input_low, weight))

def layer_norm(total, gain, shift):
    centered = total - lax.optimization_barrier(jnp.mean(total, axis=-1, keepdims=True))
    inverse = lax.rsqrt(lax.optimization_barrier(jnp.mean(centered * centered, axis=-1, keepdims=True)) + 1e-05)
    return centered * inverse * gain + shift

def attend(query_low, memory_low, matrices, bias_query, bias_value, bias_out, causal):
    rows = query_low.shape[0]
    columns = memory_low.shape[0]
    queries = low(project(query_low, matrices[0]) + bias_query).reshape(rows, HEADS, HEAD_DIM)
    keys = low(project(memory_low, matrices[1])).reshape(columns, HEADS, HEAD_DIM)
    values = low(project(memory_low, matrices[2]) + bias_value).reshape(columns, HEADS, HEAD_DIM)
    scores = low_back(jnp.einsum('qhd,khd->hqk', queries, keys, precision=lax.Precision.HIGHEST) * HEAD_DIM ** (-0.5))
    if causal:
        visible = jnp.arange(rows)[:, None] >= jnp.arange(columns)[None, :]
        scores = jnp.where(visible[None], scores, -1000000000.0)
    weights = jax.nn.softmax(scores, axis=-1)
    context = jnp.einsum('hqk,khd->qhd', low(weights), values, precision=lax.Precision.HIGHEST).reshape(rows, D)
    context = low(low_back(context))
    return project(context, matrices[3]) + bias_out

def feed(input_low, weight_up, bias_up, weight_down, bias_down):
    hidden = low(jax.nn.gelu(project(input_low, weight_up) + bias_up, approximate=False))
    return project(hidden, weight_down) + bias_down

def slot_forward(params, passage, question, target_ids):
    enc_attn, enc_up, enc_down, enc_up_bias, enc_bias, enc_gain, dec_self, dec_cross, dec_up, dec_down, dec_up_bias, dec_bias, dec_gain, embed = params
    passage_low = low(passage)
    first = layer_norm(passage + attend(passage_low, passage_low, enc_attn, enc_bias[0], enc_bias[1], enc_bias[2], False), enc_gain[0], enc_bias[3])
    encoded = layer_norm(first + feed(low(first), enc_up, enc_up_bias, enc_down, enc_bias[4]), enc_gain[1], enc_bias[5])
    memory = low(encoded)
    question_low = low(question)
    state = layer_norm(question + attend(question_low, question_low, dec_self, dec_bias[0], dec_bias[1], dec_bias[2], True), dec_gain[0], dec_bias[3])
    state = layer_norm(state + attend(low(state), memory, dec_cross, dec_bias[4], dec_bias[5], dec_bias[6], False), dec_gain[1], dec_bias[7])
    state = layer_norm(state + feed(low(state), dec_up, dec_up_bias, dec_down, dec_bias[8]), dec_gain[2], dec_bias[9])
    logits = low_back(jnp.dot(low(state), embed.T, precision=lax.Precision.HIGHEST))
    totals = jax.nn.logsumexp(logits, axis=-1)
    chosen = lax.optimization_barrier(jnp.sum(jnp.where(jnp.arange(VOCAB)[None, :] == target_ids[:, None], logits, 0.0), axis=-1))
    return chosen - totals

def reference(enc_input, dec_input, doc_scores, owner, targets, enc_attn, enc_up, enc_down, enc_up_bias, enc_bias, enc_gain, dec_self, dec_cross, dec_up, dec_down, dec_up_bias, dec_bias, dec_gain, embed):
    floats = (enc_input.astype(jnp.float32), dec_input.astype(jnp.float32), doc_scores.astype(jnp.float32), enc_attn.astype(jnp.float32), enc_up.astype(jnp.float32), enc_down.astype(jnp.float32), enc_up_bias.astype(jnp.float32), enc_bias.astype(jnp.float32), enc_gain.astype(jnp.float32), dec_self.astype(jnp.float32), dec_cross.astype(jnp.float32), dec_up.astype(jnp.float32), dec_down.astype(jnp.float32), dec_up_bias.astype(jnp.float32), dec_bias.astype(jnp.float32), dec_gain.astype(jnp.float32), embed.astype(jnp.float32))
    serving = owner[:, :, None] == jnp.arange(QUESTIONS)[None, None, :]
    slot_targets = lax.optimization_barrier(jnp.sum(jnp.where(serving[..., None], targets[:, None, :, :], 0), axis=2)).astype(jnp.int32)

    def objective(passages, questions, scores, *params):

        def one_slot(items):
            return slot_forward(params, items[0], items[1], items[2])
        picked = lax.map(jax.checkpoint(one_slot), (passages.reshape(GROUPS * SLOTS, SRC_LEN, D), questions.reshape(GROUPS * SLOTS, TGT_LEN, D), slot_targets.reshape(GROUPS * SLOTS, TGT_LEN)))
        picked = picked.reshape(GROUPS, SLOTS, TGT_LEN)
        score_terms = jnp.where(serving, scores[:, :, None], -1e+30)
        norms = jax.nn.logsumexp(score_terms, axis=1)
        token_terms = jnp.where(serving[..., None], (scores[:, :, None] + picked)[:, :, None, :], -1e+30)
        mixed = jax.nn.logsumexp(token_terms, axis=1)
        return -lax.optimization_barrier(jnp.sum(mixed - norms[:, :, None], axis=(1, 2))) / (QUESTIONS * TGT_LEN)
    loss, pullback = jax.vjp(objective, *floats)
    grads = pullback(jnp.ones_like(loss) / GROUPS)
    return (loss, grads[0], grads[1], grads[2], grads[3], grads[4], grads[5], grads[6], grads[7], grads[8], grads[9], grads[10], grads[11], grads[12], grads[13], grads[14], grads[15], grads[16])
```

```python
import functools

import jax
import jax.numpy as jnp
from jax import lax
from jax.experimental import pallas as pl
from jax.experimental.pallas import tpu as pltpu
from jax.sharding import PartitionSpec as P

D = 1024
HEADS = 16
HEAD_DIM = 64
SRC_LEN = 384
TGT_LEN = 128
MESH = pl.DeviceIdType.MESH
UNIT = 256
UNITS = 28
RING = 8


BIG_NEGATIVE = -1e30
MASK_FILL = -1000000000.0


def matmul(left, right):
    return jnp.dot(left, right, preferred_element_type=jnp.float32)


def matmul_nt(left, right):
    return lax.dot_general(
        left, right, (((1,), (1,)), ((), ())), preferred_element_type=jnp.float32
    )


def matmul_tn(left, right):
    return lax.dot_general(
        left, right, (((0,), (0,)), ((), ())), preferred_element_type=jnp.float32
    )


def to_low(value):
    return value.astype(jnp.bfloat16)


def norm_forward(total, gain, shift):
    centered = total - jnp.mean(total, axis=-1, keepdims=True)
    inverse = lax.rsqrt(jnp.mean(centered * centered, axis=-1, keepdims=True) + 1e-05)
    normed = centered * inverse
    return (normed * gain + shift, (normed, inverse))


def norm_backward(upstream, saved, gain):
    normed, inverse = saved
    scaled = upstream * gain
    inner = (
        scaled
        - jnp.mean(scaled, axis=-1, keepdims=True)
        - normed * jnp.mean(scaled * normed, axis=-1, keepdims=True)
    )
    return (inverse * inner, jnp.sum(upstream * normed, axis=0), jnp.sum(upstream, axis=0))


def attend_forward(query_low, memory_low, matrices, bias_query, bias_value, bias_out, causal):
    rows = query_low.shape[0]
    columns = memory_low.shape[0]
    queries = to_low(matmul(query_low, matrices[0]) + bias_query).reshape(rows, HEADS, HEAD_DIM)
    keys = to_low(matmul(memory_low, matrices[1])).reshape(columns, HEADS, HEAD_DIM)
    values = to_low(matmul(memory_low, matrices[2]) + bias_value).reshape(columns, HEADS, HEAD_DIM)
    scores = jnp.einsum(
        "qhd,khd->hqk", queries, keys, preferred_element_type=jnp.float32
    ) * HEAD_DIM ** (-0.5)
    if causal:
        visible = jnp.arange(rows)[:, None] >= jnp.arange(columns)[None, :]
        scores = jnp.where(visible[None], scores, MASK_FILL)
    shifted = jnp.exp(scores - jnp.max(scores, axis=-1, keepdims=True))
    probs = shifted / jnp.sum(shifted, axis=-1, keepdims=True)
    context = to_low(
        jnp.einsum(
            "hqk,khd->qhd", to_low(probs), values, preferred_element_type=jnp.float32
        ).reshape(rows, D)
    )
    output = matmul(context, matrices[3]) + bias_out
    return (output, (queries, keys, values, probs, context))


def attend_backward(upstream, query_low, memory_low, matrices, saved):
    queries, keys, values, probs, context = saved
    rows = query_low.shape[0]
    columns = memory_low.shape[0]
    scale = HEAD_DIM ** (-0.5)
    upstream_low = to_low(upstream)
    grad_context = to_low(matmul_nt(upstream_low, matrices[3])).reshape(rows, HEADS, HEAD_DIM)
    grad_probs = jnp.einsum(
        "qhd,khd->hqk", grad_context, values, preferred_element_type=jnp.float32
    )
    grad_values = jnp.einsum(
        "hqk,qhd->khd", to_low(probs), grad_context, preferred_element_type=jnp.float32
    ).reshape(columns, D)
    grad_scores = to_low(probs * (grad_probs - jnp.sum(grad_probs * probs, axis=-1, keepdims=True)))
    grad_queries = (
        jnp.einsum("hqk,khd->qhd", grad_scores, keys, preferred_element_type=jnp.float32) * scale
    ).reshape(rows, D)
    grad_keys = (
        jnp.einsum("hqk,qhd->khd", grad_scores, queries, preferred_element_type=jnp.float32) * scale
    ).reshape(columns, D)
    queries_low = to_low(grad_queries)
    keys_low = to_low(grad_keys)
    values_low = to_low(grad_values)
    grad_query_input = matmul_nt(queries_low, matrices[0])
    grad_memory_input = matmul_nt(keys_low, matrices[1]) + matmul_nt(values_low, matrices[2])
    grad_pairs = [
        (query_low, queries_low),
        (memory_low, keys_low),
        (memory_low, values_low),
        (context, upstream_low),
    ]
    bias_grads = (
        jnp.sum(grad_queries, axis=0),
        jnp.sum(grad_values, axis=0),
        jnp.sum(upstream, axis=0),
    )
    return (grad_query_input, grad_memory_input, grad_pairs, bias_grads)


def gelu_exact(value):
    return jax.nn.gelu(value, approximate=False)


def feed_forward(input_low, weight_up, bias_up, weight_down, bias_down):
    before = matmul(input_low, weight_up) + bias_up
    hidden_low = to_low(gelu_exact(before))
    return (matmul(hidden_low, weight_down) + bias_down, (before, hidden_low))


def hidden_backward(upstream_low, weight_down, before):
    grad_hidden = matmul_nt(upstream_low, weight_down)
    unused, pullback = jax.vjp(gelu_exact, before)
    return pullback(grad_hidden)[0]


def bit_of(name, mask):
    return (lax.axis_index(name) // mask) % 2


def swap(value, name, mask):
    size = lax.axis_size(name)
    return lax.ppermute(value, name, [(i, i ^ mask) for i in range(size)])


def take(value, index, count, axis):
    size = value.shape[axis] // count
    return lax.dynamic_slice_in_dim(value, index * size, size, axis)


def masks_of(name):
    return masks_below(lax.axis_size(name))


class Ticker:
    def __init__(self):
        self.active = []

    def add(self, steps):
        self.active.append((steps, next(steps)))

    def tick(self, *values):
        held, tree = jax.tree.flatten((values, [arrays for _, arrays in self.active]))
        values, arrays = jax.tree.unflatten(tree, lax.optimization_barrier(held))
        going = []
        for (steps, _), mine in zip(self.active, arrays):
            try:
                going.append((steps, steps.send(mine)))
            except StopIteration:
                pass
        self.active = going
        return values if len(values) != 1 else values[0]

    def drain(self):
        while self.active:
            self.tick()


def gather_rows(shard, axis, box):
    size = lax.axis_size("pb")
    me = lax.axis_index("pb")
    side = bit_of("slot", 1)
    rows = shard.shape[axis]
    far = size // 2
    half = rows // 2

    def spread(pieces):
        mask = 1
        while mask < far:
            pieces = pieces + [
                ((start // rows ^ mask) * rows + start % rows, swap(piece, "pb", mask))
                for start, piece in pieces
            ]
            mask *= 2
        return pieces

    first = swap(take(shard, side, 2, axis), "pb", far)
    near = spread([(me * rows, shard)])
    starts = [start for start, _ in near]
    arrays = yield ([piece for _, piece in near], first)
    near = list(zip(starts, arrays[0]))
    first = arrays[1]
    second = swap(first, "slot", 1)
    pieces = near + spread([((me ^ far) * rows + side * half, first)])
    pieces = pieces + spread([((me ^ far) * rows + (1 - side) * half, second)])
    starts = [start for start, _ in pieces]
    arrays = yield [piece for _, piece in pieces]
    shape = list(shard.shape)
    shape[axis] = rows * size
    full = jnp.zeros(tuple(shape), shard.dtype)
    for start, piece in zip(starts, arrays):
        full = lax.dynamic_update_slice_in_dim(full, piece, start, axis)
    box.append(full)


def gather_small(value, names, box):
    held = value[None]
    for name in names:
        for mask in masks_of(name):
            side = bit_of(name, mask)
            came = swap(held, name, mask)
            held = jnp.concatenate(
                [jnp.where(side == 0, held, came), jnp.where(side == 0, came, held)], axis=0
            )
    held = yield held
    box.append(held)


def masks_below(size):
    return [1 << i for i in range(size.bit_length() - 1)]


def xor(value, mask):
    return jnp.where((value // mask) % 2 == 0, value + mask, value - mask)


def sync_kernel(
    slots,
    count,
    parts,
    small,
    out,
    small_out,
    keep,
    core_in,
    far_out,
    far_keep,
    far_in,
    half_out,
    half_keep,
    half_in,
    full,
    small_core,
    small_far,
    small_in,
    small_out_far,
    small_out_slot,
    load_sem,
    store_sem,
    send_sem,
    recv_sem,
    small_send,
    small_recv,
):
    masks = masks_below(slots)
    levels = len(masks)
    rows = full.shape[1]
    slot, pb = lax.axis_index("slot"), lax.axis_index("pb")
    core, far = xor(pb, 1), xor(pb, 2)
    far_core = xor(core, 2)
    partners = [(slot, core), (slot, far)] + [(xor(slot, mask), pb) for mask in masks]
    bits = [(slot // mask) % 2 for mask in masks]

    barrier = pltpu.get_barrier_semaphore()
    for partner in partners:
        pl.semaphore_signal(barrier, inc=1, device_id=partner, device_id_type=MESH)
    pl.semaphore_wait(barrier, len(partners))

    def remote(source, target, stage, at, partner):
        return pltpu.make_async_remote_copy(
            src_ref=source,
            dst_ref=target,
            send_sem=send_sem.at[stage, at],
            recv_sem=recv_sem.at[stage, at],
            device_id=partner,
            device_id_type=MESH,
        )

    def core_copies(c):
        at = lax.rem(c, RING)
        ring = lax.rem(c, 4)
        return (
            remote(parts.at[c, core], core_in.at[ring, 0], 0, at, partners[0]),
            remote(parts.at[c, far_core], core_in.at[ring, 1], 1, at, partners[0]),
        )

    def loads(c):
        ring = lax.rem(c, 4)
        return (
            pltpu.make_async_copy(parts.at[c, pb], keep.at[ring, 0], load_sem.at[0, ring]),
            pltpu.make_async_copy(parts.at[c, far], keep.at[ring, 1], load_sem.at[1, ring]),
        )

    def far_copy(c):
        ring = lax.rem(c, 4)
        return remote(far_out.at[ring], far_in.at[ring], 2, lax.rem(c, RING), partners[1])

    def halve_copy(level, c):
        ring = lax.rem(c, 4)
        return remote(
            half_out[level].at[ring],
            half_in[level].at[ring],
            3 + level,
            lax.rem(c, RING),
            partners[2 + level],
        )

    def join_copy(level, c):
        at = lax.rem(c, RING)
        size = rows >> (level + 1)
        offset = sum(bits[i] * (rows >> (i + 1)) for i in range(level + 1))
        where = pl.ds(pl.multiple_of(offset, size), size)
        return remote(
            full.at[at, where], full.at[at, where], 3 + levels + level, at, partners[2 + level]
        )

    def store(c):
        at = lax.rem(c, RING)
        return pltpu.make_async_copy(full.at[at], out.at[c], store_sem.at[at])

    def add(target, left, right, size):
        tile = min(size, 32)

        @pl.loop(0, size // tile)
        def _(i):
            at = pl.ds(pl.multiple_of(i * tile, tile), tile)
            total = left[at, :].astype(jnp.float32) + right[at, :].astype(jnp.float32)
            target[at, :] = total.astype(target.dtype)

    def small_core_copies():
        return [
            pltpu.make_async_remote_copy(
                src_ref=small.at[source],
                dst_ref=small_core.at[i],
                send_sem=small_send.at[i],
                recv_sem=small_recv.at[i],
                device_id=partners[0],
                device_id_type=MESH,
            )
            for i, source in ((0, core), (1, far_core))
        ]

    def small_far_copy():
        return pltpu.make_async_remote_copy(
            src_ref=small_out_far,
            dst_ref=small_far,
            send_sem=small_send.at[2],
            recv_sem=small_recv.at[2],
            device_id=partners[1],
            device_id_type=MESH,
        )

    def small_slot_copy(level):
        return pltpu.make_async_remote_copy(
            src_ref=small_out_slot.at[level],
            dst_ref=small_in.at[level],
            send_sem=small_send.at[3 + level],
            recv_sem=small_recv.at[3 + level],
            device_id=partners[2 + level],
            device_id_type=MESH,
        )

    def small_stage(step):
        if step == 0:
            for copy in small_core_copies():
                copy.start()
        elif step == 1:
            for copy in small_core_copies():
                copy.wait()
            small_out_far[...] = small[far] + small_core[1]
            small_out[...] = small[pb] + small_core[0]
            small_far_copy().start()
        elif step == 2:
            small_far_copy().wait()
            small_out[...] = small_out[...] + small_far[...]
            small_out_slot[0] = small_out[...]
            small_slot_copy(0).start()
        else:
            level = step - 3
            small_slot_copy(level).wait()
            small_out[...] = small_out[...] + small_in[level]
            if level + 1 < levels:
                small_out_slot[level + 1] = small_out[...]
                small_slot_copy(level + 1).start()

    def stage(step, c):
        ring = lax.rem(c, 4)
        at = lax.rem(c, RING)
        if step == 0:
            for copy in core_copies(c) + loads(c):
                copy.start()
        elif step == 1:
            for copy in core_copies(c) + loads(c):
                copy.wait()
            add(far_out.at[ring], keep.at[ring, 1], core_in.at[ring, 1], rows)
            far_copy(c).start()
            add(far_keep.at[ring], keep.at[ring, 0], core_in.at[ring, 0], rows)
        elif step < 2 + levels:
            level = step - 2
            size = rows >> (level + 1)
            if level == 0:
                far_copy(c).wait()
                left, right = far_keep.at[ring], far_in.at[ring]
            else:
                halve_copy(level - 1, c).wait()
                left, right = half_keep[level - 1].at[ring], half_in[level - 1].at[ring]
            mine = pl.ds(pl.multiple_of(bits[level] * size, size), size)
            other = pl.ds(pl.multiple_of((1 - bits[level]) * size, size), size)
            add(half_out[level].at[ring], left.at[other], right.at[other], size)
            halve_copy(level, c).start()
            add(half_keep[level].at[ring], left.at[mine], right.at[mine], size)
        elif step == 2 + levels:
            level = levels - 1
            size = rows >> levels
            halve_copy(level, c).wait()
            offset = sum(bits[i] * (rows >> (i + 1)) for i in range(levels))
            where = pl.ds(pl.multiple_of(offset, size), size)
            add(full.at[at, where], half_keep[level].at[ring], half_in[level].at[ring], size)
            join_copy(level, c).start()
        elif step < 2 + 2 * levels:
            level = levels - 1 - (step - 3 - levels)
            join_copy(level, c).wait()
            join_copy(level - 1, c).start()
        elif step == 2 + 2 * levels:
            join_copy(0, c).wait()
            store(c).start()
        else:
            store(c).wait()

    stages = 4 + 2 * levels

    @pl.loop(0, count + stages - 1)
    def _(it):
        for step in range(3 + levels):

            @pl.when(it == step)
            def _():
                small_stage(step)

        for step in range(stages):
            c = it - step

            @pl.when(jnp.logical_and(c >= 0, c < count))
            def _():
                stage(step, c)


def sync_gradients(parts, small):
    slots = lax.axis_size("slot")
    count, size, rows, columns = parts.shape
    levels = slots.bit_length() - 1
    small_rows = small.shape[1:]
    low = jnp.bfloat16
    block = lambda *lead: pltpu.VMEM(lead + (columns,), low)
    halves = [block(4, rows >> (i + 1)) for i in range(levels)]
    return pl.pallas_call(
        functools.partial(sync_kernel, slots, count),
        out_shape=(
            jax.ShapeDtypeStruct((count, rows, columns), low),
            jax.ShapeDtypeStruct(small_rows, jnp.float32),
        ),
        in_specs=[
            pl.BlockSpec(memory_space=pl.ANY),
            pl.BlockSpec(memory_space=pltpu.VMEM),
        ],
        out_specs=(
            pl.BlockSpec(memory_space=pl.ANY),
            pl.BlockSpec(memory_space=pltpu.VMEM),
        ),
        scratch_shapes=[
            block(4, 2, rows),
            block(4, 2, rows),
            block(4, rows),
            block(4, rows),
            block(4, rows),
            halves,
            halves,
            halves,
            block(RING, rows),
            pltpu.VMEM((2,) + small_rows, jnp.float32),
            pltpu.VMEM(small_rows, jnp.float32),
            pltpu.VMEM((levels,) + small_rows, jnp.float32),
            pltpu.VMEM(small_rows, jnp.float32),
            pltpu.VMEM((levels,) + small_rows, jnp.float32),
            pltpu.SemaphoreType.DMA((2, 4)),
            pltpu.SemaphoreType.DMA((RING,)),
            pltpu.SemaphoreType.DMA((3 + 2 * levels, RING)),
            pltpu.SemaphoreType.DMA((3 + 2 * levels, RING)),
            pltpu.SemaphoreType.DMA((3 + levels,)),
            pltpu.SemaphoreType.DMA((3 + levels,)),
        ],
        compiler_params=pltpu.CompilerParams(
            collective_id=1, has_side_effects=True, vmem_limit_bytes=54 << 20
        ),
    )(parts, small)


def weight_grad_kernel(left, right, *rest):
    out = rest[-1]
    product = lax.dot_general(
        left[...], right[...], (((0,), (0,)), ((), ())), preferred_element_type=jnp.float32
    )
    out[0, 0] = product.astype(out.dtype)


def weight_grad(stack, left, right, first, tall=False):
    slots, parts = lax.axis_size("slot"), lax.axis_size("pb")
    rows = max(UNIT, 16 * slots)
    per = rows // UNIT
    tokens = left.shape[0]
    units = left.shape[1] * right.shape[1] // (D * D)
    left_map = (lambda k, p: (0, p * units + k)) if tall else (lambda k, p: (0, p))
    right_map = (lambda k, p: (0, 0)) if tall else (lambda k, p: (0, k))
    specs = [pl.BlockSpec((tokens, UNIT), left_map), pl.BlockSpec((tokens, D), right_map)]
    operands = [left, right]
    if stack is not None:
        specs.append(pl.BlockSpec(memory_space=pl.ANY))
        operands.append(stack)
    return pl.pallas_call(
        weight_grad_kernel,
        grid=(units, parts),
        out_shape=jax.ShapeDtypeStruct((UNITS // per, parts, rows, D), jnp.bfloat16),
        in_specs=specs,
        out_specs=pl.BlockSpec(
            (1, 1, UNIT, D),
            lambda k, p: ((first + k) // per, p, (first + k) % per, 0),
        ),
        input_output_aliases={2: 0} if stack is not None else {},
    )(*operands)


EVERY = ("slot", "pb")


def own_targets(targets, owner):
    serving = jnp.arange(targets.shape[1]) == owner[0, 0]
    own = jnp.sum(jnp.where(serving[:, None], targets[0], 0), axis=0)
    return jnp.concatenate([own, jnp.broadcast_to(owner[0, 0], (TGT_LEN,))])


def vocabulary_head(state_low, target_slots, owner_slots, questions, doc_scores, embed):
    slots, groups = lax.axis_size("slot"), lax.axis_size("pb")
    me = lax.axis_index("slot") * groups + lax.axis_index("pb")
    entries = embed.shape[0]
    tokens = slots * groups * TGT_LEN
    states = lax.all_gather(state_low, EVERY, axis=0, tiled=True)
    logits = matmul_nt(states, embed)
    hit = (
        target_slots.reshape(tokens, 1) - me * entries
        == lax.broadcasted_iota(jnp.int32, (tokens, entries), 1)
    )
    top = jnp.max(logits, axis=1)
    total = jnp.sum(jnp.exp(logits - top[:, None]), axis=1)
    pick = jnp.sum(jnp.where(hit, logits, 0.0), axis=1)
    own_score = jnp.broadcast_to(doc_scores.reshape(1), (TGT_LEN,))
    stats = lax.all_gather(jnp.concatenate([top, total, pick, own_score]), EVERY, axis=0)
    tops, totals = stats[:, :tokens], stats[:, tokens : 2 * tokens]
    scores = stats[:, 3 * tokens].reshape(slots, groups)
    best = jnp.max(tops, axis=0)
    log_total = best + jnp.log(jnp.sum(totals * jnp.exp(tops - best[None]), axis=0))
    picked = jnp.sum(stats[:, 2 * tokens : 3 * tokens], axis=0) - log_total
    picked = picked.reshape(slots, groups, TGT_LEN)
    owners = owner_slots.reshape(slots, groups)
    serving = owners[:, :, None] == jnp.arange(questions)
    score_terms = jnp.where(serving, scores[:, :, None], BIG_NEGATIVE)
    token_terms = jnp.where(
        serving[..., None], (scores[:, :, None] + picked)[:, :, None, :], BIG_NEGATIVE
    )
    score_top, token_top = jnp.max(score_terms, axis=0), jnp.max(token_terms, axis=0)
    score_norm = score_top + jnp.log(jnp.sum(jnp.exp(score_terms - score_top), axis=0))
    token_mix = token_top + jnp.log(jnp.sum(jnp.exp(token_terms - token_top), axis=0))
    group_tokens = questions * TGT_LEN
    count = groups * group_tokens
    losses = -jnp.sum(token_mix - score_norm[:, :, None], axis=(1, 2)) / group_tokens
    own_mix = jnp.sum(jnp.where(serving[..., None], token_mix[None], 0.0), axis=2)
    own_norm = jnp.sum(jnp.where(serving, score_norm[None], 0.0), axis=2)
    posterior = jnp.exp(scores[:, :, None] + picked - own_mix)
    prior = jnp.exp(scores - own_norm)
    token_grad = (-posterior / count).reshape(tokens, 1)
    score_grads = -jnp.sum(posterior - prior[:, :, None], axis=2) / count
    delta = to_low(
        token_grad * (jnp.where(hit, 1.0, 0.0) - jnp.exp(logits - log_total[:, None]))
    )
    grad_state = lax.psum_scatter(
        to_low(matmul(delta, embed)), EVERY, scatter_dimension=0, tiled=True
    ).astype(jnp.float32)
    slot, group = lax.axis_index("slot"), lax.axis_index("pb")
    loss = lax.dynamic_slice(losses, (group,), (1,))
    score_grad = lax.dynamic_slice(score_grads, (slot, group), (1, 1))
    return (loss, score_grad, grad_state, delta, states)


def local(
    enc_input,
    dec_input,
    doc_scores,
    owner,
    targets,
    enc_attn,
    enc_up,
    enc_down,
    enc_up_bias,
    enc_bias,
    enc_gain,
    dec_self,
    dec_cross,
    dec_up,
    dec_down,
    dec_up_bias,
    dec_bias,
    dec_gain,
    embed,
):
    pb_size = lax.axis_size("pb")
    width = D // pb_size
    vectors = (enc_up_bias, enc_bias, enc_gain, dec_up_bias, dec_bias, dec_gain)
    rows = [v.size // width for v in vectors]
    starts = [sum(rows[:i]) for i in range(len(rows) + 1)]
    passage_low = enc_input[0, 0]
    passage = passage_low.astype(jnp.float32)
    question_low = dec_input[0, 0]
    question = question_low.astype(jnp.float32)

    full = []
    ticker = Ticker()
    ticker.add(
        gather_small(jnp.concatenate([v.reshape(-1, width) for v in vectors]), ("pb",), full)
    )
    ticker.add(gather_rows(enc_attn, 1, full))
    ticker.tick()
    packed = full[0].astype(jnp.float32)
    unpacked = [packed[:, starts[i] : starts[i + 1], :] for i in range(len(rows))]
    encoder_upbias = unpacked[0].reshape(-1)
    encoder_bias = unpacked[1].transpose(1, 0, 2).reshape(-1, D)
    encoder_gain = unpacked[2].transpose(1, 0, 2).reshape(-1, D)
    decoder_upbias = unpacked[3].reshape(-1)
    decoder_bias = unpacked[4].transpose(1, 0, 2).reshape(-1, D)
    decoder_gain = unpacked[5].transpose(1, 0, 2).reshape(-1, D)
    ticker.add(gather_rows(enc_up, 0, full))
    ticker.tick()
    encoder_attn = full[1]
    ticker.add(gather_rows(enc_down, 0, full))
    attn_out, enc_saved = attend_forward(
        passage_low,
        passage_low,
        encoder_attn,
        encoder_bias[0],
        encoder_bias[1],
        encoder_bias[2],
        False,
    )
    attn_out = ticker.tick(attn_out)
    encoder_up = full[2]
    ticker.add(gather_rows(dec_self, 1, full))
    enc_first, enc_norm_one = norm_forward(passage + attn_out, encoder_gain[0], encoder_bias[3])
    enc_first_low = to_low(enc_first)
    enc_before = matmul(enc_first_low, encoder_up) + encoder_upbias
    enc_hidden_low = to_low(gelu_exact(enc_before))
    enc_hidden_low, enc_before = ticker.tick(enc_hidden_low, enc_before)
    encoder_down = full[3]
    ticker.add(gather_rows(dec_cross, 1, full))
    ticker.add(gather_small(own_targets(targets, owner), EVERY[::-1], full))
    ffn_out = matmul(enc_hidden_low, encoder_down) + encoder_bias[4]
    encoded, enc_norm_two = norm_forward(enc_first + ffn_out, encoder_gain[1], encoder_bias[5])
    memory_low = to_low(encoded)
    memory_low = ticker.tick(memory_low)
    decoder_self = full[4]
    targets_all = full[5]
    target_slots, owner_slots = targets_all[:, :TGT_LEN], targets_all[:, TGT_LEN]
    ticker.add(gather_rows(dec_up, 0, full))
    self_out, self_saved = attend_forward(
        question_low,
        question_low,
        decoder_self,
        decoder_bias[0],
        decoder_bias[1],
        decoder_bias[2],
        True,
    )
    dec_first, dec_norm_one = norm_forward(question + self_out, decoder_gain[0], decoder_bias[3])
    dec_first = ticker.tick(dec_first)
    dec_first_low = to_low(dec_first)
    decoder_cross = full[6]
    ticker.add(gather_rows(dec_down, 0, full))
    cross_out, cross_saved = attend_forward(
        dec_first_low,
        memory_low,
        decoder_cross,
        decoder_bias[4],
        decoder_bias[5],
        decoder_bias[6],
        False,
    )
    dec_second, dec_norm_two = norm_forward(dec_first + cross_out, decoder_gain[1], decoder_bias[7])
    dec_second = ticker.tick(dec_second)
    dec_second_low = to_low(dec_second)
    decoder_up = full[7]
    dec_before = matmul(dec_second_low, decoder_up) + decoder_upbias
    dec_hidden_low = to_low(gelu_exact(dec_before))
    dec_hidden_low, dec_before = ticker.tick(dec_hidden_low, dec_before)
    decoder_down = full[8]
    dec_ffn_out = matmul(dec_hidden_low, decoder_down) + decoder_bias[8]
    state, dec_norm_three = norm_forward(dec_second + dec_ffn_out, decoder_gain[2], decoder_bias[9])
    state_low = to_low(state)

    loss, score_grad, grad_state_sum, delta, states = vocabulary_head(
        state_low, target_slots, owner_slots, targets.shape[1], doc_scores, embed
    )

    embed_grad = matmul_tn(delta, states)
    grad_third, gain_third, shift_third = norm_backward(
        grad_state_sum, dec_norm_three, decoder_gain[2]
    )
    dec_downbias_grad = jnp.sum(grad_third, axis=0)
    third_low = to_low(grad_third)
    grad_before = hidden_backward(third_low, decoder_down, dec_before)
    dec_upbias_grad = jnp.sum(grad_before, axis=0)
    before_low = to_low(grad_before)
    grad_second, gain_second, shift_second = norm_backward(
        grad_third + matmul_nt(before_low, decoder_up), dec_norm_two, decoder_gain[1]
    )
    cross_query, grad_memory, dec_cross_pairs, cross_biases = attend_backward(
        grad_second, dec_first_low, memory_low, decoder_cross, cross_saved
    )
    grad_first, gain_first, shift_first = norm_backward(
        grad_second + cross_query, dec_norm_one, decoder_gain[0]
    )
    self_query, self_memory, dec_self_pairs, self_biases = attend_backward(
        grad_first, question_low, question_low, decoder_self, self_saved
    )
    question_grad = grad_first + self_query + self_memory
    enc_grad_two, enc_gain_two, enc_shift_two = norm_backward(
        grad_memory, enc_norm_two, encoder_gain[1]
    )
    enc_downbias_grad = jnp.sum(enc_grad_two, axis=0)
    enc_two_low = to_low(enc_grad_two)
    enc_grad_before = hidden_backward(enc_two_low, encoder_down, enc_before)
    enc_upbias_grad = jnp.sum(enc_grad_before, axis=0)
    enc_before_low = to_low(enc_grad_before)
    enc_grad_one, enc_gain_one, enc_shift_one = norm_backward(
        enc_grad_two + matmul_nt(enc_before_low, encoder_up), enc_norm_one, encoder_gain[0]
    )
    enc_query, enc_memory, enc_attn_pairs, enc_biases = attend_backward(
        enc_grad_one, passage_low, passage_low, encoder_attn, enc_saved
    )
    passage_grad = enc_grad_one + enc_query + enc_memory
    stack = weight_grad(None, dec_hidden_low, third_low, 24, tall=True)
    stack = weight_grad(stack, dec_second_low, before_low, 20)
    for i, (left, right) in enumerate(dec_cross_pairs):
        stack = weight_grad(stack, left, right, 16 + i)
    for i, (left, right) in enumerate(dec_self_pairs):
        stack = weight_grad(stack, left, right, 12 + i)
    stack = weight_grad(stack, enc_hidden_low, enc_two_low, 8, tall=True)
    stack = weight_grad(stack, enc_first_low, enc_before_low, 4)
    for i, (left, right) in enumerate(enc_attn_pairs):
        stack = weight_grad(stack, left, right, i)
    enc_bias_grad = jnp.stack(
        [
            enc_biases[0],
            enc_biases[1],
            enc_biases[2],
            enc_shift_one,
            enc_downbias_grad,
            enc_shift_two,
        ]
    )
    enc_gain_grad = jnp.stack([enc_gain_one, enc_gain_two])
    dec_bias_grad = jnp.stack(
        [
            self_biases[0],
            self_biases[1],
            self_biases[2],
            shift_first,
            cross_biases[0],
            cross_biases[1],
            cross_biases[2],
            shift_second,
            dec_downbias_grad,
            shift_third,
        ]
    )
    dec_gain_grad = jnp.stack([gain_first, gain_second, gain_third])
    vector_grads = jnp.concatenate(
        [
            enc_upbias_grad.reshape(pb_size, -1, width),
            enc_bias_grad.reshape(-1, pb_size, width).transpose(1, 0, 2),
            enc_gain_grad.reshape(-1, pb_size, width).transpose(1, 0, 2),
            dec_upbias_grad.reshape(pb_size, -1, width),
            dec_bias_grad.reshape(-1, pb_size, width).transpose(1, 0, 2),
            dec_gain_grad.reshape(-1, pb_size, width).transpose(1, 0, 2),
        ],
        axis=1,
    )
    spare = -starts[-1] % 32
    small = jnp.pad(vector_grads, ((0, 0), (0, spare), (0, 0))).reshape(pb_size, -1, D)
    summed_parts, small_sum = sync_gradients(stack, small)
    units = summed_parts.reshape(UNITS, width, D)
    square = lambda at: units[at : at + 4].astype(jnp.float32)
    wide = lambda at: jnp.concatenate([units[at + i].astype(jnp.float32) for i in range(4)], axis=1)
    tall = lambda at: square(at).reshape(-1, D)
    vector_sum = small_sum.reshape(-1, width)
    vector_out = [
        vector_sum[starts[i] : starts[i + 1]].reshape(v.shape) for i, v in enumerate(vectors)
    ]
    summed = (
        (square(0), wide(4), tall(8))
        + tuple(vector_out[:3])
        + (square(12), square(16), wide(20), tall(24))
        + tuple(vector_out[3:])
    )
    return (
        (
            loss,
            passage_grad.reshape(1, 1, SRC_LEN, D),
            question_grad.reshape(1, 1, TGT_LEN, D),
            score_grad,
        )
        + tuple(summed)
        + (embed_grad,)
    )


def solution(mesh):
    placed = (
        P("pb", "slot", None, None),
        P("pb", "slot", None, None),
        P("pb", "slot"),
        P("pb", "slot"),
        P("pb", None, None),
        P(None, "pb", None),
        P("pb", None),
        P("pb", None),
        P("pb"),
        P(None, "pb"),
        P(None, "pb"),
        P(None, "pb", None),
        P(None, "pb", None),
        P("pb", None),
        P("pb", None),
        P("pb"),
        P(None, "pb"),
        P(None, "pb"),
        P(("slot", "pb"), None),
    )
    return jax.shard_map(
        local,
        mesh=mesh,
        in_specs=placed,
        out_specs=(
            P("pb"),
            P("pb", "slot", None, None),
            P("pb", "slot", None, None),
            P("pb", "slot"),
            P(None, "pb", None),
            P("pb", None),
            P("pb", None),
            P("pb"),
            P(None, "pb"),
            P(None, "pb"),
            P(None, "pb", None),
            P(None, "pb", None),
            P("pb", None),
            P("pb", None),
            P("pb"),
            P(None, "pb"),
            P(None, "pb"),
            P(("slot", "pb"), None),
        ),
        check_vma=False,
    )
```

```python
import functools

import jax
import jax.numpy as jnp
from jax import lax
from jax.experimental import pallas as pl
from jax.experimental.pallas import tpu as pltpu
from jax.sharding import PartitionSpec as P

D = 1024
HEADS = 16
HEAD_DIM = 64
SRC_LEN = 384
TGT_LEN = 128
MESH = pl.DeviceIdType.MESH
UNIT = 256
RING = 8


BIG_NEGATIVE = -1e30
MASK_FILL = -1000000000.0


def matmul(left, right):
    return jnp.dot(left, right, preferred_element_type=jnp.float32)


def matmul_nt(left, right):
    return lax.dot_general(
        left, right, (((1,), (1,)), ((), ())), preferred_element_type=jnp.float32
    )


def matmul_tn(left, right):
    return lax.dot_general(
        left, right, (((0,), (0,)), ((), ())), preferred_element_type=jnp.float32
    )


def to_low(value):
    return value.astype(jnp.bfloat16)


def norm_forward(total, gain, shift):
    centered = total - jnp.mean(total, axis=-1, keepdims=True)
    inverse = lax.rsqrt(jnp.mean(centered * centered, axis=-1, keepdims=True) + 1e-05)
    normed = centered * inverse
    return (normed * gain + shift, (normed, inverse))


def norm_backward(upstream, saved, gain):
    normed, inverse = saved
    scaled = upstream * gain
    inner = (
        scaled
        - jnp.mean(scaled, axis=-1, keepdims=True)
        - normed * jnp.mean(scaled * normed, axis=-1, keepdims=True)
    )
    return (inverse * inner, jnp.sum(upstream * normed, axis=0), jnp.sum(upstream, axis=0))


def attend_forward(query_low, memory_low, matrices, bias_query, bias_value, bias_out, causal):
    rows = query_low.shape[0]
    columns = memory_low.shape[0]
    queries = to_low(matmul(query_low, matrices[0]) + bias_query).reshape(rows, HEADS, HEAD_DIM)
    keys = to_low(matmul(memory_low, matrices[1])).reshape(columns, HEADS, HEAD_DIM)
    values = to_low(matmul(memory_low, matrices[2]) + bias_value).reshape(columns, HEADS, HEAD_DIM)
    scores = jnp.einsum(
        "qhd,khd->hqk", queries, keys, preferred_element_type=jnp.float32
    ) * HEAD_DIM ** (-0.5)
    if causal:
        visible = jnp.arange(rows)[:, None] >= jnp.arange(columns)[None, :]
        scores = jnp.where(visible[None], scores, MASK_FILL)
    shifted = jnp.exp(scores - jnp.max(scores, axis=-1, keepdims=True))
    probs = shifted / jnp.sum(shifted, axis=-1, keepdims=True)
    context = to_low(
        jnp.einsum(
            "hqk,khd->qhd", to_low(probs), values, preferred_element_type=jnp.float32
        ).reshape(rows, D)
    )
    output = matmul(context, matrices[3]) + bias_out
    return (output, (queries, keys, values, probs, context))


def attend_backward(upstream, query_low, memory_low, matrices, saved):
    queries, keys, values, probs, context = saved
    rows = query_low.shape[0]
    columns = memory_low.shape[0]
    scale = HEAD_DIM ** (-0.5)
    upstream_low = to_low(upstream)
    grad_context = to_low(matmul_nt(upstream_low, matrices[3])).reshape(rows, HEADS, HEAD_DIM)
    grad_probs = jnp.einsum(
        "qhd,khd->hqk", grad_context, values, preferred_element_type=jnp.float32
    )
    grad_values = jnp.einsum(
        "hqk,qhd->khd", to_low(probs), grad_context, preferred_element_type=jnp.float32
    ).reshape(columns, D)
    grad_scores = to_low(probs * (grad_probs - jnp.sum(grad_probs * probs, axis=-1, keepdims=True)))
    grad_queries = (
        jnp.einsum("hqk,khd->qhd", grad_scores, keys, preferred_element_type=jnp.float32) * scale
    ).reshape(rows, D)
    grad_keys = (
        jnp.einsum("hqk,qhd->khd", grad_scores, queries, preferred_element_type=jnp.float32) * scale
    ).reshape(columns, D)
    queries_low = to_low(grad_queries)
    keys_low = to_low(grad_keys)
    values_low = to_low(grad_values)
    grad_query_input = matmul_nt(queries_low, matrices[0])
    grad_memory_input = matmul_nt(keys_low, matrices[1]) + matmul_nt(values_low, matrices[2])
    grad_pairs = [
        (query_low, queries_low),
        (memory_low, keys_low),
        (memory_low, values_low),
        (context, upstream_low),
    ]
    bias_grads = (
        jnp.sum(grad_queries, axis=0),
        jnp.sum(grad_values, axis=0),
        jnp.sum(upstream, axis=0),
    )
    return (grad_query_input, grad_memory_input, grad_pairs, bias_grads)


def gelu_exact(value):
    return jax.nn.gelu(value, approximate=False)


def feed_forward(input_low, weight_up, bias_up, weight_down, bias_down):
    before = matmul(input_low, weight_up) + bias_up
    hidden_low = to_low(gelu_exact(before))
    return (matmul(hidden_low, weight_down) + bias_down, (before, hidden_low))


def hidden_backward(upstream_low, weight_down, before):
    grad_hidden = matmul_nt(upstream_low, weight_down)
    unused, pullback = jax.vjp(gelu_exact, before)
    return pullback(grad_hidden)[0]


def bit_of(name, mask):
    return (lax.axis_index(name) // mask) % 2


def swap(value, name, mask):
    size = lax.axis_size(name)
    return lax.ppermute(value, name, [(i, i ^ mask) for i in range(size)])


def take(value, index, count, axis):
    size = value.shape[axis] // count
    return lax.dynamic_slice_in_dim(value, index * size, size, axis)


def masks_of(name):
    return masks_below(lax.axis_size(name))


def natural_order(held, name):
    count = held.shape[0]
    for mask in masks_of(name):
        pairs = held.reshape((count // (2 * mask), 2, mask) + held.shape[1:])
        turned = jnp.where(bit_of(name, mask) == 0, pairs, pairs[:, ::-1])
        held = turned.reshape(held.shape)
    return held


class Ticker:
    def __init__(self):
        self.active = []

    def add(self, steps):
        self.active.append((steps, next(steps)))

    def tick(self, *values):
        held, tree = jax.tree.flatten((values, [arrays for _, arrays in self.active]))
        values, arrays = jax.tree.unflatten(tree, lax.optimization_barrier(held))
        going = []
        for (steps, _), mine in zip(self.active, arrays):
            try:
                going.append((steps, steps.send(mine)))
            except StopIteration:
                pass
        self.active = going
        return values if len(values) != 1 else values[0]

    def drain(self):
        while self.active:
            self.tick()


def gather_rows(shard, axis, box):
    size = lax.axis_size("pb")
    me = lax.axis_index("pb")
    side = bit_of("slot", 1)
    rows = shard.shape[axis]
    far = size // 2
    half = rows // 2

    def spread(pieces):
        mask = 1
        while mask < far:
            pieces = pieces + [
                ((start // rows ^ mask) * rows + start % rows, swap(piece, "pb", mask))
                for start, piece in pieces
            ]
            mask *= 2
        return pieces

    first = swap(take(shard, side, 2, axis), "pb", far)
    near = spread([(me * rows, shard)])
    starts = [start for start, _ in near]
    arrays = yield ([piece for _, piece in near], first)
    near = list(zip(starts, arrays[0]))
    first = arrays[1]
    second = swap(first, "slot", 1)
    pieces = near + spread([((me ^ far) * rows + side * half, first)])
    pieces = pieces + spread([((me ^ far) * rows + (1 - side) * half, second)])
    starts = [start for start, _ in pieces]
    arrays = yield [piece for _, piece in pieces]
    shape = list(shard.shape)
    shape[axis] = rows * size
    full = jnp.zeros(tuple(shape), shard.dtype)
    for start, piece in zip(starts, arrays):
        full = lax.dynamic_update_slice_in_dim(full, piece, start, axis)
    box.append(full)


def gather_small(value, names, box):
    held = value[None]
    for name in names:
        for mask in masks_of(name):
            held = jnp.concatenate([held, swap(held, name, mask)], axis=0)
    held = yield held
    box.append(held)


def masks_below(size):
    return [1 << i for i in range(size.bit_length() - 1)]


def xor(value, mask):
    return jnp.where((value // mask) % 2 == 0, value + mask, value - mask)


def sync_kernel(slots, count, plan, operands, small, out, small_out, scratch):
    left_buffer, right_buffer, parts, core_in, far_out, far_keep, far_in = scratch[:7]
    half_out, half_keep, half_in, full = scratch[7:11]
    small_core, small_far, small_in, small_out_far, small_out_slot = scratch[11:16]
    load_sem, store_sem, send_sem, recv_sem, small_send, small_recv = scratch[16:]
    masks = masks_below(slots)
    levels = len(masks)
    rows = full.shape[1]
    slot, pb = lax.axis_index("slot"), lax.axis_index("pb")
    core, far = xor(pb, 1), xor(pb, 2)
    far_core = xor(core, 2)
    partners = [(slot, core), (slot, far)] + [(xor(slot, mask), pb) for mask in masks]
    bits = [(slot // mask) % 2 for mask in masks]

    barrier = pltpu.get_barrier_semaphore()
    for partner in partners:
        pl.semaphore_signal(barrier, inc=1, device_id=partner, device_id_type=MESH)
    pl.semaphore_wait(barrier, len(partners))

    def remote(source, target, stage, at, partner):
        return pltpu.make_async_remote_copy(
            src_ref=source,
            dst_ref=target,
            send_sem=send_sem.at[stage, at],
            recv_sem=recv_sem.at[stage, at],
            device_id=partner,
            device_id_type=MESH,
        )

    def core_copies(c):
        at = lax.rem(c, RING)
        ring = lax.rem(c, 4)
        pair = lax.rem(c, 2)
        return (
            remote(parts.at[pair, core], core_in.at[ring, 0], 0, at, partners[0]),
            remote(parts.at[pair, far_core], core_in.at[ring, 1], 1, at, partners[0]),
        )

    def load(unit):
        pair = lax.rem(unit, 2)
        for at, (left, right, k, tall) in enumerate(plan):

            @pl.when(unit == at)
            def _():
                tokens = operands[left].shape[0]
                rows_at = pl.ds(0, tokens)
                if tall:
                    for p in range(4):
                        pltpu.make_async_copy(
                            operands[left].at[:, pl.ds((4 * p + k) * UNIT, UNIT)],
                            left_buffer.at[pair, rows_at, pl.ds(p * UNIT, UNIT)],
                            load_sem.at[0, pair],
                        ).start()
                else:
                    pltpu.make_async_copy(
                        operands[left], left_buffer.at[pair, rows_at], load_sem.at[0, pair]
                    ).start()
                column = 0 if tall else k * D
                pltpu.make_async_copy(
                    operands[right].at[:, pl.ds(column, D)],
                    right_buffer.at[pair, rows_at],
                    load_sem.at[1, pair],
                ).start()

    def product(unit, chunk, offset):
        pair = lax.rem(unit, 2)
        lengths = [operands[left].shape[0] for left, _, _, _ in plan]
        for tokens in sorted(set(lengths)):
            among = functools.reduce(
                jnp.logical_or, [unit == at for at, n in enumerate(lengths) if n == tokens]
            )

            @pl.when(among)
            def _():
                rows_at = pl.ds(0, tokens)
                for i, buffer in enumerate((left_buffer, right_buffer)):
                    whole = buffer.at[pair, rows_at]
                    pltpu.make_async_copy(whole, whole, load_sem.at[i, pair]).wait()

                @pl.loop(0, 4)
                def _(p):
                    columns = pl.ds(pl.multiple_of(p * UNIT, UNIT), UNIT)
                    total = lax.dot_general(
                        left_buffer[pair, rows_at, columns],
                        right_buffer[pair, rows_at, :],
                        (((0,), (0,)), ((), ())),
                        preferred_element_type=jnp.float32,
                    )
                    parts[lax.rem(chunk, 2), p, pl.ds(offset, UNIT), :] = total.astype(
                        parts.dtype
                    )

    def far_copy(c):
        ring = lax.rem(c, 4)
        return remote(far_out.at[ring], far_in.at[ring], 2, lax.rem(c, RING), partners[1])

    def halve_copy(level, c):
        ring = lax.rem(c, 4)
        return remote(
            half_out[level].at[ring],
            half_in[level].at[ring],
            3 + level,
            lax.rem(c, RING),
            partners[2 + level],
        )

    def join_copy(level, c):
        at = lax.rem(c, RING)
        size = rows >> (level + 1)
        offset = sum(bits[i] * (rows >> (i + 1)) for i in range(level + 1))
        where = pl.ds(pl.multiple_of(offset, size), size)
        return remote(
            full.at[at, where], full.at[at, where], 3 + levels + level, at, partners[2 + level]
        )

    def store(c):
        at = lax.rem(c, RING)
        return pltpu.make_async_copy(full.at[at], out.at[c], store_sem.at[at])

    def add(target, left, right, size):
        tile = min(size, 32)

        @pl.loop(0, size // tile)
        def _(i):
            at = pl.ds(pl.multiple_of(i * tile, tile), tile)
            total = left[at, :].astype(jnp.float32) + right[at, :].astype(jnp.float32)
            target[at, :] = total.astype(target.dtype)

    def small_core_copies():
        return [
            pltpu.make_async_remote_copy(
                src_ref=small.at[source],
                dst_ref=small_core.at[i],
                send_sem=small_send.at[i],
                recv_sem=small_recv.at[i],
                device_id=partners[0],
                device_id_type=MESH,
            )
            for i, source in ((0, core), (1, far_core))
        ]

    def small_far_copy():
        return pltpu.make_async_remote_copy(
            src_ref=small_out_far,
            dst_ref=small_far,
            send_sem=small_send.at[2],
            recv_sem=small_recv.at[2],
            device_id=partners[1],
            device_id_type=MESH,
        )

    def small_slot_copy(level):
        return pltpu.make_async_remote_copy(
            src_ref=small_out_slot.at[level],
            dst_ref=small_in.at[level],
            send_sem=small_send.at[3 + level],
            recv_sem=small_recv.at[3 + level],
            device_id=partners[2 + level],
            device_id_type=MESH,
        )

    def small_stage(step):
        if step == 0:
            for copy in small_core_copies():
                copy.start()
        elif step == 1:
            for copy in small_core_copies():
                copy.wait()
            small_out_far[...] = small[far] + small_core[1]
            small_out[...] = small[pb] + small_core[0]
            small_far_copy().start()
        elif step == 2:
            small_far_copy().wait()
            small_out[...] = small_out[...] + small_far[...]
            small_out_slot[0] = small_out[...]
            small_slot_copy(0).start()
        else:
            level = step - 3
            small_slot_copy(level).wait()
            small_out[...] = small_out[...] + small_in[level]
            if level + 1 < levels:
                small_out_slot[level + 1] = small_out[...]
                small_slot_copy(level + 1).start()

    def stage(step, c):
        ring = lax.rem(c, 4)
        pair = lax.rem(c, 2)
        at = lax.rem(c, RING)
        if step == 0:
            for copy in core_copies(c):
                copy.start()
        elif step == 1:
            for copy in core_copies(c):
                copy.wait()
            add(far_out.at[ring], parts.at[pair, far], core_in.at[ring, 1], rows)
            far_copy(c).start()
            add(far_keep.at[ring], parts.at[pair, pb], core_in.at[ring, 0], rows)
        elif step < 2 + levels:
            level = step - 2
            size = rows >> (level + 1)
            if level == 0:
                far_copy(c).wait()
                left, right = far_keep.at[ring], far_in.at[ring]
            else:
                halve_copy(level - 1, c).wait()
                left, right = half_keep[level - 1].at[ring], half_in[level - 1].at[ring]
            mine = pl.ds(pl.multiple_of(bits[level] * size, size), size)
            other = pl.ds(pl.multiple_of((1 - bits[level]) * size, size), size)
            add(half_out[level].at[ring], left.at[other], right.at[other], size)
            halve_copy(level, c).start()
            add(half_keep[level].at[ring], left.at[mine], right.at[mine], size)
        elif step == 2 + levels:
            level = levels - 1
            size = rows >> levels
            halve_copy(level, c).wait()
            offset = sum(bits[i] * (rows >> (i + 1)) for i in range(levels))
            where = pl.ds(pl.multiple_of(offset, size), size)
            add(full.at[at, where], half_keep[level].at[ring], half_in[level].at[ring], size)
            join_copy(level, c).start()
        elif step < 2 + 2 * levels:
            level = levels - 1 - (step - 3 - levels)
            join_copy(level, c).wait()
            join_copy(level - 1, c).start()
        elif step == 2 + 2 * levels:
            join_copy(0, c).wait()
            store(c).start()
        else:
            store(c).wait()

    stages = 4 + 2 * levels

    per = rows // UNIT
    load(jnp.int32(0))

    @pl.loop(0, count + stages)
    def _(it):
        for step in range(3 + levels):

            @pl.when(it == step)
            def _():
                small_stage(step)

        for step in range(stages):
            c = it - 1 - step

            @pl.when(jnp.logical_and(c >= 0, c < count))
            def _():
                stage(step, c)

        for i in range(per):

            @pl.when(it < count)
            def _():
                unit = it * per + i
                load(unit + 1)
                product(unit, it, i * UNIT)


def sync_gradients(plan, operands, small):
    slots = lax.axis_size("slot")
    rows, columns = max(UNIT, 16 * slots), D
    count = len(plan) * UNIT // rows
    levels = slots.bit_length() - 1
    small_rows = small.shape[1:]
    low = jnp.bfloat16
    longest = max(operand.shape[0] for operand in operands)
    block = lambda *lead: pltpu.VMEM(lead + (columns,), low)
    halves = [block(4, rows >> (i + 1)) for i in range(levels)]
    used = len(operands)

    def kernel(*refs):
        small_ref, out, small_out = refs[used : used + 3]
        sync_kernel(slots, count, plan, refs[:used], small_ref, out, small_out, refs[used + 3 :])

    return pl.pallas_call(
        kernel,
        out_shape=(
            jax.ShapeDtypeStruct((count, rows, columns), low),
            jax.ShapeDtypeStruct(small_rows, jnp.float32),
        ),
        in_specs=[pl.BlockSpec(memory_space=pl.ANY)] * used
        + [pl.BlockSpec(memory_space=pltpu.VMEM)],
        out_specs=(
            pl.BlockSpec(memory_space=pl.ANY),
            pl.BlockSpec(memory_space=pltpu.VMEM),
        ),
        scratch_shapes=[
            block(2, longest),
            block(2, longest),
            block(2, 4, rows),
            block(4, 2, rows),
            block(4, rows),
            block(4, rows),
            block(4, rows),
            halves,
            halves,
            halves,
            block(RING, rows),
            pltpu.VMEM((2,) + small_rows, jnp.float32),
            pltpu.VMEM(small_rows, jnp.float32),
            pltpu.VMEM((levels,) + small_rows, jnp.float32),
            pltpu.VMEM(small_rows, jnp.float32),
            pltpu.VMEM((levels,) + small_rows, jnp.float32),
            pltpu.SemaphoreType.DMA((2, 2)),
            pltpu.SemaphoreType.DMA((RING,)),
            pltpu.SemaphoreType.DMA((3 + 2 * levels, RING)),
            pltpu.SemaphoreType.DMA((3 + 2 * levels, RING)),
            pltpu.SemaphoreType.DMA((3 + levels,)),
            pltpu.SemaphoreType.DMA((3 + levels,)),
        ],
        compiler_params=pltpu.CompilerParams(
            collective_id=1, has_side_effects=True, vmem_limit_bytes=56 << 20
        ),
    )(*operands, small)


EVERY = ("slot", "pb")


def code_bits():
    return [("slot", mask) for mask in masks_below(lax.axis_size("slot"))[::-1]] + [
        ("pb", mask) for mask in masks_below(lax.axis_size("pb"))[::-1]
    ]


def exchange_parts(bits):
    slot_bits = [i for i, (name, mask) in enumerate(bits) if name == "slot"]
    pb_bits = [i for i, (name, mask) in enumerate(bits) if name == "pb"]
    high, low, far, near = slot_bits[:-1], slot_bits[-1:], pb_bits[:-1], pb_bits[-1:]
    first, second = high + low + far + near, far + high + low + near
    return [
        (0, 256, first),
        (256, 256, second),
        (512, 256, first),
        (768, 128, second),
        (896, 128, low + far + high + near),
    ]


def partner_of(bit):
    name, mask = bit
    slot, pb = lax.axis_index("slot"), lax.axis_index("pb")
    return (xor(slot, mask), pb) if name == "slot" else (slot, xor(pb, mask))


def meet(partners):
    barrier = pltpu.get_barrier_semaphore()
    for partner in partners:
        pl.semaphore_signal(barrier, inc=1, device_id=partner, device_id_type=MESH)
    pl.semaphore_wait(barrier, len(partners))


def within(held, count, fixed, value, columns):
    lead = [pl.ds(0, 2) if i in held else 0 for i in range(count)]
    if fixed is not None:
        lead[fixed] = value
    return tuple(lead) + (slice(None), columns)


def gather_kernel(bits, parts, own, out, local_sem, send_sem, recv_sem):
    count = len(bits)
    partners = [partner_of(bit) for bit in bits]
    meet(partners)
    local = pltpu.make_async_copy(
        own, out.at[within([], count, None, 0, slice(None))], local_sem
    )
    local.start()
    pending = [None] * len(parts)
    for step in range(count):
        for p, (start, width, order) in enumerate(parts):
            columns = pl.ds(start, width)
            if step > 0:
                pending[p].wait()
            if step == 1 and p == 0:
                local.wait()
            bit = order[step]
            held = order[:step]
            source = (
                own.at[:, columns] if step == 0 else out.at[within(held, count, None, 0, columns)]
            )
            pending[p] = pltpu.make_async_remote_copy(
                src_ref=source,
                dst_ref=out.at[within(held, count, bit, 1, columns)],
                send_sem=send_sem.at[p, step],
                recv_sem=recv_sem.at[p, step],
                device_id=partners[bit],
                device_id_type=MESH,
            )
            pending[p].start()
    for copy in pending:
        copy.wait()


def gather_states(own):
    bits = code_bits()
    parts = exchange_parts(bits)
    out = pl.pallas_call(
        functools.partial(gather_kernel, bits, parts),
        out_shape=jax.ShapeDtypeStruct((2,) * len(bits) + own.shape, own.dtype),
        in_specs=[pl.BlockSpec(memory_space=pl.ANY)],
        out_specs=pl.BlockSpec(memory_space=pl.ANY),
        scratch_shapes=[
            pltpu.SemaphoreType.DMA,
            pltpu.SemaphoreType.DMA((len(parts), len(bits))),
            pltpu.SemaphoreType.DMA((len(parts), len(bits))),
        ],
        compiler_params=pltpu.CompilerParams(collective_id=2, has_side_effects=True),
    )(own)
    return out.reshape(-1, own.shape[-1])


def scatter_kernel(bits, parts, shares, out, held, near_in, came, load_sem, send_sem, recv_sem):
    count = len(bits)
    partners = [partner_of(bit) for bit in bits]
    near = count - 1
    meet(partners)

    def codes(free):
        out = [()]
        for i in range(near):
            out = [code + (bit,) for code in out for bit in ((0, 1) if i in free else (0,))]
        return out

    def add(target, left, right):
        rows = target.shape[0]

        @pl.loop(0, rows // 32)
        def _(i):
            at = pl.ds(pl.multiple_of(i * 32, 32), 32)
            total = left[at, :].astype(jnp.float32) + right[at, :].astype(jnp.float32)
            target[at, :] = total.astype(target.dtype)

    pending = [None] * len(parts)
    loads = [None] * len(parts)
    for p, (start, width, order) in enumerate(parts):
        columns = pl.ds(start, width)
        every = list(range(near))
        pending[p] = pltpu.make_async_remote_copy(
            src_ref=shares.at[within(every, count, near, 1, columns)],
            dst_ref=near_in[p],
            send_sem=send_sem.at[p, 0],
            recv_sem=recv_sem.at[p, 0],
            device_id=partners[near],
            device_id_type=MESH,
        )
        pending[p].start()
        loads[p] = pltpu.make_async_copy(
            shares.at[within(every, count, near, 0, columns)], held[p], load_sem.at[p]
        )
        loads[p].start()
    for step in range(near):
        for p, (start, width, order) in enumerate(parts):
            turns = order[:-1][::-1]
            bit = turns[step]
            free = turns[step:]
            left = turns[step + 1 :]
            if step == 0:
                loads[p].wait()
            pending[p].wait()
            arrived = near_in[p] if step == 0 else came[p][step - 1]

            def merge(code):
                other = code if step == 0 else tuple(code[i] for i in sorted(free))
                add(held[p].at[code], held[p].at[code], arrived.at[other])

            for code in codes(free):
                if code[bit] == 1:
                    merge(code)
            lead = tuple(pl.ds(0, 2) if i in left else int(i == bit) for i in range(near))
            pending[p] = pltpu.make_async_remote_copy(
                src_ref=held[p].at[lead],
                dst_ref=came[p][step],
                send_sem=send_sem.at[p, step + 1],
                recv_sem=recv_sem.at[p, step + 1],
                device_id=partners[bit],
                device_id_type=MESH,
            )
            pending[p].start()
            for code in codes(free):
                if code[bit] == 0:
                    merge(code)
    for p, (start, width, order) in enumerate(parts):
        pending[p].wait()
        mine = (0,) * near
        out[:, pl.ds(start, width)] = held[p][mine].astype(jnp.float32) + came[p][near - 1][
            ...
        ].astype(jnp.float32)


def scatter_states(shares):
    bits = code_bits()
    parts = exchange_parts(bits)
    count = len(bits)
    low = jnp.bfloat16
    held = [pltpu.VMEM((2,) * (count - 1) + (TGT_LEN, width), low) for _, width, _ in parts]
    came = [
        [
            pltpu.VMEM((2,) * (count - 2 - step) + (TGT_LEN, width), low)
            for step in range(count - 1)
        ]
        for _, width, _ in parts
    ]
    return pl.pallas_call(
        functools.partial(scatter_kernel, bits, parts),
        out_shape=jax.ShapeDtypeStruct((TGT_LEN, D), jnp.float32),
        in_specs=[pl.BlockSpec(memory_space=pl.ANY)],
        out_specs=pl.BlockSpec(memory_space=pltpu.VMEM),
        scratch_shapes=[
            held,
            held,
            came,
            pltpu.SemaphoreType.DMA((len(parts),)),
            pltpu.SemaphoreType.DMA((len(parts), count)),
            pltpu.SemaphoreType.DMA((len(parts), count)),
        ],
        compiler_params=pltpu.CompilerParams(
            collective_id=3, has_side_effects=True, vmem_limit_bytes=56 << 20
        ),
    )(shares.reshape((2,) * count + (TGT_LEN, D)))


def merge_kernel(bits, stats, out, came, sent, send_sem, recv_sem):
    partners = [partner_of(bit) for bit in bits]
    meet(partners)
    count = len(bits)
    size = 1 << count
    out[...] = stats[...]
    position = lax.broadcasted_iota(jnp.int32, (size, TGT_LEN), 0)
    for step in range(count):
        mask = 1 << (count - 1 - step)
        sent[step] = out[...]
        copy = pltpu.make_async_remote_copy(
            src_ref=sent.at[step],
            dst_ref=came.at[step],
            send_sem=send_sem.at[step],
            recv_sem=recv_sem.at[step],
            device_id=partners[step],
            device_id_type=MESH,
        )
        copy.start()
        copy.wait()
        lower = (position // mask) % 2 == 0
        other = [
            jnp.where(
                lower,
                pltpu.roll(came[step, i], size - mask, 0),
                pltpu.roll(came[step, i], mask, 0),
            )
            for i in range(3)
        ]
        top = jnp.maximum(out[0], other[0])
        out[1] = out[1] * jnp.exp(out[0] - top) + other[1] * jnp.exp(other[0] - top)
        out[0] = top
        out[2] = out[2] + other[2]


def merge_stats(stats):
    bits = code_bits()
    shape = stats.shape
    return pl.pallas_call(
        functools.partial(merge_kernel, bits),
        out_shape=jax.ShapeDtypeStruct(shape, jnp.float32),
        in_specs=[pl.BlockSpec(memory_space=pltpu.VMEM)],
        out_specs=pl.BlockSpec(memory_space=pltpu.VMEM),
        scratch_shapes=[
            pltpu.VMEM((len(bits),) + shape, jnp.float32),
            pltpu.VMEM((len(bits),) + shape, jnp.float32),
            pltpu.SemaphoreType.DMA((len(bits),)),
            pltpu.SemaphoreType.DMA((len(bits),)),
        ],
        compiler_params=pltpu.CompilerParams(collective_id=4, has_side_effects=True),
    )(stats)


def own_facts(targets, owner, doc_scores):
    serving = jnp.arange(targets.shape[1]) == owner[0, 0]
    own = jnp.sum(jnp.where(serving[:, None], targets[0], 0), axis=0)
    half = (TGT_LEN // 2,)
    return jnp.concatenate(
        [
            own.astype(jnp.float32),
            jnp.broadcast_to(owner[0, 0].astype(jnp.float32), half),
            jnp.broadcast_to(doc_scores[0, 0], half),
        ]
    )


def vocabulary_head(state_low, facts, questions, embed):
    slots, groups = lax.axis_size("slot"), lax.axis_size("pb")
    me = lax.axis_index("slot") * groups + lax.axis_index("pb")
    entries = embed.shape[0]
    tokens = slots * groups * TGT_LEN
    target_ids = facts[:, :TGT_LEN].astype(jnp.int32).reshape(tokens, 1)
    owners = facts[:, TGT_LEN].astype(jnp.int32).reshape(slots, groups)
    scores = facts[:, TGT_LEN + TGT_LEN // 2].reshape(slots, groups)
    states = gather_states(state_low)
    logits = matmul_nt(states, embed)
    hit = target_ids - me * entries == lax.broadcasted_iota(jnp.int32, (tokens, entries), 1)
    top = jnp.max(logits, axis=1)
    total = jnp.sum(jnp.exp(logits - top[:, None]), axis=1)
    pick = jnp.sum(jnp.where(hit, logits, 0.0), axis=1)
    merged = merge_stats(jnp.stack([top, total, pick]).reshape(3, -1, TGT_LEN))
    log_total = (merged[0] + jnp.log(merged[1])).reshape(tokens)
    picked = merged[2].reshape(slots, groups, TGT_LEN) - log_total.reshape(slots, groups, TGT_LEN)
    serving = owners[:, :, None] == jnp.arange(questions)
    score_terms = jnp.where(serving, scores[:, :, None], BIG_NEGATIVE)
    token_terms = jnp.where(
        serving[..., None], (scores[:, :, None] + picked)[:, :, None, :], BIG_NEGATIVE
    )
    score_top, token_top = jnp.max(score_terms, axis=0), jnp.max(token_terms, axis=0)
    score_norm = score_top + jnp.log(jnp.sum(jnp.exp(score_terms - score_top), axis=0))
    token_mix = token_top + jnp.log(jnp.sum(jnp.exp(token_terms - token_top), axis=0))
    group_tokens = questions * TGT_LEN
    count = groups * group_tokens
    losses = -jnp.sum(token_mix - score_norm[:, :, None], axis=(1, 2)) / group_tokens
    own_mix = jnp.sum(jnp.where(serving[..., None], token_mix[None], 0.0), axis=2)
    own_norm = jnp.sum(jnp.where(serving, score_norm[None], 0.0), axis=2)
    posterior = jnp.exp(scores[:, :, None] + picked - own_mix)
    prior = jnp.exp(scores - own_norm)
    token_grad = (-posterior / count).reshape(tokens, 1)
    score_grads = -jnp.sum(posterior - prior[:, :, None], axis=2) / count
    delta = to_low(
        token_grad * (jnp.where(hit, 1.0, 0.0) - jnp.exp(logits - log_total[:, None]))
    )
    grad_state = scatter_states(to_low(matmul(delta, embed)))
    return (losses[:1], score_grads[:1, :1], grad_state, delta, states)


def local(
    enc_input,
    dec_input,
    doc_scores,
    owner,
    targets,
    enc_attn,
    enc_up,
    enc_down,
    enc_up_bias,
    enc_bias,
    enc_gain,
    dec_self,
    dec_cross,
    dec_up,
    dec_down,
    dec_up_bias,
    dec_bias,
    dec_gain,
    embed,
):
    pb_size = lax.axis_size("pb")
    width = D // pb_size
    vectors = (enc_up_bias, enc_bias, enc_gain, dec_up_bias, dec_bias, dec_gain)
    rows = [v.size // width for v in vectors]
    starts = [sum(rows[:i]) for i in range(len(rows) + 1)]
    passage_low = enc_input[0, 0]
    passage = passage_low.astype(jnp.float32)
    question_low = dec_input[0, 0]
    question = question_low.astype(jnp.float32)

    full = []
    ticker = Ticker()
    ticker.add(
        gather_small(jnp.concatenate([v.reshape(-1, width) for v in vectors]), ("pb",), full)
    )
    ticker.add(gather_rows(enc_attn, 1, full))
    ticker.tick()
    packed = natural_order(full[0], "pb").astype(jnp.float32)
    unpacked = [packed[:, starts[i] : starts[i + 1], :] for i in range(len(rows))]
    encoder_upbias = unpacked[0].reshape(-1)
    encoder_bias = unpacked[1].transpose(1, 0, 2).reshape(-1, D)
    encoder_gain = unpacked[2].transpose(1, 0, 2).reshape(-1, D)
    decoder_upbias = unpacked[3].reshape(-1)
    decoder_bias = unpacked[4].transpose(1, 0, 2).reshape(-1, D)
    decoder_gain = unpacked[5].transpose(1, 0, 2).reshape(-1, D)
    ticker.add(gather_rows(enc_up, 0, full))
    ticker.tick()
    encoder_attn = full[1]
    ticker.add(gather_rows(enc_down, 0, full))
    attn_out, enc_saved = attend_forward(
        passage_low,
        passage_low,
        encoder_attn,
        encoder_bias[0],
        encoder_bias[1],
        encoder_bias[2],
        False,
    )
    attn_out = ticker.tick(attn_out)
    encoder_up = full[2]
    ticker.add(gather_rows(dec_self, 1, full))
    enc_first, enc_norm_one = norm_forward(passage + attn_out, encoder_gain[0], encoder_bias[3])
    enc_first_low = to_low(enc_first)
    enc_before = matmul(enc_first_low, encoder_up) + encoder_upbias
    enc_hidden_low = to_low(gelu_exact(enc_before))
    enc_hidden_low, enc_before = ticker.tick(enc_hidden_low, enc_before)
    encoder_down = full[3]
    ticker.add(gather_rows(dec_cross, 1, full))
    ticker.add(gather_small(own_facts(targets, owner, doc_scores), EVERY[::-1], full))
    ffn_out = matmul(enc_hidden_low, encoder_down) + encoder_bias[4]
    encoded, enc_norm_two = norm_forward(enc_first + ffn_out, encoder_gain[1], encoder_bias[5])
    memory_low = to_low(encoded)
    memory_low = ticker.tick(memory_low)
    decoder_self = full[4]
    facts = full[5]
    ticker.add(gather_rows(dec_up, 0, full))
    self_out, self_saved = attend_forward(
        question_low,
        question_low,
        decoder_self,
        decoder_bias[0],
        decoder_bias[1],
        decoder_bias[2],
        True,
    )
    dec_first, dec_norm_one = norm_forward(question + self_out, decoder_gain[0], decoder_bias[3])
    dec_first = ticker.tick(dec_first)
    dec_first_low = to_low(dec_first)
    decoder_cross = full[6]
    ticker.add(gather_rows(dec_down, 0, full))
    cross_out, cross_saved = attend_forward(
        dec_first_low,
        memory_low,
        decoder_cross,
        decoder_bias[4],
        decoder_bias[5],
        decoder_bias[6],
        False,
    )
    dec_second, dec_norm_two = norm_forward(dec_first + cross_out, decoder_gain[1], decoder_bias[7])
    dec_second = ticker.tick(dec_second)
    dec_second_low = to_low(dec_second)
    decoder_up = full[7]
    dec_before = matmul(dec_second_low, decoder_up) + decoder_upbias
    dec_hidden_low = to_low(gelu_exact(dec_before))
    dec_hidden_low, dec_before = ticker.tick(dec_hidden_low, dec_before)
    decoder_down = full[8]
    dec_ffn_out = matmul(dec_hidden_low, decoder_down) + decoder_bias[8]
    state, dec_norm_three = norm_forward(dec_second + dec_ffn_out, decoder_gain[2], decoder_bias[9])
    state_low = to_low(state)

    loss, score_grad, grad_state_sum, delta, states = vocabulary_head(
        state_low, facts, targets.shape[1], embed
    )

    embed_grad = matmul_tn(delta, states)
    grad_third, gain_third, shift_third = norm_backward(
        grad_state_sum, dec_norm_three, decoder_gain[2]
    )
    dec_downbias_grad = jnp.sum(grad_third, axis=0)
    third_low = to_low(grad_third)
    grad_before = hidden_backward(third_low, decoder_down, dec_before)
    dec_upbias_grad = jnp.sum(grad_before, axis=0)
    before_low = to_low(grad_before)
    grad_second, gain_second, shift_second = norm_backward(
        grad_third + matmul_nt(before_low, decoder_up), dec_norm_two, decoder_gain[1]
    )
    cross_query, grad_memory, dec_cross_pairs, cross_biases = attend_backward(
        grad_second, dec_first_low, memory_low, decoder_cross, cross_saved
    )
    grad_first, gain_first, shift_first = norm_backward(
        grad_second + cross_query, dec_norm_one, decoder_gain[0]
    )
    self_query, self_memory, dec_self_pairs, self_biases = attend_backward(
        grad_first, question_low, question_low, decoder_self, self_saved
    )
    question_grad = grad_first + self_query + self_memory
    enc_grad_two, enc_gain_two, enc_shift_two = norm_backward(
        grad_memory, enc_norm_two, encoder_gain[1]
    )
    enc_downbias_grad = jnp.sum(enc_grad_two, axis=0)
    enc_two_low = to_low(enc_grad_two)
    enc_grad_before = hidden_backward(enc_two_low, encoder_down, enc_before)
    enc_upbias_grad = jnp.sum(enc_grad_before, axis=0)
    enc_before_low = to_low(enc_grad_before)
    enc_grad_one, enc_gain_one, enc_shift_one = norm_backward(
        enc_grad_two + matmul_nt(enc_before_low, encoder_up), enc_norm_one, encoder_gain[0]
    )
    enc_query, enc_memory, enc_attn_pairs, enc_biases = attend_backward(
        enc_grad_one, passage_low, passage_low, encoder_attn, enc_saved
    )
    passage_grad = enc_grad_one + enc_query + enc_memory
    operands, plan = [], []

    def share(left, right, tall=False):
        where = []
        for operand in (left, right):
            known = [i for i, other in enumerate(operands) if other is operand]
            where.append(known[0] if known else len(operands))
            if not known:
                operands.append(operand)
        for i in range(left.shape[1] * right.shape[1] // (D * D)):
            plan.append((where[0], where[1], i, tall))

    for left, right in enc_attn_pairs:
        share(left, right)
    share(enc_first_low, enc_before_low)
    share(enc_hidden_low, enc_two_low, tall=True)
    for left, right in dec_self_pairs + dec_cross_pairs:
        share(left, right)
    share(dec_second_low, before_low)
    share(dec_hidden_low, third_low, tall=True)
    enc_bias_grad = jnp.stack(
        [
            enc_biases[0],
            enc_biases[1],
            enc_biases[2],
            enc_shift_one,
            enc_downbias_grad,
            enc_shift_two,
        ]
    )
    enc_gain_grad = jnp.stack([enc_gain_one, enc_gain_two])
    dec_bias_grad = jnp.stack(
        [
            self_biases[0],
            self_biases[1],
            self_biases[2],
            shift_first,
            cross_biases[0],
            cross_biases[1],
            cross_biases[2],
            shift_second,
            dec_downbias_grad,
            shift_third,
        ]
    )
    dec_gain_grad = jnp.stack([gain_first, gain_second, gain_third])
    vector_grads = jnp.concatenate(
        [
            enc_upbias_grad.reshape(pb_size, -1, width),
            enc_bias_grad.reshape(-1, pb_size, width).transpose(1, 0, 2),
            enc_gain_grad.reshape(-1, pb_size, width).transpose(1, 0, 2),
            dec_upbias_grad.reshape(pb_size, -1, width),
            dec_bias_grad.reshape(-1, pb_size, width).transpose(1, 0, 2),
            dec_gain_grad.reshape(-1, pb_size, width).transpose(1, 0, 2),
        ],
        axis=1,
    )
    spare = -starts[-1] % 32
    small = jnp.pad(vector_grads, ((0, 0), (0, spare), (0, 0))).reshape(pb_size, -1, D)
    summed_parts, small_sum = sync_gradients(plan, operands, small)
    units = summed_parts.reshape(-1, width, D)
    square = lambda at: units[at : at + 4].astype(jnp.float32)
    wide = lambda at: jnp.concatenate([units[at + i].astype(jnp.float32) for i in range(4)], axis=1)
    tall = lambda at: square(at).reshape(-1, D)
    vector_sum = small_sum.reshape(-1, width)
    vector_out = [
        vector_sum[starts[i] : starts[i + 1]].reshape(v.shape) for i, v in enumerate(vectors)
    ]
    summed = (
        (square(0), wide(4), tall(8))
        + tuple(vector_out[:3])
        + (square(12), square(16), wide(20), tall(24))
        + tuple(vector_out[3:])
    )
    return (
        (
            loss,
            passage_grad.reshape(1, 1, SRC_LEN, D),
            question_grad.reshape(1, 1, TGT_LEN, D),
            score_grad,
        )
        + tuple(summed)
        + (embed_grad,)
    )


def solution(mesh):
    placed = (
        P("pb", "slot", None, None),
        P("pb", "slot", None, None),
        P("pb", "slot"),
        P("pb", "slot"),
        P("pb", None, None),
        P(None, "pb", None),
        P("pb", None),
        P("pb", None),
        P("pb"),
        P(None, "pb"),
        P(None, "pb"),
        P(None, "pb", None),
        P(None, "pb", None),
        P("pb", None),
        P("pb", None),
        P("pb"),
        P(None, "pb"),
        P(None, "pb"),
        P(("slot", "pb"), None),
    )
    return jax.shard_map(
        local,
        mesh=mesh,
        in_specs=placed,
        out_specs=(
            P("pb"),
            P("pb", "slot", None, None),
            P("pb", "slot", None, None),
            P("pb", "slot"),
            P(None, "pb", None),
            P("pb", None),
            P("pb", None),
            P("pb"),
            P(None, "pb"),
            P(None, "pb"),
            P(None, "pb", None),
            P(None, "pb", None),
            P("pb", None),
            P("pb", None),
            P("pb"),
            P(None, "pb"),
            P(None, "pb"),
            P(("slot", "pb"), None),
        ),
        check_vma=False,
    )
```

```python
import functools
import math

import jax
import jax.numpy as jnp
from jax import lax
from jax.experimental import pallas as pl
from jax.experimental.pallas import tpu as pltpu
from jax.sharding import PartitionSpec as P

D = 1024
HEADS = 16
HEAD_DIM = 64
SRC_LEN = 384
TGT_LEN = 128
MESH = pl.DeviceIdType.MESH
UNIT = 256
RING = 8


BIG_NEGATIVE = -1e30
MASK_FILL = -1000000000.0


def matmul(left, right):
    return jnp.dot(left, right, preferred_element_type=jnp.float32)


def matmul_nt(left, right):
    return lax.dot_general(
        left, right, (((1,), (1,)), ((), ())), preferred_element_type=jnp.float32
    )


def matmul_tn(left, right):
    return lax.dot_general(
        left, right, (((0,), (0,)), ((), ())), preferred_element_type=jnp.float32
    )


def to_low(value):
    return value.astype(jnp.bfloat16)


def norm_forward(total, gain, shift):
    centered = total - jnp.mean(total, axis=-1, keepdims=True)
    inverse = lax.rsqrt(jnp.mean(centered * centered, axis=-1, keepdims=True) + 1e-05)
    normed = centered * inverse
    return (normed * gain + shift, (normed, inverse))


def norm_backward(upstream, saved, gain):
    normed, inverse = saved
    scaled = upstream * gain
    inner = (
        scaled
        - jnp.mean(scaled, axis=-1, keepdims=True)
        - normed * jnp.mean(scaled * normed, axis=-1, keepdims=True)
    )
    return (inverse * inner, jnp.sum(upstream * normed, axis=0), jnp.sum(upstream, axis=0))


def head_mask(which):
    return lax.broadcasted_iota(jnp.int32, (1, 2 * HEAD_DIM), 1) // HEAD_DIM == which


def only_head(pair, which):
    return jnp.where(head_mask(which), pair.astype(jnp.float32), 0.0).astype(pair.dtype)


def both_heads(first, second):
    return jnp.where(head_mask(0), first, second)


def attention_weights(queries, keys, causal):
    scores = matmul_nt(queries, keys) * HEAD_DIM ** (-0.5)
    if causal:
        rows = lax.broadcasted_iota(jnp.int32, scores.shape, 0)
        columns = lax.broadcasted_iota(jnp.int32, scores.shape, 1)
        scores = jnp.where(rows >= columns, scores, MASK_FILL)
    shifted = jnp.exp(scores - jnp.max(scores, axis=-1, keepdims=True))
    return shifted / jnp.sum(shifted, axis=-1, keepdims=True)


def attend_kernel(causal, queries, keys, values, out):
    parts = []
    for which in range(2):
        probs = attention_weights(only_head(queries[...], which), keys[...], causal)
        parts.append(matmul(to_low(probs), values[...]))
    out[...] = to_low(both_heads(*parts))


def attend_grad_kernel(
    causal, queries, keys, values, upstream, grad_q, grad_k, grad_v, sum_q, sum_v
):
    parts = []
    for which in range(2):
        probs = attention_weights(only_head(queries[...], which), keys[...], causal)
        grad_probs = matmul_nt(only_head(upstream[...], which), values[...])
        inner = jnp.sum(grad_probs * probs, axis=-1, keepdims=True)
        grad_scores = to_low(probs * (grad_probs - inner))
        parts.append(
            (
                matmul(grad_scores, keys[...]),
                matmul_tn(grad_scores, queries[...]),
                matmul_tn(to_low(probs), upstream[...]),
            )
        )
    scale = HEAD_DIM ** (-0.5)
    query, key, value = [both_heads(*pair) for pair in zip(*parts)]
    query = query * scale
    grad_q[...] = to_low(query)
    grad_k[...] = to_low(key * scale)
    grad_v[...] = to_low(value)
    sum_q[...] = jnp.broadcast_to(jnp.sum(query, axis=0, keepdims=True), sum_q.shape)
    sum_v[...] = jnp.broadcast_to(jnp.sum(value, axis=0, keepdims=True), sum_v.shape)


def head_pairs(rows):
    return pl.BlockSpec((rows, 2 * HEAD_DIM), lambda pair: (0, pair))


def attention_cost(rows, columns, products):
    return pl.CostEstimate(
        flops=2 * products * rows * columns * D,
        bytes_accessed=4 * (rows + columns) * D * products,
        transcendentals=HEADS * rows * columns,
    )


def attend_forward(query_low, memory_low, matrices, bias_query, bias_value, bias_out, causal):
    rows, columns = query_low.shape[0], memory_low.shape[0]
    queries = to_low(matmul(query_low, matrices[0]) + bias_query)
    keys = to_low(matmul(memory_low, matrices[1]))
    values = to_low(matmul(memory_low, matrices[2]) + bias_value)
    context = pl.pallas_call(
        functools.partial(attend_kernel, causal),
        grid=(HEADS // 2,),
        out_shape=jax.ShapeDtypeStruct((rows, D), jnp.bfloat16),
        in_specs=[head_pairs(rows), head_pairs(columns), head_pairs(columns)],
        out_specs=head_pairs(rows),
        cost_estimate=attention_cost(rows, columns, 2),
        compiler_params=pltpu.CompilerParams(vmem_limit_bytes=24 << 20),
    )(queries, keys, values)
    output = matmul(context, matrices[3]) + bias_out
    return (output, (queries, keys, values, context))


def attend_backward(upstream, query_low, memory_low, matrices, saved, causal):
    queries, keys, values, context = saved
    rows, columns = query_low.shape[0], memory_low.shape[0]
    upstream_low = to_low(upstream)
    grad_context = to_low(matmul_nt(upstream_low, matrices[3]))
    low, sums = jnp.bfloat16, jax.ShapeDtypeStruct((8, D), jnp.float32)
    queries_low, keys_low, values_low, query_sum, value_sum = pl.pallas_call(
        functools.partial(attend_grad_kernel, causal),
        grid=(HEADS // 2,),
        out_shape=(
            jax.ShapeDtypeStruct((rows, D), low),
            jax.ShapeDtypeStruct((columns, D), low),
            jax.ShapeDtypeStruct((columns, D), low),
            sums,
            sums,
        ),
        in_specs=[head_pairs(n) for n in (rows, columns, columns, rows)],
        out_specs=tuple(head_pairs(n) for n in (rows, columns, columns, 8, 8)),
        cost_estimate=attention_cost(rows, columns, 5),
        compiler_params=pltpu.CompilerParams(vmem_limit_bytes=24 << 20),
    )(queries, keys, values, grad_context)
    grad_query_input = matmul_nt(queries_low, matrices[0])
    grad_memory_input = matmul_nt(keys_low, matrices[1]) + matmul_nt(values_low, matrices[2])
    grad_pairs = [
        (query_low, queries_low),
        (memory_low, keys_low),
        (memory_low, values_low),
        (context, upstream_low),
    ]
    bias_grads = (query_sum[0], value_sum[0], jnp.sum(upstream, axis=0))
    return (grad_query_input, grad_memory_input, grad_pairs, bias_grads)


def gelu_with_slope(value):
    share = 0.5 * (1.0 + lax.erf(value * 0.5**0.5))
    density = jnp.exp(-0.5 * value * value) * (2.0 * math.pi) ** -0.5
    return value * share, share + value * density


def masks_below(size):
    return [1 << i for i in range(size.bit_length() - 1)]


def xor(value, mask):
    return jnp.where((value // mask) % 2 == 0, value + mask, value - mask)


def sync_kernel(slots, count, plan, operands, small, out, small_out, scratch):
    left_buffer, right_buffer, parts, core_in, far_out, far_keep, far_in = scratch[:7]
    half_out, half_keep, half_in, full = scratch[7:11]
    small_core, small_far, small_in, small_out_far, small_out_slot = scratch[11:16]
    load_sem, store_sem, send_sem, recv_sem, small_send, small_recv = scratch[16:]
    masks = masks_below(slots)
    levels = len(masks)
    rows = full.shape[1]
    slot, pb = lax.axis_index("slot"), lax.axis_index("pb")
    core, far = xor(pb, 1), xor(pb, 2)
    far_core = xor(core, 2)
    partners = [(slot, core), (slot, far)] + [(xor(slot, mask), pb) for mask in masks]
    bits = [(slot // mask) % 2 for mask in masks]

    barrier = pltpu.get_barrier_semaphore()
    for partner in partners:
        pl.semaphore_signal(barrier, inc=1, device_id=partner, device_id_type=MESH)
    pl.semaphore_wait(barrier, len(partners))

    def remote(source, target, stage, at, partner):
        return pltpu.make_async_remote_copy(
            src_ref=source,
            dst_ref=target,
            send_sem=send_sem.at[stage, at],
            recv_sem=recv_sem.at[stage, at],
            device_id=partner,
            device_id_type=MESH,
        )

    def core_copies(c):
        at = lax.rem(c, RING)
        ring = lax.rem(c, 4)
        pair = lax.rem(c, 2)
        return (
            remote(parts.at[pair, core], core_in.at[ring, 0], 0, at, partners[0]),
            remote(parts.at[pair, far_core], core_in.at[ring, 1], 1, at, partners[0]),
        )

    def load(unit):
        pair = lax.rem(unit, 2)
        for at, (left, right, k, tall) in enumerate(plan):

            @pl.when(unit == at)
            def _():
                tokens = operands[left].shape[0]
                rows_at = pl.ds(0, tokens)
                if tall:
                    for p in range(4):
                        pltpu.make_async_copy(
                            operands[left].at[:, pl.ds((4 * p + k) * UNIT, UNIT)],
                            left_buffer.at[pair, rows_at, pl.ds(p * UNIT, UNIT)],
                            load_sem.at[0, pair],
                        ).start()
                else:
                    pltpu.make_async_copy(
                        operands[left], left_buffer.at[pair, rows_at], load_sem.at[0, pair]
                    ).start()
                column = 0 if tall else k * D
                pltpu.make_async_copy(
                    operands[right].at[:, pl.ds(column, D)],
                    right_buffer.at[pair, rows_at],
                    load_sem.at[1, pair],
                ).start()

    def product(unit, chunk, offset):
        pair = lax.rem(unit, 2)
        lengths = [operands[left].shape[0] for left, _, _, _ in plan]
        for tokens in sorted(set(lengths)):
            among = functools.reduce(
                jnp.logical_or, [unit == at for at, n in enumerate(lengths) if n == tokens]
            )

            @pl.when(among)
            def _():
                rows_at = pl.ds(0, tokens)
                for i, buffer in enumerate((left_buffer, right_buffer)):
                    whole = buffer.at[pair, rows_at]
                    pltpu.make_async_copy(whole, whole, load_sem.at[i, pair]).wait()

                @pl.loop(0, 4)
                def _(p):
                    columns = pl.ds(pl.multiple_of(p * UNIT, UNIT), UNIT)
                    total = lax.dot_general(
                        left_buffer[pair, rows_at, columns],
                        right_buffer[pair, rows_at, :],
                        (((0,), (0,)), ((), ())),
                        preferred_element_type=jnp.float32,
                    )
                    parts[lax.rem(chunk, 2), p, pl.ds(offset, UNIT), :] = total.astype(
                        parts.dtype
                    )

    def far_copy(c):
        ring = lax.rem(c, 4)
        return remote(far_out.at[ring], far_in.at[ring], 2, lax.rem(c, RING), partners[1])

    def halve_copy(level, c):
        ring = lax.rem(c, 4)
        return remote(
            half_out[level].at[ring],
            half_in[level].at[ring],
            3 + level,
            lax.rem(c, RING),
            partners[2 + level],
        )

    def join_copy(level, c):
        at = lax.rem(c, RING)
        size = rows >> (level + 1)
        offset = sum(bits[i] * (rows >> (i + 1)) for i in range(level + 1))
        where = pl.ds(pl.multiple_of(offset, size), size)
        return remote(
            full.at[at, where], full.at[at, where], 3 + levels + level, at, partners[2 + level]
        )

    def store(c):
        at = lax.rem(c, RING)
        return pltpu.make_async_copy(full.at[at], out.at[c], store_sem.at[at])

    def add(target, left, right, size):
        tile = min(size, 32)

        @pl.loop(0, size // tile)
        def _(i):
            at = pl.ds(pl.multiple_of(i * tile, tile), tile)
            total = left[at, :].astype(jnp.float32) + right[at, :].astype(jnp.float32)
            target[at, :] = total.astype(target.dtype)

    def small_core_copies():
        return [
            pltpu.make_async_remote_copy(
                src_ref=small.at[source],
                dst_ref=small_core.at[i],
                send_sem=small_send.at[i],
                recv_sem=small_recv.at[i],
                device_id=partners[0],
                device_id_type=MESH,
            )
            for i, source in ((0, core), (1, far_core))
        ]

    def small_far_copy():
        return pltpu.make_async_remote_copy(
            src_ref=small_out_far,
            dst_ref=small_far,
            send_sem=small_send.at[2],
            recv_sem=small_recv.at[2],
            device_id=partners[1],
            device_id_type=MESH,
        )

    def small_slot_copy(level):
        return pltpu.make_async_remote_copy(
            src_ref=small_out_slot.at[level],
            dst_ref=small_in.at[level],
            send_sem=small_send.at[3 + level],
            recv_sem=small_recv.at[3 + level],
            device_id=partners[2 + level],
            device_id_type=MESH,
        )

    def small_stage(step):
        if step == 0:
            for copy in small_core_copies():
                copy.start()
        elif step == 1:
            for copy in small_core_copies():
                copy.wait()
            small_out_far[...] = small[far] + small_core[1]
            small_out[...] = small[pb] + small_core[0]
            small_far_copy().start()
        elif step == 2:
            small_far_copy().wait()
            small_out[...] = small_out[...] + small_far[...]
            small_out_slot[0] = small_out[...]
            small_slot_copy(0).start()
        else:
            level = step - 3
            small_slot_copy(level).wait()
            small_out[...] = small_out[...] + small_in[level]
            if level + 1 < levels:
                small_out_slot[level + 1] = small_out[...]
                small_slot_copy(level + 1).start()

    def stage(step, c):
        ring = lax.rem(c, 4)
        pair = lax.rem(c, 2)
        at = lax.rem(c, RING)
        if step == 0:
            for copy in core_copies(c):
                copy.start()
        elif step == 1:
            for copy in core_copies(c):
                copy.wait()
            add(far_out.at[ring], parts.at[pair, far], core_in.at[ring, 1], rows)
            far_copy(c).start()
            add(far_keep.at[ring], parts.at[pair, pb], core_in.at[ring, 0], rows)
        elif step < 2 + levels:
            level = step - 2
            size = rows >> (level + 1)
            if level == 0:
                far_copy(c).wait()
                left, right = far_keep.at[ring], far_in.at[ring]
            else:
                halve_copy(level - 1, c).wait()
                left, right = half_keep[level - 1].at[ring], half_in[level - 1].at[ring]
            mine = pl.ds(pl.multiple_of(bits[level] * size, size), size)
            other = pl.ds(pl.multiple_of((1 - bits[level]) * size, size), size)
            add(half_out[level].at[ring], left.at[other], right.at[other], size)
            halve_copy(level, c).start()
            add(half_keep[level].at[ring], left.at[mine], right.at[mine], size)
        elif step == 2 + levels:
            level = levels - 1
            size = rows >> levels
            halve_copy(level, c).wait()
            offset = sum(bits[i] * (rows >> (i + 1)) for i in range(levels))
            where = pl.ds(pl.multiple_of(offset, size), size)
            add(full.at[at, where], half_keep[level].at[ring], half_in[level].at[ring], size)
            join_copy(level, c).start()
        elif step < 2 + 2 * levels:
            level = levels - 1 - (step - 3 - levels)
            join_copy(level, c).wait()
            join_copy(level - 1, c).start()
        elif step == 2 + 2 * levels:
            join_copy(0, c).wait()
            store(c).start()
        else:
            store(c).wait()

    stages = 4 + 2 * levels

    per = rows // UNIT
    load(jnp.int32(0))

    @pl.loop(0, count + stages)
    def _(it):
        for step in range(3 + levels):

            @pl.when(it == step)
            def _():
                small_stage(step)

        for step in range(stages):
            c = it - 1 - step

            @pl.when(jnp.logical_and(c >= 0, c < count))
            def _():
                stage(step, c)

        for i in range(per):

            @pl.when(it < count)
            def _():
                unit = it * per + i
                load(unit + 1)
                product(unit, it, i * UNIT)


def sync_gradients(plan, operands, small):
    slots = lax.axis_size("slot")
    rows, columns = max(UNIT, 16 * slots), D
    count = len(plan) * UNIT // rows
    levels = slots.bit_length() - 1
    small_rows = small.shape[1:]
    low = jnp.bfloat16
    longest = max(operand.shape[0] for operand in operands)
    block = lambda *lead: pltpu.VMEM(lead + (columns,), low)
    halves = [block(4, rows >> (i + 1)) for i in range(levels)]
    used = len(operands)

    def kernel(*refs):
        small_ref, out, small_out = refs[used : used + 3]
        sync_kernel(slots, count, plan, refs[:used], small_ref, out, small_out, refs[used + 3 :])

    return pl.pallas_call(
        kernel,
        out_shape=(
            jax.ShapeDtypeStruct((count, rows, columns), low),
            jax.ShapeDtypeStruct(small_rows, jnp.float32),
        ),
        in_specs=[pl.BlockSpec(memory_space=pl.ANY)] * used
        + [pl.BlockSpec(memory_space=pltpu.VMEM)],
        out_specs=(
            pl.BlockSpec(memory_space=pl.ANY),
            pl.BlockSpec(memory_space=pltpu.VMEM),
        ),
        scratch_shapes=[
            block(2, longest),
            block(2, longest),
            block(2, 4, rows),
            block(4, 2, rows),
            block(4, rows),
            block(4, rows),
            block(4, rows),
            halves,
            halves,
            halves,
            block(RING, rows),
            pltpu.VMEM((2,) + small_rows, jnp.float32),
            pltpu.VMEM(small_rows, jnp.float32),
            pltpu.VMEM((levels,) + small_rows, jnp.float32),
            pltpu.VMEM(small_rows, jnp.float32),
            pltpu.VMEM((levels,) + small_rows, jnp.float32),
            pltpu.SemaphoreType.DMA((2, 2)),
            pltpu.SemaphoreType.DMA((RING,)),
            pltpu.SemaphoreType.DMA((3 + 2 * levels, RING)),
            pltpu.SemaphoreType.DMA((3 + 2 * levels, RING)),
            pltpu.SemaphoreType.DMA((3 + levels,)),
            pltpu.SemaphoreType.DMA((3 + levels,)),
        ],
        compiler_params=pltpu.CompilerParams(
            collective_id=1, has_side_effects=True, vmem_limit_bytes=56 << 20
        ),
    )(*operands, small)


def code_bits():
    return [("slot", mask) for mask in masks_below(lax.axis_size("slot"))[::-1]] + [
        ("pb", mask) for mask in masks_below(lax.axis_size("pb"))[::-1]
    ]


def exchange_parts(bits):
    slot_bits = [i for i, (name, mask) in enumerate(bits) if name == "slot"]
    pb_bits = [i for i, (name, mask) in enumerate(bits) if name == "pb"]
    high, low, far, near = slot_bits[:-1], slot_bits[-1:], pb_bits[:-1], pb_bits[-1:]
    first, second = high + low + far + near, far + high + low + near
    return [
        (0, 256, first),
        (256, 256, second),
        (512, 256, first),
        (768, 128, second),
        (896, 128, low + far + high + near),
    ]


def partner_of(bit):
    name, mask = bit
    slot, pb = lax.axis_index("slot"), lax.axis_index("pb")
    return (xor(slot, mask), pb) if name == "slot" else (slot, xor(pb, mask))


def meet(partners):
    barrier = pltpu.get_barrier_semaphore()
    for partner in partners:
        pl.semaphore_signal(barrier, inc=1, device_id=partner, device_id_type=MESH)
    pl.semaphore_wait(barrier, len(partners))


def within(held, count, fixed, value, columns):
    lead = [pl.ds(0, 2) if i in held else 0 for i in range(count)]
    if fixed is not None:
        lead[fixed] = value
    return tuple(lead) + (slice(None), columns)


def gather_kernel(bits, parts, own, out, local_sem, send_sem, recv_sem):
    count = len(bits)
    partners = [partner_of(bit) for bit in bits]
    meet(partners)
    local = pltpu.make_async_copy(
        own, out.at[within([], count, None, 0, slice(None))], local_sem
    )
    local.start()
    pending = [None] * len(parts)
    for step in range(count):
        for p, (start, width, order) in enumerate(parts):
            columns = pl.ds(start, width)
            if step > 0:
                pending[p].wait()
            if step == 1 and p == 0:
                local.wait()
            bit = order[step]
            held = order[:step]
            source = (
                own.at[:, columns] if step == 0 else out.at[within(held, count, None, 0, columns)]
            )
            pending[p] = pltpu.make_async_remote_copy(
                src_ref=source,
                dst_ref=out.at[within(held, count, bit, 1, columns)],
                send_sem=send_sem.at[p, step],
                recv_sem=recv_sem.at[p, step],
                device_id=partners[bit],
                device_id_type=MESH,
            )
            pending[p].start()
    for copy in pending:
        copy.wait()


def gather_states(own):
    bits = code_bits()
    parts = exchange_parts(bits)
    out = pl.pallas_call(
        functools.partial(gather_kernel, bits, parts),
        out_shape=jax.ShapeDtypeStruct((2,) * len(bits) + own.shape, own.dtype),
        in_specs=[pl.BlockSpec(memory_space=pl.ANY)],
        out_specs=pl.BlockSpec(memory_space=pl.ANY),
        scratch_shapes=[
            pltpu.SemaphoreType.DMA,
            pltpu.SemaphoreType.DMA((len(parts), len(bits))),
            pltpu.SemaphoreType.DMA((len(parts), len(bits))),
        ],
        compiler_params=pltpu.CompilerParams(collective_id=2, has_side_effects=True),
    )(own)
    return out.reshape(-1, own.shape[-1])


def scatter_kernel(bits, parts, shares, out, held, near_in, came, load_sem, send_sem, recv_sem):
    count = len(bits)
    partners = [partner_of(bit) for bit in bits]
    near = count - 1
    meet(partners)

    def codes(free):
        out = [()]
        for i in range(near):
            out = [code + (bit,) for code in out for bit in ((0, 1) if i in free else (0,))]
        return out

    def add(target, left, right):
        rows = target.shape[0]

        @pl.loop(0, rows // 32)
        def _(i):
            at = pl.ds(pl.multiple_of(i * 32, 32), 32)
            total = left[at, :].astype(jnp.float32) + right[at, :].astype(jnp.float32)
            target[at, :] = total.astype(target.dtype)

    pending = [None] * len(parts)
    loads = [None] * len(parts)
    for p, (start, width, order) in enumerate(parts):
        columns = pl.ds(start, width)
        every = list(range(near))
        pending[p] = pltpu.make_async_remote_copy(
            src_ref=shares.at[within(every, count, near, 1, columns)],
            dst_ref=near_in[p],
            send_sem=send_sem.at[p, 0],
            recv_sem=recv_sem.at[p, 0],
            device_id=partners[near],
            device_id_type=MESH,
        )
        pending[p].start()
        loads[p] = pltpu.make_async_copy(
            shares.at[within(every, count, near, 0, columns)], held[p], load_sem.at[p]
        )
        loads[p].start()
    for step in range(near):
        for p, (start, width, order) in enumerate(parts):
            turns = order[:-1][::-1]
            bit = turns[step]
            free = turns[step:]
            left = turns[step + 1 :]
            if step == 0:
                loads[p].wait()
            pending[p].wait()
            arrived = near_in[p] if step == 0 else came[p][step - 1]

            def merge(code):
                other = code if step == 0 else tuple(code[i] for i in sorted(free))
                add(held[p].at[code], held[p].at[code], arrived.at[other])

            for code in codes(free):
                if code[bit] == 1:
                    merge(code)
            lead = tuple(pl.ds(0, 2) if i in left else int(i == bit) for i in range(near))
            pending[p] = pltpu.make_async_remote_copy(
                src_ref=held[p].at[lead],
                dst_ref=came[p][step],
                send_sem=send_sem.at[p, step + 1],
                recv_sem=recv_sem.at[p, step + 1],
                device_id=partners[bit],
                device_id_type=MESH,
            )
            pending[p].start()
            for code in codes(free):
                if code[bit] == 0:
                    merge(code)
    for p, (start, width, order) in enumerate(parts):
        pending[p].wait()
        mine = (0,) * near
        out[:, pl.ds(start, width)] = held[p][mine].astype(jnp.float32) + came[p][near - 1][
            ...
        ].astype(jnp.float32)


def scatter_states(shares):
    bits = code_bits()
    parts = exchange_parts(bits)
    count = len(bits)
    low = jnp.bfloat16
    held = [pltpu.VMEM((2,) * (count - 1) + (TGT_LEN, width), low) for _, width, _ in parts]
    came = [
        [
            pltpu.VMEM((2,) * (count - 2 - step) + (TGT_LEN, width), low)
            for step in range(count - 1)
        ]
        for _, width, _ in parts
    ]
    return pl.pallas_call(
        functools.partial(scatter_kernel, bits, parts),
        out_shape=jax.ShapeDtypeStruct((TGT_LEN, D), jnp.float32),
        in_specs=[pl.BlockSpec(memory_space=pl.ANY)],
        out_specs=pl.BlockSpec(memory_space=pltpu.VMEM),
        scratch_shapes=[
            held,
            held,
            came,
            pltpu.SemaphoreType.DMA((len(parts),)),
            pltpu.SemaphoreType.DMA((len(parts), count)),
            pltpu.SemaphoreType.DMA((len(parts), count)),
        ],
        compiler_params=pltpu.CompilerParams(
            collective_id=3, has_side_effects=True, vmem_limit_bytes=56 << 20
        ),
    )(shares.reshape((2,) * count + (TGT_LEN, D)))


def merge_kernel(bits, stats, out, came, sent, send_sem, recv_sem):
    partners = [partner_of(bit) for bit in bits]
    meet(partners)
    count = len(bits)
    size = 1 << count
    out[...] = stats[...]
    position = lax.broadcasted_iota(jnp.int32, (size, TGT_LEN), 0)
    for step in range(count):
        mask = 1 << (count - 1 - step)
        sent[step] = out[...]
        copy = pltpu.make_async_remote_copy(
            src_ref=sent.at[step],
            dst_ref=came.at[step],
            send_sem=send_sem.at[step],
            recv_sem=recv_sem.at[step],
            device_id=partners[step],
            device_id_type=MESH,
        )
        copy.start()
        copy.wait()
        lower = (position // mask) % 2 == 0
        other = [
            jnp.where(
                lower,
                pltpu.roll(came[step, i], size - mask, 0),
                pltpu.roll(came[step, i], mask, 0),
            )
            for i in range(3)
        ]
        top = jnp.maximum(out[0], other[0])
        out[1] = out[1] * jnp.exp(out[0] - top) + other[1] * jnp.exp(other[0] - top)
        out[0] = top
        out[2] = out[2] + other[2]


def merge_stats(stats):
    bits = code_bits()
    shape = stats.shape
    return pl.pallas_call(
        functools.partial(merge_kernel, bits),
        out_shape=jax.ShapeDtypeStruct(shape, jnp.float32),
        in_specs=[pl.BlockSpec(memory_space=pltpu.VMEM)],
        out_specs=pl.BlockSpec(memory_space=pltpu.VMEM),
        scratch_shapes=[
            pltpu.VMEM((len(bits),) + shape, jnp.float32),
            pltpu.VMEM((len(bits),) + shape, jnp.float32),
            pltpu.SemaphoreType.DMA((len(bits),)),
            pltpu.SemaphoreType.DMA((len(bits),)),
        ],
        compiler_params=pltpu.CompilerParams(collective_id=4, has_side_effects=True),
    )(stats)


def weights_kernel(slots, groups, shards, vector, fact, fulls, vectors, facts, sems):
    holds, local_sem, send_sem, recv_sem, small_local, small_send, small_recv = sems
    slot, pb = lax.axis_index("slot"), lax.axis_index("pb")
    core, far = xor(pb, 1), xor(pb, 2)
    to_core, to_far = (slot, core), (slot, far)
    across = [(xor(slot, mask), pb) for mask in masks_below(slots)]
    meet([to_core, to_far] + across)

    jobs = []
    for shard, full in zip(shards, fulls):
        if len(shard.shape) == 3:
            for half in range(2):
                lead = pl.ds(half * (shard.shape[0] // 2), shard.shape[0] // 2)
                view = lambda ref, at, size, lead=lead: ref.at[lead, pl.ds(at, size)]
                jobs.append((shard, full, shard.shape[1], shard.shape[1], 0, view))
        elif shard.shape[1] > D:
            for half in range(2):
                lanes = pl.ds(half * (shard.shape[1] // 2), shard.shape[1] // 2)
                view = lambda ref, at, size, lanes=lanes: ref.at[pl.ds(at, size), lanes]
                jobs.append((shard, full, shard.shape[0], shard.shape[0], 0, view))
        else:
            for half in range(2):
                rows = shard.shape[0] // 2
                view = lambda ref, at, size: ref.at[pl.ds(at, size)]
                jobs.append((shard, full, shard.shape[0], rows, half * rows, view))

    def remote(source, target, job, kind, partner):
        return pltpu.make_async_remote_copy(
            src_ref=source,
            dst_ref=target,
            send_sem=send_sem.at[job, kind],
            recv_sem=recv_sem.at[job, kind],
            device_id=partner,
            device_id_type=MESH,
        )

    def describe(job):
        shard, full, block, rows, base, view = jobs[job]
        turn = job % 2
        first, second = (slot // (1 << turn)) % 2, (slot // (2 >> turn)) % 2
        to_first, to_second = across[turn], across[1 - turn]
        quarter, half = 3 * rows // 16, rows // 8
        split = base + 3 * rows // 4
        mine = pl.multiple_of(base + (second * 2 + first) * quarter, 16)
        pair = pl.multiple_of(base + second * 2 * quarter, 16)
        side = pl.multiple_of(split + second * half, 16)

        def there(owner, at):
            return pl.multiple_of(owner * block + at, 16)

        def send(kind, partner, owner, at, size, source=None):
            target = view(full, there(owner, at), size)
            return remote(target if source is None else source, target, job, kind, partner)

        own = view(shard, base, rows)
        stages = [
            [
                send(0, to_far, pb, mine, quarter, view(shard, mine, quarter)),
                send(1, to_far, pb, side, half, view(shard, side, half)),
                send(2, to_core, pb, base, rows, own),
            ],
            [
                send(3, to_first, far, mine, quarter),
                send(4, to_second, far, side, half),
            ],
            [send(5, to_second, far, pair, 2 * quarter)],
            [send(6, to_core, far, base, rows)],
        ]
        held = holds[job]
        into = pltpu.make_async_copy(own, held, local_sem.at[job, 0])
        onto = pltpu.make_async_copy(held, view(full, there(pb, base), rows), local_sem.at[job, 1])
        return stages, (into, onto)

    bits = [("pb", mask) for mask in masks_below(groups)] + [
        ("slot", mask) for mask in masks_below(slots)
    ]

    def small_copy(kind, source, target, partner):
        return pltpu.make_async_remote_copy(
            src_ref=source,
            dst_ref=target,
            send_sem=small_send.at[kind],
            recv_sem=small_recv.at[kind],
            device_id=partner,
            device_id_type=MESH,
        )

    def fact_copy(step):
        name, mask = bits[step]
        partner = (slot, xor(pb, mask)) if name == "pb" else (xor(slot, mask), pb)
        count = 1 << step
        source = fact if step == 0 else facts.at[pl.ds(0, count)]
        return small_copy(step, source, facts.at[pl.ds(count, count)], partner)

    near = len(bits)
    vector_copies = [
        small_copy(near, vector, vectors.at[pb], to_core),
        small_copy(near + 1, vector, vectors.at[pb], to_far),
    ]
    vector_last = small_copy(near + 2, vectors.at[far], vectors.at[far], to_core)
    small_own = [
        pltpu.make_async_copy(fact.at[0], facts.at[0], small_local.at[0]),
        pltpu.make_async_copy(vector, vectors.at[pb], small_local.at[1]),
    ]
    for copy in small_own + vector_copies:
        copy.start()
    plans = [describe(job) for job in range(len(jobs))]
    for step in range(max(len(jobs) + 4, len(bits) + 1)):
        for stage in range(5):
            job = step - stage
            if not 0 <= job < len(jobs):
                continue
            stages, (into, onto) = plans[job]
            if stage == 0:
                into.start()
            else:
                for copy in stages[stage - 1]:
                    copy.wait()
            if stage < 4:
                for copy in stages[stage]:
                    copy.start()
                if stage == 1:
                    into.wait()
                    onto.start()
            else:
                onto.wait()
        if step == 0:
            for copy in small_own:
                copy.wait()
        if step == 1:
            for copy in vector_copies:
                copy.wait()
            vector_last.start()
        if step == 2:
            vector_last.wait()
        if 0 < step <= len(bits):
            fact_copy(step - 1).wait()
        if step < len(bits):
            fact_copy(step).start()


def gather_weights(shards, vector, fact):
    slots, groups = lax.axis_size("slot"), lax.axis_size("pb")
    bits = (slots * groups).bit_length() - 1

    def widened(shard):
        axis = 1 if shard.ndim == 3 else 0
        shape = list(shard.shape)
        shape[axis] *= groups
        return jax.ShapeDtypeStruct(tuple(shape), shard.dtype)

    used = len(shards)

    def kernel(*refs):
        ins, outs, sems = refs[: used + 2], refs[used + 2 : 2 * used + 4], refs[2 * used + 4 :]
        weights_kernel(
            slots, groups, ins[:used], ins[used], ins[used + 1], outs[:used], outs[used],
            outs[used + 1], sems,
        )

    jobs = 2 * used
    holds = []
    for shard in shards:
        axis = 1 if shard.ndim == 2 and shard.shape[1] > D else 0
        shape = list(shard.shape)
        shape[axis] //= 2
        holds += [pltpu.VMEM(tuple(shape), shard.dtype)] * 2
    return pl.pallas_call(
        kernel,
        out_shape=[widened(shard) for shard in shards]
        + [
            jax.ShapeDtypeStruct((groups,) + vector.shape, vector.dtype),
            jax.ShapeDtypeStruct((slots * groups,) + fact.shape[1:], fact.dtype),
        ],
        in_specs=[pl.BlockSpec(memory_space=pl.ANY)] * (used + 2),
        out_specs=[pl.BlockSpec(memory_space=pl.ANY)] * (used + 2),
        scratch_shapes=[
            holds,
            pltpu.SemaphoreType.DMA((jobs, 2)),
            pltpu.SemaphoreType.DMA((jobs, 7)),
            pltpu.SemaphoreType.DMA((jobs, 7)),
            pltpu.SemaphoreType.DMA((2,)),
            pltpu.SemaphoreType.DMA((bits + 3,)),
            pltpu.SemaphoreType.DMA((bits + 3,)),
        ],
        compiler_params=pltpu.CompilerParams(
            collective_id=5, has_side_effects=True, vmem_limit_bytes=32 << 20
        ),
    )(*shards, vector, fact)


def own_facts(targets, owner, doc_scores):
    serving = jnp.arange(targets.shape[1]) == owner[0, 0]
    own = jnp.sum(jnp.where(serving[:, None], targets[0], 0), axis=0)
    half = (TGT_LEN // 2,)
    facts = [
        own.astype(jnp.float32),
        jnp.broadcast_to(owner[0, 0].astype(jnp.float32), half),
        jnp.broadcast_to(doc_scores[0, 0], half),
    ]
    return jnp.pad(jnp.concatenate(facts).reshape(1, 2, TGT_LEN), ((0, 0), (0, 6), (0, 0)))


def vocabulary_head(state_low, facts, questions, embed):
    slots, groups = lax.axis_size("slot"), lax.axis_size("pb")
    me = lax.axis_index("slot") * groups + lax.axis_index("pb")
    entries = embed.shape[0]
    tokens = slots * groups * TGT_LEN
    target_ids = facts[:, 0].astype(jnp.int32).reshape(tokens, 1)
    owners = facts[:, 1, 0].astype(jnp.int32).reshape(slots, groups)
    scores = facts[:, 1, TGT_LEN // 2].reshape(slots, groups)
    states = gather_states(state_low)
    logits = matmul_nt(states, embed)
    hit = target_ids - me * entries == lax.broadcasted_iota(jnp.int32, (tokens, entries), 1)
    top = jnp.max(logits, axis=1)
    total = jnp.sum(jnp.exp(logits - top[:, None]), axis=1)
    pick = jnp.sum(jnp.where(hit, logits, 0.0), axis=1)
    merged = merge_stats(jnp.stack([top, total, pick]).reshape(3, -1, TGT_LEN))
    log_total = (merged[0] + jnp.log(merged[1])).reshape(tokens)
    picked = merged[2].reshape(slots, groups, TGT_LEN) - log_total.reshape(slots, groups, TGT_LEN)
    serving = owners[:, :, None] == jnp.arange(questions)
    score_terms = jnp.where(serving, scores[:, :, None], BIG_NEGATIVE)
    token_terms = jnp.where(
        serving[..., None], (scores[:, :, None] + picked)[:, :, None, :], BIG_NEGATIVE
    )
    score_top, token_top = jnp.max(score_terms, axis=0), jnp.max(token_terms, axis=0)
    score_norm = score_top + jnp.log(jnp.sum(jnp.exp(score_terms - score_top), axis=0))
    token_mix = token_top + jnp.log(jnp.sum(jnp.exp(token_terms - token_top), axis=0))
    group_tokens = questions * TGT_LEN
    count = groups * group_tokens
    losses = -jnp.sum(token_mix - score_norm[:, :, None], axis=(1, 2)) / group_tokens
    own_mix = jnp.sum(jnp.where(serving[..., None], token_mix[None], 0.0), axis=2)
    own_norm = jnp.sum(jnp.where(serving, score_norm[None], 0.0), axis=2)
    posterior = jnp.exp(scores[:, :, None] + picked - own_mix)
    prior = jnp.exp(scores - own_norm)
    token_grad = (-posterior / count).reshape(tokens, 1)
    score_grads = -jnp.sum(posterior - prior[:, :, None], axis=2) / count
    delta = to_low(
        token_grad * (jnp.where(hit, 1.0, 0.0) - jnp.exp(logits - log_total[:, None]))
    )
    grad_state = scatter_states(to_low(matmul(delta, embed)))
    return (losses[:1], score_grads[:1, :1], grad_state, delta, states)


def local(
    enc_input,
    dec_input,
    doc_scores,
    owner,
    targets,
    enc_attn,
    enc_up,
    enc_down,
    enc_up_bias,
    enc_bias,
    enc_gain,
    dec_self,
    dec_cross,
    dec_up,
    dec_down,
    dec_up_bias,
    dec_bias,
    dec_gain,
    embed,
):
    pb_size = lax.axis_size("pb")
    width = D // pb_size
    vectors = (enc_up_bias, enc_bias, enc_gain, dec_up_bias, dec_bias, dec_gain)
    rows = [v.size // width for v in vectors]
    starts = [sum(rows[:i]) for i in range(len(rows) + 1)]
    passage_low = enc_input[0, 0]
    passage = passage_low.astype(jnp.float32)
    question_low = dec_input[0, 0]
    question = question_low.astype(jnp.float32)

    own_vectors = jnp.concatenate([v.reshape(-1, width) for v in vectors])
    (
        encoder_attn,
        encoder_up,
        encoder_down,
        decoder_self,
        decoder_cross,
        decoder_down,
        packed,
        facts,
    ) = gather_weights(
        (enc_attn, enc_up, enc_down, dec_self, dec_cross, dec_down),
        jnp.pad(own_vectors, ((0, -starts[-1] % 32), (0, 0))),
        own_facts(targets, owner, doc_scores),
    )
    packed, dec_up = lax.optimization_barrier((packed, dec_up))
    decoder_up = lax.all_gather(dec_up, "pb", axis=0, tiled=True)
    packed = packed.astype(jnp.float32)
    unpacked = [packed[:, starts[i] : starts[i + 1], :] for i in range(len(rows))]
    encoder_upbias = unpacked[0].reshape(-1)
    encoder_bias = unpacked[1].transpose(1, 0, 2).reshape(-1, D)
    encoder_gain = unpacked[2].transpose(1, 0, 2).reshape(-1, D)
    decoder_upbias = unpacked[3].reshape(-1)
    decoder_bias = unpacked[4].transpose(1, 0, 2).reshape(-1, D)
    decoder_gain = unpacked[5].transpose(1, 0, 2).reshape(-1, D)
    attn_out, enc_saved = attend_forward(
        passage_low,
        passage_low,
        encoder_attn,
        encoder_bias[0],
        encoder_bias[1],
        encoder_bias[2],
        False,
    )
    enc_first, enc_norm_one = norm_forward(passage + attn_out, encoder_gain[0], encoder_bias[3])
    enc_first_low = to_low(enc_first)
    enc_hidden, enc_slope = gelu_with_slope(matmul(enc_first_low, encoder_up) + encoder_upbias)
    enc_hidden_low = to_low(enc_hidden)
    ffn_out = matmul(enc_hidden_low, encoder_down) + encoder_bias[4]
    encoded, enc_norm_two = norm_forward(enc_first + ffn_out, encoder_gain[1], encoder_bias[5])
    memory_low = to_low(encoded)
    self_out, self_saved = attend_forward(
        question_low,
        question_low,
        decoder_self,
        decoder_bias[0],
        decoder_bias[1],
        decoder_bias[2],
        True,
    )
    dec_first, dec_norm_one = norm_forward(question + self_out, decoder_gain[0], decoder_bias[3])
    dec_first_low = to_low(dec_first)
    cross_out, cross_saved = attend_forward(
        dec_first_low,
        memory_low,
        decoder_cross,
        decoder_bias[4],
        decoder_bias[5],
        decoder_bias[6],
        False,
    )
    dec_second, dec_norm_two = norm_forward(dec_first + cross_out, decoder_gain[1], decoder_bias[7])
    dec_second_low = to_low(dec_second)
    dec_hidden, dec_slope = gelu_with_slope(matmul(dec_second_low, decoder_up) + decoder_upbias)
    dec_hidden_low = to_low(dec_hidden)
    dec_ffn_out = matmul(dec_hidden_low, decoder_down) + decoder_bias[8]
    state, dec_norm_three = norm_forward(dec_second + dec_ffn_out, decoder_gain[2], decoder_bias[9])
    state_low = to_low(state)

    loss, score_grad, grad_state_sum, delta, states = vocabulary_head(
        state_low, facts, targets.shape[1], embed
    )

    embed_grad = matmul_tn(delta, states)
    grad_third, gain_third, shift_third = norm_backward(
        grad_state_sum, dec_norm_three, decoder_gain[2]
    )
    dec_downbias_grad = jnp.sum(grad_third, axis=0)
    third_low = to_low(grad_third)
    grad_before = matmul_nt(third_low, decoder_down) * dec_slope
    dec_upbias_grad = jnp.sum(grad_before, axis=0)
    before_low = to_low(grad_before)
    grad_second, gain_second, shift_second = norm_backward(
        grad_third + matmul_nt(before_low, decoder_up), dec_norm_two, decoder_gain[1]
    )
    cross_query, grad_memory, dec_cross_pairs, cross_biases = attend_backward(
        grad_second, dec_first_low, memory_low, decoder_cross, cross_saved, False
    )
    grad_first, gain_first, shift_first = norm_backward(
        grad_second + cross_query, dec_norm_one, decoder_gain[0]
    )
    self_query, self_memory, dec_self_pairs, self_biases = attend_backward(
        grad_first, question_low, question_low, decoder_self, self_saved, True
    )
    question_grad = grad_first + self_query + self_memory
    enc_grad_two, enc_gain_two, enc_shift_two = norm_backward(
        grad_memory, enc_norm_two, encoder_gain[1]
    )
    enc_downbias_grad = jnp.sum(enc_grad_two, axis=0)
    enc_two_low = to_low(enc_grad_two)
    enc_grad_before = matmul_nt(enc_two_low, encoder_down) * enc_slope
    enc_upbias_grad = jnp.sum(enc_grad_before, axis=0)
    enc_before_low = to_low(enc_grad_before)
    enc_grad_one, enc_gain_one, enc_shift_one = norm_backward(
        enc_grad_two + matmul_nt(enc_before_low, encoder_up), enc_norm_one, encoder_gain[0]
    )
    enc_query, enc_memory, enc_attn_pairs, enc_biases = attend_backward(
        enc_grad_one, passage_low, passage_low, encoder_attn, enc_saved, False
    )
    passage_grad = enc_grad_one + enc_query + enc_memory
    operands, plan = [], []

    def share(left, right, tall=False):
        where = []
        for operand in (left, right):
            known = [i for i, other in enumerate(operands) if other is operand]
            where.append(known[0] if known else len(operands))
            if not known:
                operands.append(operand)
        for i in range(left.shape[1] * right.shape[1] // (D * D)):
            plan.append((where[0], where[1], i, tall))

    for left, right in enc_attn_pairs:
        share(left, right)
    share(enc_first_low, enc_before_low)
    share(enc_hidden_low, enc_two_low, tall=True)
    for left, right in dec_self_pairs + dec_cross_pairs:
        share(left, right)
    share(dec_second_low, before_low)
    share(dec_hidden_low, third_low, tall=True)
    enc_bias_grad = jnp.stack(
        [
            enc_biases[0],
            enc_biases[1],
            enc_biases[2],
            enc_shift_one,
            enc_downbias_grad,
            enc_shift_two,
        ]
    )
    enc_gain_grad = jnp.stack([enc_gain_one, enc_gain_two])
    dec_bias_grad = jnp.stack(
        [
            self_biases[0],
            self_biases[1],
            self_biases[2],
            shift_first,
            cross_biases[0],
            cross_biases[1],
            cross_biases[2],
            shift_second,
            dec_downbias_grad,
            shift_third,
        ]
    )
    dec_gain_grad = jnp.stack([gain_first, gain_second, gain_third])
    vector_grads = jnp.concatenate(
        [
            enc_upbias_grad.reshape(pb_size, -1, width),
            enc_bias_grad.reshape(-1, pb_size, width).transpose(1, 0, 2),
            enc_gain_grad.reshape(-1, pb_size, width).transpose(1, 0, 2),
            dec_upbias_grad.reshape(pb_size, -1, width),
            dec_bias_grad.reshape(-1, pb_size, width).transpose(1, 0, 2),
            dec_gain_grad.reshape(-1, pb_size, width).transpose(1, 0, 2),
        ],
        axis=1,
    )
    spare = -starts[-1] % 32
    small = jnp.pad(vector_grads, ((0, 0), (0, spare), (0, 0))).reshape(pb_size, -1, D)
    summed_parts, small_sum = sync_gradients(plan, operands, small)
    units = summed_parts.reshape(-1, width, D)
    square = lambda at: units[at : at + 4].astype(jnp.float32)
    wide = lambda at: jnp.concatenate([units[at + i].astype(jnp.float32) for i in range(4)], axis=1)
    tall = lambda at: square(at).reshape(-1, D)
    vector_sum = small_sum.reshape(-1, width)
    vector_out = [
        vector_sum[starts[i] : starts[i + 1]].reshape(v.shape) for i, v in enumerate(vectors)
    ]
    summed = (
        (square(0), wide(4), tall(8))
        + tuple(vector_out[:3])
        + (square(12), square(16), wide(20), tall(24))
        + tuple(vector_out[3:])
    )
    return (
        (
            loss,
            passage_grad.reshape(1, 1, SRC_LEN, D),
            question_grad.reshape(1, 1, TGT_LEN, D),
            score_grad,
        )
        + tuple(summed)
        + (embed_grad,)
    )


def solution(mesh):
    placed = (
        P("pb", "slot", None, None),
        P("pb", "slot", None, None),
        P("pb", "slot"),
        P("pb", "slot"),
        P("pb", None, None),
        P(None, "pb", None),
        P("pb", None),
        P("pb", None),
        P("pb"),
        P(None, "pb"),
        P(None, "pb"),
        P(None, "pb", None),
        P(None, "pb", None),
        P("pb", None),
        P("pb", None),
        P("pb"),
        P(None, "pb"),
        P(None, "pb"),
        P(("slot", "pb"), None),
    )
    return jax.shard_map(
        local,
        mesh=mesh,
        in_specs=placed,
        out_specs=(
            P("pb"),
            P("pb", "slot", None, None),
            P("pb", "slot", None, None),
            P("pb", "slot"),
            P(None, "pb", None),
            P("pb", None),
            P("pb", None),
            P("pb"),
            P(None, "pb"),
            P(None, "pb"),
            P(None, "pb", None),
            P(None, "pb", None),
            P("pb", None),
            P("pb", None),
            P("pb"),
            P(None, "pb"),
            P(None, "pb"),
            P(("slot", "pb"), None),
        ),
        check_vma=False,
    )
```

```python
import functools
import math

import jax
import jax.numpy as jnp
from jax import lax
from jax.experimental import pallas as pl
from jax.experimental.pallas import tpu as pltpu
from jax.sharding import PartitionSpec as P

D = 1024
HEADS = 16
HEAD_DIM = 64
SRC_LEN = 384
TGT_LEN = 128
MESH = pl.DeviceIdType.MESH
UNIT = 256
RING = 8
SIDE_STEPS = 16


BIG_NEGATIVE = -1e30
MASK_FILL = -1000000000.0


def matmul(left, right):
    return jnp.dot(left, right, preferred_element_type=jnp.float32)


def matmul_nt(left, right):
    return lax.dot_general(
        left, right, (((1,), (1,)), ((), ())), preferred_element_type=jnp.float32
    )


def matmul_tn(left, right):
    return lax.dot_general(
        left, right, (((0,), (0,)), ((), ())), preferred_element_type=jnp.float32
    )


def to_low(value):
    return value.astype(jnp.bfloat16)


def norm_forward(total, gain, shift):
    centered = total - jnp.mean(total, axis=-1, keepdims=True)
    inverse = lax.rsqrt(jnp.mean(centered * centered, axis=-1, keepdims=True) + 1e-05)
    normed = centered * inverse
    return (normed * gain + shift, (normed, inverse))


def norm_backward(upstream, saved, gain):
    normed, inverse = saved
    scaled = upstream * gain
    inner = (
        scaled
        - jnp.mean(scaled, axis=-1, keepdims=True)
        - normed * jnp.mean(scaled * normed, axis=-1, keepdims=True)
    )
    return (inverse * inner, jnp.sum(upstream * normed, axis=0), jnp.sum(upstream, axis=0))


def head_mask(which):
    return lax.broadcasted_iota(jnp.int32, (1, 2 * HEAD_DIM), 1) // HEAD_DIM == which


def only_head(pair, which):
    return jnp.where(head_mask(which), pair.astype(jnp.float32), 0.0).astype(pair.dtype)


def both_heads(first, second):
    return jnp.where(head_mask(0), first, second)


def attention_weights(queries, keys, causal):
    scores = matmul_nt(queries, keys) * HEAD_DIM ** (-0.5)
    if causal:
        rows = lax.broadcasted_iota(jnp.int32, scores.shape, 0)
        columns = lax.broadcasted_iota(jnp.int32, scores.shape, 1)
        scores = jnp.where(rows >= columns, scores, MASK_FILL)
    shifted = jnp.exp(scores - jnp.max(scores, axis=-1, keepdims=True))
    return shifted / jnp.sum(shifted, axis=-1, keepdims=True)


def attend_kernel(causal, queries, keys, values, out):
    parts = []
    for which in range(2):
        probs = attention_weights(only_head(queries[...], which), keys[...], causal)
        parts.append(matmul(to_low(probs), values[...]))
    out[...] = to_low(both_heads(*parts))


def attend_grad_kernel(
    causal, queries, keys, values, upstream, grad_q, grad_k, grad_v, sum_q, sum_v
):
    parts = []
    for which in range(2):
        probs = attention_weights(only_head(queries[...], which), keys[...], causal)
        grad_probs = matmul_nt(only_head(upstream[...], which), values[...])
        inner = jnp.sum(grad_probs * probs, axis=-1, keepdims=True)
        grad_scores = to_low(probs * (grad_probs - inner))
        parts.append(
            (
                matmul(grad_scores, keys[...]),
                matmul_tn(grad_scores, queries[...]),
                matmul_tn(to_low(probs), upstream[...]),
            )
        )
    scale = HEAD_DIM ** (-0.5)
    query, key, value = [both_heads(*pair) for pair in zip(*parts)]
    query = query * scale
    grad_q[...] = to_low(query)
    grad_k[...] = to_low(key * scale)
    grad_v[...] = to_low(value)
    sum_q[...] = jnp.broadcast_to(jnp.sum(query, axis=0, keepdims=True), sum_q.shape)
    sum_v[...] = jnp.broadcast_to(jnp.sum(value, axis=0, keepdims=True), sum_v.shape)


def head_pairs(rows):
    return pl.BlockSpec((rows, 2 * HEAD_DIM), lambda pair: (0, pair))


def attention_cost(rows, columns, products):
    return pl.CostEstimate(
        flops=2 * products * rows * columns * D,
        bytes_accessed=4 * (rows + columns) * D * products,
        transcendentals=HEADS * rows * columns,
    )


def attend_forward(query_low, memory_low, matrices, bias_query, bias_value, bias_out, causal):
    rows, columns = query_low.shape[0], memory_low.shape[0]
    queries = to_low(matmul(query_low, matrices[0]) + bias_query)
    keys = to_low(matmul(memory_low, matrices[1]))
    values = to_low(matmul(memory_low, matrices[2]) + bias_value)
    context = pl.pallas_call(
        functools.partial(attend_kernel, causal),
        grid=(HEADS // 2,),
        out_shape=jax.ShapeDtypeStruct((rows, D), jnp.bfloat16),
        in_specs=[head_pairs(rows), head_pairs(columns), head_pairs(columns)],
        out_specs=head_pairs(rows),
        cost_estimate=attention_cost(rows, columns, 2),
        compiler_params=pltpu.CompilerParams(vmem_limit_bytes=24 << 20),
    )(queries, keys, values)
    output = matmul(context, matrices[3]) + bias_out
    return (output, (queries, keys, values, context))


def attend_backward(upstream, query_low, memory_low, matrices, saved, causal):
    queries, keys, values, context = saved
    rows, columns = query_low.shape[0], memory_low.shape[0]
    upstream_low = to_low(upstream)
    grad_context = to_low(matmul_nt(upstream_low, matrices[3]))
    low, sums = jnp.bfloat16, jax.ShapeDtypeStruct((8, D), jnp.float32)
    queries_low, keys_low, values_low, query_sum, value_sum = pl.pallas_call(
        functools.partial(attend_grad_kernel, causal),
        grid=(HEADS // 2,),
        out_shape=(
            jax.ShapeDtypeStruct((rows, D), low),
            jax.ShapeDtypeStruct((columns, D), low),
            jax.ShapeDtypeStruct((columns, D), low),
            sums,
            sums,
        ),
        in_specs=[head_pairs(n) for n in (rows, columns, columns, rows)],
        out_specs=tuple(head_pairs(n) for n in (rows, columns, columns, 8, 8)),
        cost_estimate=attention_cost(rows, columns, 5),
        compiler_params=pltpu.CompilerParams(vmem_limit_bytes=24 << 20),
    )(queries, keys, values, grad_context)
    grad_query_input = matmul_nt(queries_low, matrices[0])
    grad_memory_input = matmul_nt(keys_low, matrices[1]) + matmul_nt(values_low, matrices[2])
    grad_pairs = [
        (query_low, queries_low),
        (memory_low, keys_low),
        (memory_low, values_low),
        (context, upstream_low),
    ]
    bias_grads = (query_sum[0], value_sum[0], jnp.sum(upstream, axis=0))
    return (grad_query_input, grad_memory_input, grad_pairs, bias_grads)


def gelu_with_slope(value):
    share = 0.5 * (1.0 + lax.erf(value * 0.5**0.5))
    density = jnp.exp(-0.5 * value * value) * (2.0 * math.pi) ** -0.5
    return value * share, share + value * density


def masks_below(size):
    return [1 << i for i in range(size.bit_length() - 1)]


def xor(value, mask):
    return jnp.where((value // mask) % 2 == 0, value + mask, value - mask)


def sync_kernel(slots, count, plan, operands, small, side, out, small_out, side_out, scratch):
    left_buffer, right_buffer, parts, core_in, far_out, far_keep, far_in = scratch[:7]
    half_out, half_keep, half_in, full = scratch[7:11]
    small_core, small_far, small_in, small_out_far, small_out_slot = scratch[11:16]
    load_sem, store_sem, send_sem, recv_sem, small_send, small_recv = scratch[16:22]
    if side:
        side_left, side_right, side_total, side_sem, side_store = scratch[22:]
    masks = masks_below(slots)
    levels = len(masks)
    rows = full.shape[1]
    slot, pb = lax.axis_index("slot"), lax.axis_index("pb")
    core, far = xor(pb, 1), xor(pb, 2)
    far_core = xor(core, 2)
    partners = [(slot, core), (slot, far)] + [(xor(slot, mask), pb) for mask in masks]
    bits = [(slot // mask) % 2 for mask in masks]

    barrier = pltpu.get_barrier_semaphore()
    for partner in partners:
        pl.semaphore_signal(barrier, inc=1, device_id=partner, device_id_type=MESH)
    pl.semaphore_wait(barrier, len(partners))

    def remote(source, target, stage, at, partner):
        return pltpu.make_async_remote_copy(
            src_ref=source,
            dst_ref=target,
            send_sem=send_sem.at[stage, at],
            recv_sem=recv_sem.at[stage, at],
            device_id=partner,
            device_id_type=MESH,
        )

    def core_copies(c):
        at = lax.rem(c, RING)
        ring = lax.rem(c, 4)
        pair = lax.rem(c, 2)
        return (
            remote(parts.at[pair, core], core_in.at[ring, 0], 0, at, partners[0]),
            remote(parts.at[pair, far_core], core_in.at[ring, 1], 1, at, partners[0]),
        )

    def load(unit):
        pair = lax.rem(unit, 2)
        for at, (left, right, k, tall) in enumerate(plan):

            @pl.when(unit == at)
            def _():
                tokens = operands[left].shape[0]
                rows_at = pl.ds(0, tokens)
                if tall:
                    for p in range(4):
                        pltpu.make_async_copy(
                            operands[left].at[:, pl.ds((4 * p + k) * UNIT, UNIT)],
                            left_buffer.at[pair, rows_at, pl.ds(p * UNIT, UNIT)],
                            load_sem.at[0, pair],
                        ).start()
                else:
                    pltpu.make_async_copy(
                        operands[left], left_buffer.at[pair, rows_at], load_sem.at[0, pair]
                    ).start()
                column = 0 if tall else k * D
                pltpu.make_async_copy(
                    operands[right].at[:, pl.ds(column, D)],
                    right_buffer.at[pair, rows_at],
                    load_sem.at[1, pair],
                ).start()

    def product(unit, chunk, offset):
        pair = lax.rem(unit, 2)
        lengths = [operands[left].shape[0] for left, _, _, _ in plan]
        for tokens in sorted(set(lengths)):
            among = functools.reduce(
                jnp.logical_or, [unit == at for at, n in enumerate(lengths) if n == tokens]
            )

            @pl.when(among)
            def _():
                rows_at = pl.ds(0, tokens)
                for i, buffer in enumerate((left_buffer, right_buffer)):
                    whole = buffer.at[pair, rows_at]
                    pltpu.make_async_copy(whole, whole, load_sem.at[i, pair]).wait()

                @pl.loop(0, 4)
                def _(p):
                    columns = pl.ds(pl.multiple_of(p * UNIT, UNIT), UNIT)
                    total = lax.dot_general(
                        left_buffer[pair, rows_at, columns],
                        right_buffer[pair, rows_at, :],
                        (((0,), (0,)), ((), ())),
                        preferred_element_type=jnp.float32,
                    )
                    parts[lax.rem(chunk, 2), p, pl.ds(offset, UNIT), :] = total.astype(
                        parts.dtype
                    )

    def far_copy(c):
        ring = lax.rem(c, 4)
        return remote(far_out.at[ring], far_in.at[ring], 2, lax.rem(c, RING), partners[1])

    def halve_copy(level, c):
        ring = lax.rem(c, 4)
        return remote(
            half_out[level].at[ring],
            half_in[level].at[ring],
            3 + level,
            lax.rem(c, RING),
            partners[2 + level],
        )

    def join_copy(level, c):
        at = lax.rem(c, RING)
        size = rows >> (level + 1)
        offset = sum(bits[i] * (rows >> (i + 1)) for i in range(level + 1))
        where = pl.ds(pl.multiple_of(offset, size), size)
        return remote(
            full.at[at, where], full.at[at, where], 3 + levels + level, at, partners[2 + level]
        )

    def store(c):
        at = lax.rem(c, RING)
        return pltpu.make_async_copy(full.at[at], out.at[c], store_sem.at[at])

    def add(target, left, right, size):
        tile = min(size, 32)

        @pl.loop(0, size // tile)
        def _(i):
            at = pl.ds(pl.multiple_of(i * tile, tile), tile)
            total = left[at, :].astype(jnp.float32) + right[at, :].astype(jnp.float32)
            target[at, :] = total.astype(target.dtype)

    def small_core_copies():
        return [
            pltpu.make_async_remote_copy(
                src_ref=small.at[source],
                dst_ref=small_core.at[i],
                send_sem=small_send.at[i],
                recv_sem=small_recv.at[i],
                device_id=partners[0],
                device_id_type=MESH,
            )
            for i, source in ((0, core), (1, far_core))
        ]

    def small_far_copy():
        return pltpu.make_async_remote_copy(
            src_ref=small_out_far,
            dst_ref=small_far,
            send_sem=small_send.at[2],
            recv_sem=small_recv.at[2],
            device_id=partners[1],
            device_id_type=MESH,
        )

    def small_slot_copy(level):
        return pltpu.make_async_remote_copy(
            src_ref=small_out_slot.at[level],
            dst_ref=small_in.at[level],
            send_sem=small_send.at[3 + level],
            recv_sem=small_recv.at[3 + level],
            device_id=partners[2 + level],
            device_id_type=MESH,
        )

    def small_stage(step):
        if step == 0:
            for copy in small_core_copies():
                copy.start()
        elif step == 1:
            for copy in small_core_copies():
                copy.wait()
            small_out_far[...] = small[far] + small_core[1]
            small_out[...] = small[pb] + small_core[0]
            small_far_copy().start()
        elif step == 2:
            small_far_copy().wait()
            small_out[...] = small_out[...] + small_far[...]
            small_out_slot[0] = small_out[...]
            small_slot_copy(0).start()
        else:
            level = step - 3
            small_slot_copy(level).wait()
            small_out[...] = small_out[...] + small_in[level]
            if level + 1 < levels:
                small_out_slot[level + 1] = small_out[...]
                small_slot_copy(level + 1).start()

    def stage(step, c):
        ring = lax.rem(c, 4)
        pair = lax.rem(c, 2)
        at = lax.rem(c, RING)
        if step == 0:
            for copy in core_copies(c):
                copy.start()
        elif step == 1:
            for copy in core_copies(c):
                copy.wait()
            add(far_out.at[ring], parts.at[pair, far], core_in.at[ring, 1], rows)
            far_copy(c).start()
            add(far_keep.at[ring], parts.at[pair, pb], core_in.at[ring, 0], rows)
        elif step < 2 + levels:
            level = step - 2
            size = rows >> (level + 1)
            if level == 0:
                far_copy(c).wait()
                left, right = far_keep.at[ring], far_in.at[ring]
            else:
                halve_copy(level - 1, c).wait()
                left, right = half_keep[level - 1].at[ring], half_in[level - 1].at[ring]
            mine = pl.ds(pl.multiple_of(bits[level] * size, size), size)
            other = pl.ds(pl.multiple_of((1 - bits[level]) * size, size), size)
            add(half_out[level].at[ring], left.at[other], right.at[other], size)
            halve_copy(level, c).start()
            add(half_keep[level].at[ring], left.at[mine], right.at[mine], size)
        elif step == 2 + levels:
            level = levels - 1
            size = rows >> levels
            halve_copy(level, c).wait()
            offset = sum(bits[i] * (rows >> (i + 1)) for i in range(levels))
            where = pl.ds(pl.multiple_of(offset, size), size)
            add(full.at[at, where], half_keep[level].at[ring], half_in[level].at[ring], size)
            join_copy(level, c).start()
        elif step < 2 + 2 * levels:
            level = levels - 1 - (step - 3 - levels)
            join_copy(level, c).wait()
            join_copy(level - 1, c).start()
        elif step == 2 + 2 * levels:
            join_copy(0, c).wait()
            store(c).start()
        else:
            store(c).wait()

    stages = 4 + 2 * levels

    def side_loads(step):
        pair = lax.rem(step, 2)
        tokens = side_right.shape[1]
        at = pl.ds(pl.multiple_of(step * tokens, tokens), tokens)
        return (
            pltpu.make_async_copy(side[0].at[:, at], side_left.at[pair], side_sem.at[0, pair]),
            pltpu.make_async_copy(side[1].at[at], side_right.at[pair], side_sem.at[1, pair]),
        )

    def side_product(step):
        pair = lax.rem(step, 2)
        for copy in side_loads(step):
            copy.wait()

        @pl.loop(0, side_total.shape[0] // UNIT)
        def _(i):
            at = pl.ds(pl.multiple_of(i * UNIT, UNIT), UNIT)
            side_total[at, :] += matmul(side_left[pair, at, :], side_right[pair])

    per = rows // UNIT
    load(jnp.int32(0))
    if side:
        side_total[...] = jnp.zeros_like(side_total)
        side_copy = pltpu.make_async_copy(side_total, side_out, side_store)
        for copy in side_loads(jnp.int32(0)):
            copy.start()

    @pl.loop(0, count + stages)
    def _(it):
        for step in range(3 + levels):

            @pl.when(it == step)
            def _():
                small_stage(step)

        for step in range(stages):
            c = it - 1 - step

            @pl.when(jnp.logical_and(c >= 0, c < count))
            def _():
                stage(step, c)

        for i in range(per):

            @pl.when(it < count)
            def _():
                unit = it * per + i
                load(unit + 1)
                product(unit, it, i * UNIT)

        if side:

            @pl.when(it < SIDE_STEPS - 1)
            def _():
                for copy in side_loads(it + 1):
                    copy.start()

            @pl.when(it < SIDE_STEPS)
            def _():
                side_product(it)

            @pl.when(it == SIDE_STEPS)
            def _():
                side_copy.start()

    if side:
        side_copy.wait()


def sync_gradients(plan, operands, small, side=()):
    slots = lax.axis_size("slot")
    rows, columns = max(UNIT, 16 * slots), D
    count = len(plan) * UNIT // rows
    levels = slots.bit_length() - 1
    small_rows = small.shape[1:]
    low = jnp.bfloat16
    longest = max(operand.shape[0] for operand in operands)
    block = lambda *lead: pltpu.VMEM(lead + (columns,), low)
    halves = [block(4, rows >> (i + 1)) for i in range(levels)]
    used, more = len(operands), len(side)
    outs = 3 if side else 2
    shapes = [
        jax.ShapeDtypeStruct((count, rows, columns), low),
        jax.ShapeDtypeStruct(small_rows, jnp.float32),
    ]
    places = [pl.BlockSpec(memory_space=pl.ANY), pl.BlockSpec(memory_space=pltpu.VMEM)]
    side_scratch = []
    if side:
        entries, tokens = side[0].shape
        shapes.append(jax.ShapeDtypeStruct((entries, columns), jnp.float32))
        places.append(pl.BlockSpec(memory_space=pl.ANY))
        side_scratch = [
            pltpu.VMEM((2, entries, tokens // SIDE_STEPS), low),
            pltpu.VMEM((2, tokens // SIDE_STEPS, columns), low),
            pltpu.VMEM((entries, columns), jnp.float32),
            pltpu.SemaphoreType.DMA((2, 2)),
            pltpu.SemaphoreType.DMA,
        ]

    def kernel(*refs):
        ins, results = refs[: used + 1 + more], refs[used + 1 + more :]
        sync_kernel(
            slots,
            count,
            plan,
            ins[:used],
            ins[used],
            ins[used + 1 :],
            results[0],
            results[1],
            results[2] if side else None,
            results[outs:],
        )

    return pl.pallas_call(
        kernel,
        out_shape=shapes,
        in_specs=[pl.BlockSpec(memory_space=pl.ANY)] * used
        + [pl.BlockSpec(memory_space=pltpu.VMEM)]
        + [pl.BlockSpec(memory_space=pl.ANY)] * more,
        out_specs=places,
        scratch_shapes=[
            block(2, longest),
            block(2, longest),
            block(2, 4, rows),
            block(4, 2, rows),
            block(4, rows),
            block(4, rows),
            block(4, rows),
            halves,
            halves,
            halves,
            block(RING, rows),
            pltpu.VMEM((2,) + small_rows, jnp.float32),
            pltpu.VMEM(small_rows, jnp.float32),
            pltpu.VMEM((levels,) + small_rows, jnp.float32),
            pltpu.VMEM(small_rows, jnp.float32),
            pltpu.VMEM((levels,) + small_rows, jnp.float32),
            pltpu.SemaphoreType.DMA((2, 2)),
            pltpu.SemaphoreType.DMA((RING,)),
            pltpu.SemaphoreType.DMA((3 + 2 * levels, RING)),
            pltpu.SemaphoreType.DMA((3 + 2 * levels, RING)),
            pltpu.SemaphoreType.DMA((3 + levels,)),
            pltpu.SemaphoreType.DMA((3 + levels,)),
        ]
        + side_scratch,
        compiler_params=pltpu.CompilerParams(
            collective_id=1, has_side_effects=True, vmem_limit_bytes=56 << 20
        ),
    )(*operands, small, *side)


def code_bits():
    return [("slot", mask) for mask in masks_below(lax.axis_size("slot"))[::-1]] + [
        ("pb", mask) for mask in masks_below(lax.axis_size("pb"))[::-1]
    ]


def exchange_parts(bits):
    slot_bits = [i for i, (name, mask) in enumerate(bits) if name == "slot"]
    pb_bits = [i for i, (name, mask) in enumerate(bits) if name == "pb"]
    high, low, far, near = slot_bits[:-1], slot_bits[-1:], pb_bits[:-1], pb_bits[-1:]
    first, second = high + low + far + near, far + high + low + near
    return [
        (0, 256, first),
        (256, 256, second),
        (512, 256, first),
        (768, 128, second),
        (896, 128, low + far + high + near),
    ]


def partner_of(bit):
    name, mask = bit
    slot, pb = lax.axis_index("slot"), lax.axis_index("pb")
    return (xor(slot, mask), pb) if name == "slot" else (slot, xor(pb, mask))


def meet(partners):
    barrier = pltpu.get_barrier_semaphore()
    for partner in partners:
        pl.semaphore_signal(barrier, inc=1, device_id=partner, device_id_type=MESH)
    pl.semaphore_wait(barrier, len(partners))


def within(held, count, fixed, value, columns):
    lead = [pl.ds(0, 2) if i in held else 0 for i in range(count)]
    if fixed is not None:
        lead[fixed] = value
    return tuple(lead) + (slice(None), columns)


def gather_kernel(bits, parts, own, out, local_sem, send_sem, recv_sem):
    count = len(bits)
    partners = [partner_of(bit) for bit in bits]
    meet(partners)
    local = pltpu.make_async_copy(
        own, out.at[within([], count, None, 0, slice(None))], local_sem
    )
    local.start()
    pending = [None] * len(parts)
    for step in range(count):
        for p, (start, width, order) in enumerate(parts):
            columns = pl.ds(start, width)
            if step > 0:
                pending[p].wait()
            if step == 1 and p == 0:
                local.wait()
            bit = order[step]
            held = order[:step]
            source = (
                own.at[:, columns] if step == 0 else out.at[within(held, count, None, 0, columns)]
            )
            pending[p] = pltpu.make_async_remote_copy(
                src_ref=source,
                dst_ref=out.at[within(held, count, bit, 1, columns)],
                send_sem=send_sem.at[p, step],
                recv_sem=recv_sem.at[p, step],
                device_id=partners[bit],
                device_id_type=MESH,
            )
            pending[p].start()
    for copy in pending:
        copy.wait()


def gather_states(own):
    bits = code_bits()
    parts = exchange_parts(bits)
    out = pl.pallas_call(
        functools.partial(gather_kernel, bits, parts),
        out_shape=jax.ShapeDtypeStruct((2,) * len(bits) + own.shape, own.dtype),
        in_specs=[pl.BlockSpec(memory_space=pl.ANY)],
        out_specs=pl.BlockSpec(memory_space=pl.ANY),
        scratch_shapes=[
            pltpu.SemaphoreType.DMA,
            pltpu.SemaphoreType.DMA((len(parts), len(bits))),
            pltpu.SemaphoreType.DMA((len(parts), len(bits))),
        ],
        compiler_params=pltpu.CompilerParams(collective_id=2, has_side_effects=True),
    )(own)
    return out.reshape(-1, own.shape[-1])


def scatter_kernel(bits, parts, shares, out, held, near_in, came, load_sem, send_sem, recv_sem):
    count = len(bits)
    partners = [partner_of(bit) for bit in bits]
    near = count - 1
    meet(partners)

    def codes(free):
        out = [()]
        for i in range(near):
            out = [code + (bit,) for code in out for bit in ((0, 1) if i in free else (0,))]
        return out

    def add(target, left, right):
        rows = target.shape[0]

        @pl.loop(0, rows // 32)
        def _(i):
            at = pl.ds(pl.multiple_of(i * 32, 32), 32)
            total = left[at, :].astype(jnp.float32) + right[at, :].astype(jnp.float32)
            target[at, :] = total.astype(target.dtype)

    pending = [None] * len(parts)
    loads = [None] * len(parts)
    for p, (start, width, order) in enumerate(parts):
        columns = pl.ds(start, width)
        every = list(range(near))
        pending[p] = pltpu.make_async_remote_copy(
            src_ref=shares.at[within(every, count, near, 1, columns)],
            dst_ref=near_in[p],
            send_sem=send_sem.at[p, 0],
            recv_sem=recv_sem.at[p, 0],
            device_id=partners[near],
            device_id_type=MESH,
        )
        pending[p].start()
        loads[p] = pltpu.make_async_copy(
            shares.at[within(every, count, near, 0, columns)], held[p], load_sem.at[p]
        )
        loads[p].start()
    for step in range(near):
        for p, (start, width, order) in enumerate(parts):
            turns = order[:-1][::-1]
            bit = turns[step]
            free = turns[step:]
            left = turns[step + 1 :]
            if step == 0:
                loads[p].wait()
            pending[p].wait()
            arrived = near_in[p] if step == 0 else came[p][step - 1]

            def merge(code):
                other = code if step == 0 else tuple(code[i] for i in sorted(free))
                add(held[p].at[code], held[p].at[code], arrived.at[other])

            for code in codes(free):
                if code[bit] == 1:
                    merge(code)
            lead = tuple(pl.ds(0, 2) if i in left else int(i == bit) for i in range(near))
            pending[p] = pltpu.make_async_remote_copy(
                src_ref=held[p].at[lead],
                dst_ref=came[p][step],
                send_sem=send_sem.at[p, step + 1],
                recv_sem=recv_sem.at[p, step + 1],
                device_id=partners[bit],
                device_id_type=MESH,
            )
            pending[p].start()
            for code in codes(free):
                if code[bit] == 0:
                    merge(code)
    for p, (start, width, order) in enumerate(parts):
        pending[p].wait()
        mine = (0,) * near
        out[:, pl.ds(start, width)] = held[p][mine].astype(jnp.float32) + came[p][near - 1][
            ...
        ].astype(jnp.float32)


def scatter_states(shares):
    bits = code_bits()
    parts = exchange_parts(bits)
    count = len(bits)
    low = jnp.bfloat16
    held = [pltpu.VMEM((2,) * (count - 1) + (TGT_LEN, width), low) for _, width, _ in parts]
    came = [
        [
            pltpu.VMEM((2,) * (count - 2 - step) + (TGT_LEN, width), low)
            for step in range(count - 1)
        ]
        for _, width, _ in parts
    ]
    return pl.pallas_call(
        functools.partial(scatter_kernel, bits, parts),
        out_shape=jax.ShapeDtypeStruct((TGT_LEN, D), jnp.float32),
        in_specs=[pl.BlockSpec(memory_space=pl.ANY)],
        out_specs=pl.BlockSpec(memory_space=pltpu.VMEM),
        scratch_shapes=[
            held,
            held,
            came,
            pltpu.SemaphoreType.DMA((len(parts),)),
            pltpu.SemaphoreType.DMA((len(parts), count)),
            pltpu.SemaphoreType.DMA((len(parts), count)),
        ],
        compiler_params=pltpu.CompilerParams(
            collective_id=3, has_side_effects=True, vmem_limit_bytes=56 << 20
        ),
    )(shares.reshape((2,) * count + (TGT_LEN, D)))


def merge_kernel(bits, stats, out, came, sent, send_sem, recv_sem):
    partners = [partner_of(bit) for bit in bits]
    meet(partners)
    count = len(bits)
    size = 1 << count
    out[...] = stats[...]
    position = lax.broadcasted_iota(jnp.int32, (size, TGT_LEN), 0)
    for step in range(count):
        mask = 1 << (count - 1 - step)
        sent[step] = out[...]
        copy = pltpu.make_async_remote_copy(
            src_ref=sent.at[step],
            dst_ref=came.at[step],
            send_sem=send_sem.at[step],
            recv_sem=recv_sem.at[step],
            device_id=partners[step],
            device_id_type=MESH,
        )
        copy.start()
        copy.wait()
        lower = (position // mask) % 2 == 0
        other = [
            jnp.where(
                lower,
                pltpu.roll(came[step, i], size - mask, 0),
                pltpu.roll(came[step, i], mask, 0),
            )
            for i in range(3)
        ]
        top = jnp.maximum(out[0], other[0])
        out[1] = out[1] * jnp.exp(out[0] - top) + other[1] * jnp.exp(other[0] - top)
        out[0] = top
        out[2] = out[2] + other[2]


def merge_stats(stats):
    bits = code_bits()
    shape = stats.shape
    return pl.pallas_call(
        functools.partial(merge_kernel, bits),
        out_shape=jax.ShapeDtypeStruct(shape, jnp.float32),
        in_specs=[pl.BlockSpec(memory_space=pltpu.VMEM)],
        out_specs=pl.BlockSpec(memory_space=pltpu.VMEM),
        scratch_shapes=[
            pltpu.VMEM((len(bits),) + shape, jnp.float32),
            pltpu.VMEM((len(bits),) + shape, jnp.float32),
            pltpu.SemaphoreType.DMA((len(bits),)),
            pltpu.SemaphoreType.DMA((len(bits),)),
        ],
        compiler_params=pltpu.CompilerParams(collective_id=4, has_side_effects=True),
    )(stats)


def weights_kernel(slots, groups, shards, vector, fact, fulls, vectors, facts, sems):
    holds, local_sem, send_sem, recv_sem, small_local, small_send, small_recv = sems
    slot, pb = lax.axis_index("slot"), lax.axis_index("pb")
    core, far = xor(pb, 1), xor(pb, 2)
    to_core, to_far = (slot, core), (slot, far)
    across = [(xor(slot, mask), pb) for mask in masks_below(slots)]
    meet([to_core, to_far] + across)

    jobs = []
    for shard, full in zip(shards, fulls):
        if len(shard.shape) == 3:
            for half in range(2):
                lead = pl.ds(half * (shard.shape[0] // 2), shard.shape[0] // 2)
                view = lambda ref, at, size, lead=lead: ref.at[lead, pl.ds(at, size)]
                jobs.append((shard, full, shard.shape[1], shard.shape[1], 0, view))
        elif shard.shape[1] > D:
            for half in range(2):
                lanes = pl.ds(half * (shard.shape[1] // 2), shard.shape[1] // 2)
                view = lambda ref, at, size, lanes=lanes: ref.at[pl.ds(at, size), lanes]
                jobs.append((shard, full, shard.shape[0], shard.shape[0], 0, view))
        else:
            for half in range(2):
                rows = shard.shape[0] // 2
                view = lambda ref, at, size: ref.at[pl.ds(at, size)]
                jobs.append((shard, full, shard.shape[0], rows, half * rows, view))

    def remote(source, target, job, kind, partner):
        return pltpu.make_async_remote_copy(
            src_ref=source,
            dst_ref=target,
            send_sem=send_sem.at[job, kind],
            recv_sem=recv_sem.at[job, kind],
            device_id=partner,
            device_id_type=MESH,
        )

    def describe(job):
        shard, full, block, rows, base, view = jobs[job]
        turn = job % 2
        first, second = (slot // (1 << turn)) % 2, (slot // (2 >> turn)) % 2
        to_first, to_second = across[turn], across[1 - turn]
        quarter, half = 3 * rows // 16, rows // 8
        split = base + 3 * rows // 4
        mine = pl.multiple_of(base + (second * 2 + first) * quarter, 16)
        pair = pl.multiple_of(base + second * 2 * quarter, 16)
        side = pl.multiple_of(split + second * half, 16)

        def there(owner, at):
            return pl.multiple_of(owner * block + at, 16)

        def send(kind, partner, owner, at, size, source=None):
            target = view(full, there(owner, at), size)
            return remote(target if source is None else source, target, job, kind, partner)

        own = view(shard, base, rows)
        stages = [
            [
                send(0, to_far, pb, mine, quarter, view(shard, mine, quarter)),
                send(1, to_far, pb, side, half, view(shard, side, half)),
                send(2, to_core, pb, base, rows, own),
            ],
            [
                send(3, to_first, far, mine, quarter),
                send(4, to_second, far, side, half),
            ],
            [send(5, to_second, far, pair, 2 * quarter)],
            [send(6, to_core, far, base, rows)],
        ]
        held = holds[job]
        into = pltpu.make_async_copy(own, held, local_sem.at[job, 0])
        onto = pltpu.make_async_copy(held, view(full, there(pb, base), rows), local_sem.at[job, 1])
        return stages, (into, onto)

    bits = [("pb", mask) for mask in masks_below(groups)] + [
        ("slot", mask) for mask in masks_below(slots)
    ]

    def small_copy(kind, source, target, partner):
        return pltpu.make_async_remote_copy(
            src_ref=source,
            dst_ref=target,
            send_sem=small_send.at[kind],
            recv_sem=small_recv.at[kind],
            device_id=partner,
            device_id_type=MESH,
        )

    def fact_copy(step):
        name, mask = bits[step]
        partner = (slot, xor(pb, mask)) if name == "pb" else (xor(slot, mask), pb)
        count = 1 << step
        source = fact if step == 0 else facts.at[pl.ds(0, count)]
        return small_copy(step, source, facts.at[pl.ds(count, count)], partner)

    near = len(bits)
    vector_copies = [
        small_copy(near, vector, vectors.at[pb], to_core),
        small_copy(near + 1, vector, vectors.at[pb], to_far),
    ]
    vector_last = small_copy(near + 2, vectors.at[far], vectors.at[far], to_core)
    small_own = [
        pltpu.make_async_copy(fact.at[0], facts.at[0], small_local.at[0]),
        pltpu.make_async_copy(vector, vectors.at[pb], small_local.at[1]),
    ]
    for copy in small_own + vector_copies:
        copy.start()
    plans = [describe(job) for job in range(len(jobs))]
    for step in range(max(len(jobs) + 4, len(bits) + 1)):
        for stage in range(5):
            job = step - stage
            if not 0 <= job < len(jobs):
                continue
            stages, (into, onto) = plans[job]
            if stage == 0:
                into.start()
            else:
                for copy in stages[stage - 1]:
                    copy.wait()
            if stage < 4:
                for copy in stages[stage]:
                    copy.start()
                if stage == 1:
                    into.wait()
                    onto.start()
            else:
                onto.wait()
        if step == 0:
            for copy in small_own:
                copy.wait()
        if step == 1:
            for copy in vector_copies:
                copy.wait()
            vector_last.start()
        if step == 2:
            vector_last.wait()
        if 0 < step <= len(bits):
            fact_copy(step - 1).wait()
        if step < len(bits):
            fact_copy(step).start()


def gather_weights(shards, vector, fact):
    slots, groups = lax.axis_size("slot"), lax.axis_size("pb")
    bits = (slots * groups).bit_length() - 1

    def widened(shard):
        axis = 1 if shard.ndim == 3 else 0
        shape = list(shard.shape)
        shape[axis] *= groups
        return jax.ShapeDtypeStruct(tuple(shape), shard.dtype)

    used = len(shards)

    def kernel(*refs):
        ins, outs, sems = refs[: used + 2], refs[used + 2 : 2 * used + 4], refs[2 * used + 4 :]
        weights_kernel(
            slots, groups, ins[:used], ins[used], ins[used + 1], outs[:used], outs[used],
            outs[used + 1], sems,
        )

    jobs = 2 * used
    holds = []
    for shard in shards:
        axis = 1 if shard.ndim == 2 and shard.shape[1] > D else 0
        shape = list(shard.shape)
        shape[axis] //= 2
        holds += [pltpu.VMEM(tuple(shape), shard.dtype)] * 2
    return pl.pallas_call(
        kernel,
        out_shape=[widened(shard) for shard in shards]
        + [
            jax.ShapeDtypeStruct((groups,) + vector.shape, vector.dtype),
            jax.ShapeDtypeStruct((slots * groups,) + fact.shape[1:], fact.dtype),
        ],
        in_specs=[pl.BlockSpec(memory_space=pl.ANY)] * (used + 2),
        out_specs=[pl.BlockSpec(memory_space=pl.ANY)] * (used + 2),
        scratch_shapes=[
            holds,
            pltpu.SemaphoreType.DMA((jobs, 2)),
            pltpu.SemaphoreType.DMA((jobs, 7)),
            pltpu.SemaphoreType.DMA((jobs, 7)),
            pltpu.SemaphoreType.DMA((2,)),
            pltpu.SemaphoreType.DMA((bits + 3,)),
            pltpu.SemaphoreType.DMA((bits + 3,)),
        ],
        compiler_params=pltpu.CompilerParams(
            collective_id=5, has_side_effects=True, vmem_limit_bytes=32 << 20
        ),
    )(*shards, vector, fact)


def own_facts(targets, owner, doc_scores):
    serving = jnp.arange(targets.shape[1]) == owner[0, 0]
    own = jnp.sum(jnp.where(serving[:, None], targets[0], 0), axis=0)
    half = (TGT_LEN // 2,)
    facts = [
        own.astype(jnp.float32),
        jnp.broadcast_to(owner[0, 0].astype(jnp.float32), half),
        jnp.broadcast_to(doc_scores[0, 0], half),
    ]
    return jnp.pad(jnp.concatenate(facts).reshape(1, 2, TGT_LEN), ((0, 0), (0, 6), (0, 0)))


def vocabulary_head(state_low, facts, questions, embed):
    slots, groups = lax.axis_size("slot"), lax.axis_size("pb")
    me = lax.axis_index("slot") * groups + lax.axis_index("pb")
    entries = embed.shape[0]
    tokens = slots * groups * TGT_LEN
    target_ids = facts[:, 0].astype(jnp.int32).reshape(tokens, 1)
    owners = facts[:, 1, 0].astype(jnp.int32).reshape(slots, groups)
    scores = facts[:, 1, TGT_LEN // 2].reshape(slots, groups)
    states = gather_states(state_low)
    logits = matmul_nt(states, embed)
    hit = target_ids - me * entries == lax.broadcasted_iota(jnp.int32, (tokens, entries), 1)
    top = jnp.max(logits, axis=1)
    total = jnp.sum(jnp.exp(logits - top[:, None]), axis=1)
    pick = jnp.sum(jnp.where(hit, logits, 0.0), axis=1)
    merged = merge_stats(jnp.stack([top, total, pick]).reshape(3, -1, TGT_LEN))
    log_total = (merged[0] + jnp.log(merged[1])).reshape(tokens)
    picked = merged[2].reshape(slots, groups, TGT_LEN) - log_total.reshape(slots, groups, TGT_LEN)
    serving = owners[:, :, None] == jnp.arange(questions)
    score_terms = jnp.where(serving, scores[:, :, None], BIG_NEGATIVE)
    token_terms = jnp.where(
        serving[..., None], (scores[:, :, None] + picked)[:, :, None, :], BIG_NEGATIVE
    )
    score_top, token_top = jnp.max(score_terms, axis=0), jnp.max(token_terms, axis=0)
    score_norm = score_top + jnp.log(jnp.sum(jnp.exp(score_terms - score_top), axis=0))
    token_mix = token_top + jnp.log(jnp.sum(jnp.exp(token_terms - token_top), axis=0))
    group_tokens = questions * TGT_LEN
    count = groups * group_tokens
    losses = -jnp.sum(token_mix - score_norm[:, :, None], axis=(1, 2)) / group_tokens
    own_mix = jnp.sum(jnp.where(serving[..., None], token_mix[None], 0.0), axis=2)
    own_norm = jnp.sum(jnp.where(serving, score_norm[None], 0.0), axis=2)
    posterior = jnp.exp(scores[:, :, None] + picked - own_mix)
    prior = jnp.exp(scores - own_norm)
    token_grad = (-posterior / count).reshape(tokens, 1)
    score_grads = -jnp.sum(posterior - prior[:, :, None], axis=2) / count
    delta = lax.optimization_barrier(
        to_low(token_grad * (jnp.where(hit, 1.0, 0.0) - jnp.exp(logits - log_total[:, None])))
    )
    grad_state = scatter_states(to_low(matmul(delta, embed)))
    return (losses[:1], score_grads[:1, :1], grad_state, delta, states)


def local(
    enc_input,
    dec_input,
    doc_scores,
    owner,
    targets,
    enc_attn,
    enc_up,
    enc_down,
    enc_up_bias,
    enc_bias,
    enc_gain,
    dec_self,
    dec_cross,
    dec_up,
    dec_down,
    dec_up_bias,
    dec_bias,
    dec_gain,
    embed,
):
    pb_size = lax.axis_size("pb")
    width = D // pb_size
    vectors = (enc_up_bias, enc_bias, enc_gain, dec_up_bias, dec_bias, dec_gain)
    rows = [v.size // width for v in vectors]
    starts = [sum(rows[:i]) for i in range(len(rows) + 1)]
    passage_low = enc_input[0, 0]
    passage = passage_low.astype(jnp.float32)
    question_low = dec_input[0, 0]
    question = question_low.astype(jnp.float32)

    own_vectors = jnp.concatenate([v.reshape(-1, width) for v in vectors])
    (
        encoder_attn,
        encoder_up,
        encoder_down,
        decoder_self,
        decoder_cross,
        decoder_down,
        packed,
        facts,
    ) = gather_weights(
        (enc_attn, enc_up, enc_down, dec_self, dec_cross, dec_down),
        jnp.pad(own_vectors, ((0, -starts[-1] % 32), (0, 0))),
        own_facts(targets, owner, doc_scores),
    )
    packed, dec_up = lax.optimization_barrier((packed, dec_up))
    decoder_up = lax.all_gather(dec_up, "pb", axis=0, tiled=True)
    packed = packed.astype(jnp.float32)
    unpacked = [packed[:, starts[i] : starts[i + 1], :] for i in range(len(rows))]
    encoder_upbias = unpacked[0].reshape(-1)
    encoder_bias = unpacked[1].transpose(1, 0, 2).reshape(-1, D)
    encoder_gain = unpacked[2].transpose(1, 0, 2).reshape(-1, D)
    decoder_upbias = unpacked[3].reshape(-1)
    decoder_bias = unpacked[4].transpose(1, 0, 2).reshape(-1, D)
    decoder_gain = unpacked[5].transpose(1, 0, 2).reshape(-1, D)
    attn_out, enc_saved = attend_forward(
        passage_low,
        passage_low,
        encoder_attn,
        encoder_bias[0],
        encoder_bias[1],
        encoder_bias[2],
        False,
    )
    enc_first, enc_norm_one = norm_forward(passage + attn_out, encoder_gain[0], encoder_bias[3])
    enc_first_low = to_low(enc_first)
    enc_hidden, enc_slope = gelu_with_slope(matmul(enc_first_low, encoder_up) + encoder_upbias)
    enc_hidden_low = to_low(enc_hidden)
    ffn_out = matmul(enc_hidden_low, encoder_down) + encoder_bias[4]
    encoded, enc_norm_two = norm_forward(enc_first + ffn_out, encoder_gain[1], encoder_bias[5])
    memory_low = to_low(encoded)
    self_out, self_saved = attend_forward(
        question_low,
        question_low,
        decoder_self,
        decoder_bias[0],
        decoder_bias[1],
        decoder_bias[2],
        True,
    )
    dec_first, dec_norm_one = norm_forward(question + self_out, decoder_gain[0], decoder_bias[3])
    dec_first_low = to_low(dec_first)
    cross_out, cross_saved = attend_forward(
        dec_first_low,
        memory_low,
        decoder_cross,
        decoder_bias[4],
        decoder_bias[5],
        decoder_bias[6],
        False,
    )
    dec_second, dec_norm_two = norm_forward(dec_first + cross_out, decoder_gain[1], decoder_bias[7])
    dec_second_low = to_low(dec_second)
    dec_hidden, dec_slope = gelu_with_slope(matmul(dec_second_low, decoder_up) + decoder_upbias)
    dec_hidden_low = to_low(dec_hidden)
    dec_ffn_out = matmul(dec_hidden_low, decoder_down) + decoder_bias[8]
    state, dec_norm_three = norm_forward(dec_second + dec_ffn_out, decoder_gain[2], decoder_bias[9])
    state_low = to_low(state)

    loss, score_grad, grad_state_sum, delta, states = vocabulary_head(
        state_low, facts, targets.shape[1], embed
    )

    grad_third, gain_third, shift_third = norm_backward(
        grad_state_sum, dec_norm_three, decoder_gain[2]
    )
    dec_downbias_grad = jnp.sum(grad_third, axis=0)
    third_low = to_low(grad_third)
    grad_before = matmul_nt(third_low, decoder_down) * dec_slope
    dec_upbias_grad = jnp.sum(grad_before, axis=0)
    before_low = to_low(grad_before)
    grad_second, gain_second, shift_second = norm_backward(
        grad_third + matmul_nt(before_low, decoder_up), dec_norm_two, decoder_gain[1]
    )
    cross_query, grad_memory, dec_cross_pairs, cross_biases = attend_backward(
        grad_second, dec_first_low, memory_low, decoder_cross, cross_saved, False
    )
    grad_first, gain_first, shift_first = norm_backward(
        grad_second + cross_query, dec_norm_one, decoder_gain[0]
    )
    self_query, self_memory, dec_self_pairs, self_biases = attend_backward(
        grad_first, question_low, question_low, decoder_self, self_saved, True
    )
    question_grad = grad_first + self_query + self_memory
    enc_grad_two, enc_gain_two, enc_shift_two = norm_backward(
        grad_memory, enc_norm_two, encoder_gain[1]
    )
    enc_downbias_grad = jnp.sum(enc_grad_two, axis=0)
    enc_two_low = to_low(enc_grad_two)
    enc_grad_before = matmul_nt(enc_two_low, encoder_down) * enc_slope
    enc_upbias_grad = jnp.sum(enc_grad_before, axis=0)
    enc_before_low = to_low(enc_grad_before)
    enc_grad_one, enc_gain_one, enc_shift_one = norm_backward(
        enc_grad_two + matmul_nt(enc_before_low, encoder_up), enc_norm_one, encoder_gain[0]
    )
    enc_query, enc_memory, enc_attn_pairs, enc_biases = attend_backward(
        enc_grad_one, passage_low, passage_low, encoder_attn, enc_saved, False
    )
    passage_grad = enc_grad_one + enc_query + enc_memory
    operands, plan = [], []

    def share(left, right, tall=False):
        where = []
        for operand in (left, right):
            known = [i for i, other in enumerate(operands) if other is operand]
            where.append(known[0] if known else len(operands))
            if not known:
                operands.append(operand)
        for i in range(left.shape[1] * right.shape[1] // (D * D)):
            plan.append((where[0], where[1], i, tall))

    for left, right in enc_attn_pairs:
        share(left, right)
    share(enc_first_low, enc_before_low)
    share(enc_hidden_low, enc_two_low, tall=True)
    for left, right in dec_self_pairs + dec_cross_pairs:
        share(left, right)
    share(dec_second_low, before_low)
    share(dec_hidden_low, third_low, tall=True)
    enc_bias_grad = jnp.stack(
        [
            enc_biases[0],
            enc_biases[1],
            enc_biases[2],
            enc_shift_one,
            enc_downbias_grad,
            enc_shift_two,
        ]
    )
    enc_gain_grad = jnp.stack([enc_gain_one, enc_gain_two])
    dec_bias_grad = jnp.stack(
        [
            self_biases[0],
            self_biases[1],
            self_biases[2],
            shift_first,
            cross_biases[0],
            cross_biases[1],
            cross_biases[2],
            shift_second,
            dec_downbias_grad,
            shift_third,
        ]
    )
    dec_gain_grad = jnp.stack([gain_first, gain_second, gain_third])
    vector_grads = jnp.concatenate(
        [
            enc_upbias_grad.reshape(pb_size, -1, width),
            enc_bias_grad.reshape(-1, pb_size, width).transpose(1, 0, 2),
            enc_gain_grad.reshape(-1, pb_size, width).transpose(1, 0, 2),
            dec_upbias_grad.reshape(pb_size, -1, width),
            dec_bias_grad.reshape(-1, pb_size, width).transpose(1, 0, 2),
            dec_gain_grad.reshape(-1, pb_size, width).transpose(1, 0, 2),
        ],
        axis=1,
    )
    spare = -starts[-1] % 32
    small = jnp.pad(vector_grads, ((0, 0), (0, spare), (0, 0))).reshape(pb_size, -1, D)
    if lax.axis_size("slot") * 16 <= UNIT:
        summed_parts, small_sum, embed_grad = sync_gradients(
            plan, operands, small, (delta.T, states)
        )
    else:
        embed_grad = matmul_tn(delta, states)
        summed_parts, small_sum = sync_gradients(plan, operands, small)
    units = summed_parts.reshape(-1, width, D)
    square = lambda at: units[at : at + 4].astype(jnp.float32)
    wide = lambda at: jnp.concatenate([units[at + i].astype(jnp.float32) for i in range(4)], axis=1)
    tall = lambda at: square(at).reshape(-1, D)
    vector_sum = small_sum.reshape(-1, width)
    vector_out = [
        vector_sum[starts[i] : starts[i + 1]].reshape(v.shape) for i, v in enumerate(vectors)
    ]
    summed = (
        (square(0), wide(4), tall(8))
        + tuple(vector_out[:3])
        + (square(12), square(16), wide(20), tall(24))
        + tuple(vector_out[3:])
    )
    return (
        (
            loss,
            passage_grad.reshape(1, 1, SRC_LEN, D),
            question_grad.reshape(1, 1, TGT_LEN, D),
            score_grad,
        )
        + tuple(summed)
        + (embed_grad,)
    )


def solution(mesh):
    placed = (
        P("pb", "slot", None, None),
        P("pb", "slot", None, None),
        P("pb", "slot"),
        P("pb", "slot"),
        P("pb", None, None),
        P(None, "pb", None),
        P("pb", None),
        P("pb", None),
        P("pb"),
        P(None, "pb"),
        P(None, "pb"),
        P(None, "pb", None),
        P(None, "pb", None),
        P("pb", None),
        P("pb", None),
        P("pb"),
        P(None, "pb"),
        P(None, "pb"),
        P(("slot", "pb"), None),
    )
    return jax.shard_map(
        local,
        mesh=mesh,
        in_specs=placed,
        out_specs=(
            P("pb"),
            P("pb", "slot", None, None),
            P("pb", "slot", None, None),
            P("pb", "slot"),
            P(None, "pb", None),
            P("pb", None),
            P("pb", None),
            P("pb"),
            P(None, "pb"),
            P(None, "pb"),
            P(None, "pb", None),
            P(None, "pb", None),
            P("pb", None),
            P("pb", None),
            P("pb"),
            P(None, "pb"),
            P(None, "pb"),
            P(("slot", "pb"), None),
        ),
        check_vma=False,
    )
```

```python
import functools
import math

import jax
import jax.numpy as jnp
from jax import lax
from jax.experimental import pallas as pl
from jax.experimental.pallas import tpu as pltpu
from jax.sharding import PartitionSpec as P

D = 1024
HEADS = 16
HEAD_DIM = 64
SRC_LEN = 384
TGT_LEN = 128
MESH = pl.DeviceIdType.MESH
UNIT = 256
RING = 8
SIDE_STEPS = 16


BIG_NEGATIVE = -1e30
MASK_FILL = -1000000000.0


def matmul(left, right):
    return jnp.dot(left, right, preferred_element_type=jnp.float32)


def matmul_nt(left, right):
    return lax.dot_general(
        left, right, (((1,), (1,)), ((), ())), preferred_element_type=jnp.float32
    )


def matmul_tn(left, right):
    return lax.dot_general(
        left, right, (((0,), (0,)), ((), ())), preferred_element_type=jnp.float32
    )


def to_low(value):
    return value.astype(jnp.bfloat16)


def norm_forward(total, gain, shift):
    centered = total - jnp.mean(total, axis=-1, keepdims=True)
    inverse = lax.rsqrt(jnp.mean(centered * centered, axis=-1, keepdims=True) + 1e-05)
    normed = centered * inverse
    return (normed * gain + shift, (normed, inverse))


def norm_backward(upstream, saved, gain):
    normed, inverse = saved
    scaled = upstream * gain
    inner = (
        scaled
        - jnp.mean(scaled, axis=-1, keepdims=True)
        - normed * jnp.mean(scaled * normed, axis=-1, keepdims=True)
    )
    return (inverse * inner, jnp.sum(upstream * normed, axis=0), jnp.sum(upstream, axis=0))


def head_mask(which):
    return lax.broadcasted_iota(jnp.int32, (1, 2 * HEAD_DIM), 1) // HEAD_DIM == which


def only_head(pair, which):
    return jnp.where(head_mask(which), pair.astype(jnp.float32), 0.0).astype(pair.dtype)


def both_heads(first, second):
    return jnp.where(head_mask(0), first, second)


def attention_weights(queries, keys, causal):
    scores = matmul_nt(queries, keys) * HEAD_DIM ** (-0.5)
    if causal:
        rows = lax.broadcasted_iota(jnp.int32, scores.shape, 0)
        columns = lax.broadcasted_iota(jnp.int32, scores.shape, 1)
        scores = jnp.where(rows >= columns, scores, MASK_FILL)
    shifted = jnp.exp(scores - jnp.max(scores, axis=-1, keepdims=True))
    return shifted / jnp.sum(shifted, axis=-1, keepdims=True)


def attend_kernel(causal, queries, keys, values, out):
    parts = []
    for which in range(2):
        probs = attention_weights(only_head(queries[...], which), keys[...], causal)
        parts.append(matmul(to_low(probs), values[...]))
    out[...] = to_low(both_heads(*parts))


def attend_grad_kernel(
    causal, queries, keys, values, upstream, grad_q, grad_k, grad_v, sum_q, sum_v
):
    parts = []
    for which in range(2):
        probs = attention_weights(only_head(queries[...], which), keys[...], causal)
        grad_probs = matmul_nt(only_head(upstream[...], which), values[...])
        inner = jnp.sum(grad_probs * probs, axis=-1, keepdims=True)
        grad_scores = to_low(probs * (grad_probs - inner))
        parts.append(
            (
                matmul(grad_scores, keys[...]),
                matmul_tn(grad_scores, queries[...]),
                matmul_tn(to_low(probs), upstream[...]),
            )
        )
    scale = HEAD_DIM ** (-0.5)
    query, key, value = [both_heads(*pair) for pair in zip(*parts)]
    query = query * scale
    grad_q[...] = to_low(query)
    grad_k[...] = to_low(key * scale)
    grad_v[...] = to_low(value)
    sum_q[...] = jnp.broadcast_to(jnp.sum(query, axis=0, keepdims=True), sum_q.shape)
    sum_v[...] = jnp.broadcast_to(jnp.sum(value, axis=0, keepdims=True), sum_v.shape)


def head_pairs(rows):
    return pl.BlockSpec((rows, 2 * HEAD_DIM), lambda pair: (0, pair))


def attention_cost(rows, columns, products):
    return pl.CostEstimate(
        flops=2 * products * rows * columns * D,
        bytes_accessed=4 * (rows + columns) * D * products,
        transcendentals=HEADS * rows * columns,
    )


def attend_forward(query_low, memory_low, matrices, bias_query, bias_value, bias_out, causal):
    rows, columns = query_low.shape[0], memory_low.shape[0]
    queries = to_low(matmul(query_low, matrices[0]) + bias_query)
    keys = to_low(matmul(memory_low, matrices[1]))
    values = to_low(matmul(memory_low, matrices[2]) + bias_value)
    context = pl.pallas_call(
        functools.partial(attend_kernel, causal),
        grid=(HEADS // 2,),
        out_shape=jax.ShapeDtypeStruct((rows, D), jnp.bfloat16),
        in_specs=[head_pairs(rows), head_pairs(columns), head_pairs(columns)],
        out_specs=head_pairs(rows),
        cost_estimate=attention_cost(rows, columns, 2),
        compiler_params=pltpu.CompilerParams(vmem_limit_bytes=24 << 20),
    )(queries, keys, values)
    output = matmul(context, matrices[3]) + bias_out
    return (output, (queries, keys, values, context))


def attend_backward(upstream, query_low, memory_low, matrices, saved, causal):
    queries, keys, values, context = saved
    rows, columns = query_low.shape[0], memory_low.shape[0]
    upstream_low = to_low(upstream)
    grad_context = to_low(matmul_nt(upstream_low, matrices[3]))
    low, sums = jnp.bfloat16, jax.ShapeDtypeStruct((8, D), jnp.float32)
    queries_low, keys_low, values_low, query_sum, value_sum = pl.pallas_call(
        functools.partial(attend_grad_kernel, causal),
        grid=(HEADS // 2,),
        out_shape=(
            jax.ShapeDtypeStruct((rows, D), low),
            jax.ShapeDtypeStruct((columns, D), low),
            jax.ShapeDtypeStruct((columns, D), low),
            sums,
            sums,
        ),
        in_specs=[head_pairs(n) for n in (rows, columns, columns, rows)],
        out_specs=tuple(head_pairs(n) for n in (rows, columns, columns, 8, 8)),
        cost_estimate=attention_cost(rows, columns, 5),
        compiler_params=pltpu.CompilerParams(vmem_limit_bytes=24 << 20),
    )(queries, keys, values, grad_context)
    grad_query_input = matmul_nt(queries_low, matrices[0])
    grad_memory_input = matmul_nt(keys_low, matrices[1]) + matmul_nt(values_low, matrices[2])
    grad_pairs = [
        (query_low, queries_low),
        (memory_low, keys_low),
        (memory_low, values_low),
        (context, upstream_low),
    ]
    bias_grads = (query_sum[0], value_sum[0], jnp.sum(upstream, axis=0))
    return (grad_query_input, grad_memory_input, grad_pairs, bias_grads)


def gelu_with_slope(value):
    share = 0.5 * (1.0 + lax.erf(value * 0.5**0.5))
    density = jnp.exp(-0.5 * value * value) * (2.0 * math.pi) ** -0.5
    return value * share, share + value * density


def masks_below(size):
    return [1 << i for i in range(size.bit_length() - 1)]


def xor(value, mask):
    return jnp.where((value // mask) % 2 == 0, value + mask, value - mask)


def sync_kernel(slots, count, plan, operands, small, side, out, small_out, side_out, scratch):
    left_buffer, right_buffer, parts, core_in, far_out, far_keep, far_in = scratch[:7]
    half_out, half_keep, half_in, full = scratch[7:11]
    small_core, small_far, small_in, small_out_far, small_out_slot = scratch[11:16]
    load_sem, store_sem, send_sem, recv_sem, small_send, small_recv = scratch[16:22]
    if side:
        side_left, side_right, side_total, side_sem, side_store = scratch[22:]
    masks = masks_below(slots)
    levels = len(masks)
    rows = full.shape[1]
    slot, pb = lax.axis_index("slot"), lax.axis_index("pb")
    core, far = xor(pb, 1), xor(pb, 2)
    far_core = xor(core, 2)
    partners = [(slot, core), (slot, far)] + [(xor(slot, mask), pb) for mask in masks]
    bits = [(slot // mask) % 2 for mask in masks]

    barrier = pltpu.get_barrier_semaphore()
    for partner in partners:
        pl.semaphore_signal(barrier, inc=1, device_id=partner, device_id_type=MESH)
    pl.semaphore_wait(barrier, len(partners))

    def remote(source, target, stage, at, partner):
        return pltpu.make_async_remote_copy(
            src_ref=source,
            dst_ref=target,
            send_sem=send_sem.at[stage, at],
            recv_sem=recv_sem.at[stage, at],
            device_id=partner,
            device_id_type=MESH,
        )

    def core_copies(c):
        at = lax.rem(c, RING)
        ring = lax.rem(c, 4)
        pair = lax.rem(c, 2)
        return (
            remote(parts.at[pair, core], core_in.at[ring, 0], 0, at, partners[0]),
            remote(parts.at[pair, far_core], core_in.at[ring, 1], 1, at, partners[0]),
        )

    def load(unit):
        pair = lax.rem(unit, 2)
        for at, (left, right, k, tall) in enumerate(plan):

            @pl.when(unit == at)
            def _():
                tokens = operands[left].shape[0]
                rows_at = pl.ds(0, tokens)
                if tall:
                    for p in range(4):
                        pltpu.make_async_copy(
                            operands[left].at[:, pl.ds((4 * p + k) * UNIT, UNIT)],
                            left_buffer.at[pair, rows_at, pl.ds(p * UNIT, UNIT)],
                            load_sem.at[0, pair],
                        ).start()
                else:
                    pltpu.make_async_copy(
                        operands[left], left_buffer.at[pair, rows_at], load_sem.at[0, pair]
                    ).start()
                column = 0 if tall else k * D
                pltpu.make_async_copy(
                    operands[right].at[:, pl.ds(column, D)],
                    right_buffer.at[pair, rows_at],
                    load_sem.at[1, pair],
                ).start()

    def product(unit, chunk, offset):
        pair = lax.rem(unit, 2)
        lengths = [operands[left].shape[0] for left, _, _, _ in plan]
        for tokens in sorted(set(lengths)):
            among = functools.reduce(
                jnp.logical_or, [unit == at for at, n in enumerate(lengths) if n == tokens]
            )

            @pl.when(among)
            def _():
                rows_at = pl.ds(0, tokens)
                for i, buffer in enumerate((left_buffer, right_buffer)):
                    whole = buffer.at[pair, rows_at]
                    pltpu.make_async_copy(whole, whole, load_sem.at[i, pair]).wait()

                @pl.loop(0, 4)
                def _(p):
                    columns = pl.ds(pl.multiple_of(p * UNIT, UNIT), UNIT)
                    total = lax.dot_general(
                        left_buffer[pair, rows_at, columns],
                        right_buffer[pair, rows_at, :],
                        (((0,), (0,)), ((), ())),
                        preferred_element_type=jnp.float32,
                    )
                    parts[lax.rem(chunk, 2), p, pl.ds(offset, UNIT), :] = total.astype(
                        parts.dtype
                    )

    def far_copy(c):
        ring = lax.rem(c, 4)
        return remote(far_out.at[ring], far_in.at[ring], 2, lax.rem(c, RING), partners[1])

    def halve_copy(level, c):
        ring = lax.rem(c, 4)
        return remote(
            half_out[level].at[ring],
            half_in[level].at[ring],
            3 + level,
            lax.rem(c, RING),
            partners[2 + level],
        )

    def join_copy(level, c):
        at = lax.rem(c, RING)
        size = rows >> (level + 1)
        offset = sum(bits[i] * (rows >> (i + 1)) for i in range(level + 1))
        where = pl.ds(pl.multiple_of(offset, size), size)
        return remote(
            full.at[at, where], full.at[at, where], 3 + levels + level, at, partners[2 + level]
        )

    def store(c):
        at = lax.rem(c, RING)
        return pltpu.make_async_copy(full.at[at], out.at[c], store_sem.at[at])

    def add(target, left, right, size):
        tile = min(size, 32)

        @pl.loop(0, size // tile)
        def _(i):
            at = pl.ds(pl.multiple_of(i * tile, tile), tile)
            total = left[at, :].astype(jnp.float32) + right[at, :].astype(jnp.float32)
            target[at, :] = total.astype(target.dtype)

    def small_core_copies():
        return [
            pltpu.make_async_remote_copy(
                src_ref=small.at[source],
                dst_ref=small_core.at[i],
                send_sem=small_send.at[i],
                recv_sem=small_recv.at[i],
                device_id=partners[0],
                device_id_type=MESH,
            )
            for i, source in ((0, core), (1, far_core))
        ]

    def small_far_copy():
        return pltpu.make_async_remote_copy(
            src_ref=small_out_far,
            dst_ref=small_far,
            send_sem=small_send.at[2],
            recv_sem=small_recv.at[2],
            device_id=partners[1],
            device_id_type=MESH,
        )

    def small_slot_copy(level):
        return pltpu.make_async_remote_copy(
            src_ref=small_out_slot.at[level],
            dst_ref=small_in.at[level],
            send_sem=small_send.at[3 + level],
            recv_sem=small_recv.at[3 + level],
            device_id=partners[2 + level],
            device_id_type=MESH,
        )

    def small_stage(step):
        if step == 0:
            for copy in small_core_copies():
                copy.start()
        elif step == 1:
            for copy in small_core_copies():
                copy.wait()
            small_out_far[...] = small[far] + small_core[1]
            small_out[...] = small[pb] + small_core[0]
            small_far_copy().start()
        elif step == 2:
            small_far_copy().wait()
            small_out[...] = small_out[...] + small_far[...]
            small_out_slot[0] = small_out[...]
            small_slot_copy(0).start()
        else:
            level = step - 3
            small_slot_copy(level).wait()
            small_out[...] = small_out[...] + small_in[level]
            if level + 1 < levels:
                small_out_slot[level + 1] = small_out[...]
                small_slot_copy(level + 1).start()

    def stage(step, c):
        ring = lax.rem(c, 4)
        pair = lax.rem(c, 2)
        at = lax.rem(c, RING)
        if step == 0:
            for copy in core_copies(c):
                copy.start()
        elif step == 1:
            for copy in core_copies(c):
                copy.wait()
            add(far_out.at[ring], parts.at[pair, far], core_in.at[ring, 1], rows)
            far_copy(c).start()
            add(far_keep.at[ring], parts.at[pair, pb], core_in.at[ring, 0], rows)
        elif step < 2 + levels:
            level = step - 2
            size = rows >> (level + 1)
            if level == 0:
                far_copy(c).wait()
                left, right = far_keep.at[ring], far_in.at[ring]
            else:
                halve_copy(level - 1, c).wait()
                left, right = half_keep[level - 1].at[ring], half_in[level - 1].at[ring]
            mine = pl.ds(pl.multiple_of(bits[level] * size, size), size)
            other = pl.ds(pl.multiple_of((1 - bits[level]) * size, size), size)
            add(half_out[level].at[ring], left.at[other], right.at[other], size)
            halve_copy(level, c).start()
            add(half_keep[level].at[ring], left.at[mine], right.at[mine], size)
        elif step == 2 + levels:
            level = levels - 1
            size = rows >> levels
            halve_copy(level, c).wait()
            offset = sum(bits[i] * (rows >> (i + 1)) for i in range(levels))
            where = pl.ds(pl.multiple_of(offset, size), size)
            add(full.at[at, where], half_keep[level].at[ring], half_in[level].at[ring], size)
            join_copy(level, c).start()
        elif step < 2 + 2 * levels:
            level = levels - 1 - (step - 3 - levels)
            join_copy(level, c).wait()
            join_copy(level - 1, c).start()
        elif step == 2 + 2 * levels:
            join_copy(0, c).wait()
            store(c).start()
        else:
            store(c).wait()

    stages = 4 + 2 * levels

    def side_loads(step):
        pair = lax.rem(step, 2)
        tokens = side_right.shape[1]
        at = pl.ds(pl.multiple_of(step * tokens, tokens), tokens)
        return (
            pltpu.make_async_copy(side[0].at[at], side_left.at[pair], side_sem.at[0, pair]),
            pltpu.make_async_copy(side[1].at[at], side_right.at[pair], side_sem.at[1, pair]),
        )

    def side_product(step):
        pair = lax.rem(step, 2)
        for copy in side_loads(step):
            copy.wait()

        @pl.loop(0, side_total.shape[0] // UNIT)
        def _(i):
            at = pl.ds(pl.multiple_of(i * UNIT, UNIT), UNIT)
            side_total[at, :] += matmul_tn(side_left[pair, :, at], side_right[pair])

    per = rows // UNIT
    load(jnp.int32(0))
    if side:
        side_total[...] = jnp.zeros_like(side_total)
        side_copy = pltpu.make_async_copy(side_total, side_out, side_store)
        for copy in side_loads(jnp.int32(0)):
            copy.start()

    @pl.loop(0, count + stages)
    def _(it):
        for step in range(3 + levels):

            @pl.when(it == step)
            def _():
                small_stage(step)

        for step in range(stages):
            c = it - 1 - step

            @pl.when(jnp.logical_and(c >= 0, c < count))
            def _():
                stage(step, c)

        for i in range(per):

            @pl.when(it < count)
            def _():
                unit = it * per + i
                load(unit + 1)
                product(unit, it, i * UNIT)

        if side:

            @pl.when(it < SIDE_STEPS - 1)
            def _():
                for copy in side_loads(it + 1):
                    copy.start()

            @pl.when(it < SIDE_STEPS)
            def _():
                side_product(it)

            @pl.when(it == SIDE_STEPS)
            def _():
                side_copy.start()

    if side:
        side_copy.wait()


def sync_gradients(plan, operands, small, side=()):
    slots = lax.axis_size("slot")
    rows, columns = max(UNIT, 16 * slots), D
    count = len(plan) * UNIT // rows
    levels = slots.bit_length() - 1
    small_rows = small.shape[1:]
    low = jnp.bfloat16
    longest = max(operand.shape[0] for operand in operands)
    block = lambda *lead: pltpu.VMEM(lead + (columns,), low)
    halves = [block(4, rows >> (i + 1)) for i in range(levels)]
    used, more = len(operands), len(side)
    outs = 3 if side else 2
    shapes = [
        jax.ShapeDtypeStruct((count, rows, columns), low),
        jax.ShapeDtypeStruct(small_rows, jnp.float32),
    ]
    places = [pl.BlockSpec(memory_space=pl.ANY), pl.BlockSpec(memory_space=pltpu.VMEM)]
    side_scratch = []
    if side:
        tokens, entries = side[0].shape
        shapes.append(jax.ShapeDtypeStruct((entries, columns), jnp.float32))
        places.append(pl.BlockSpec(memory_space=pl.ANY))
        side_scratch = [
            pltpu.VMEM((2, tokens // SIDE_STEPS, entries), low),
            pltpu.VMEM((2, tokens // SIDE_STEPS, columns), low),
            pltpu.VMEM((entries, columns), jnp.float32),
            pltpu.SemaphoreType.DMA((2, 2)),
            pltpu.SemaphoreType.DMA,
        ]

    def kernel(*refs):
        ins, results = refs[: used + 1 + more], refs[used + 1 + more :]
        sync_kernel(
            slots,
            count,
            plan,
            ins[:used],
            ins[used],
            ins[used + 1 :],
            results[0],
            results[1],
            results[2] if side else None,
            results[outs:],
        )

    return pl.pallas_call(
        kernel,
        out_shape=shapes,
        in_specs=[pl.BlockSpec(memory_space=pl.ANY)] * used
        + [pl.BlockSpec(memory_space=pltpu.VMEM)]
        + [pl.BlockSpec(memory_space=pl.ANY)] * more,
        out_specs=places,
        scratch_shapes=[
            block(2, longest),
            block(2, longest),
            block(2, 4, rows),
            block(4, 2, rows),
            block(4, rows),
            block(4, rows),
            block(4, rows),
            halves,
            halves,
            halves,
            block(RING, rows),
            pltpu.VMEM((2,) + small_rows, jnp.float32),
            pltpu.VMEM(small_rows, jnp.float32),
            pltpu.VMEM((levels,) + small_rows, jnp.float32),
            pltpu.VMEM(small_rows, jnp.float32),
            pltpu.VMEM((levels,) + small_rows, jnp.float32),
            pltpu.SemaphoreType.DMA((2, 2)),
            pltpu.SemaphoreType.DMA((RING,)),
            pltpu.SemaphoreType.DMA((3 + 2 * levels, RING)),
            pltpu.SemaphoreType.DMA((3 + 2 * levels, RING)),
            pltpu.SemaphoreType.DMA((3 + levels,)),
            pltpu.SemaphoreType.DMA((3 + levels,)),
        ]
        + side_scratch,
        compiler_params=pltpu.CompilerParams(
            collective_id=1, has_side_effects=True, vmem_limit_bytes=56 << 20
        ),
    )(*operands, small, *side)


def code_bits():
    return [("slot", mask) for mask in masks_below(lax.axis_size("slot"))[::-1]] + [
        ("pb", mask) for mask in masks_below(lax.axis_size("pb"))[::-1]
    ]


def exchange_parts(bits):
    slot_bits = [i for i, (name, mask) in enumerate(bits) if name == "slot"]
    pb_bits = [i for i, (name, mask) in enumerate(bits) if name == "pb"]
    high, low, far, near = slot_bits[:-1], slot_bits[-1:], pb_bits[:-1], pb_bits[-1:]
    first, second = high + low + far + near, far + high + low + near
    return [
        (0, 256, first),
        (256, 256, second),
        (512, 256, first),
        (768, 128, second),
        (896, 128, low + far + high + near),
    ]


def partner_of(bit):
    name, mask = bit
    slot, pb = lax.axis_index("slot"), lax.axis_index("pb")
    return (xor(slot, mask), pb) if name == "slot" else (slot, xor(pb, mask))


def meet(partners):
    barrier = pltpu.get_barrier_semaphore()
    for partner in partners:
        pl.semaphore_signal(barrier, inc=1, device_id=partner, device_id_type=MESH)
    pl.semaphore_wait(barrier, len(partners))


def within(held, count, fixed, value, columns):
    lead = [pl.ds(0, 2) if i in held else 0 for i in range(count)]
    if fixed is not None:
        lead[fixed] = value
    return tuple(lead) + (slice(None), columns)


def gather_kernel(bits, parts, own, out, local_sem, send_sem, recv_sem):
    count = len(bits)
    partners = [partner_of(bit) for bit in bits]
    meet(partners)
    local = pltpu.make_async_copy(
        own, out.at[within([], count, None, 0, slice(None))], local_sem
    )
    local.start()
    pending = [None] * len(parts)
    for step in range(count):
        for p, (start, width, order) in enumerate(parts):
            columns = pl.ds(start, width)
            if step > 0:
                pending[p].wait()
            if step == 1 and p == 0:
                local.wait()
            bit = order[step]
            held = order[:step]
            source = (
                own.at[:, columns] if step == 0 else out.at[within(held, count, None, 0, columns)]
            )
            pending[p] = pltpu.make_async_remote_copy(
                src_ref=source,
                dst_ref=out.at[within(held, count, bit, 1, columns)],
                send_sem=send_sem.at[p, step],
                recv_sem=recv_sem.at[p, step],
                device_id=partners[bit],
                device_id_type=MESH,
            )
            pending[p].start()
    for copy in pending:
        copy.wait()


def gather_states(own):
    bits = code_bits()
    parts = exchange_parts(bits)
    out = pl.pallas_call(
        functools.partial(gather_kernel, bits, parts),
        out_shape=jax.ShapeDtypeStruct((2,) * len(bits) + own.shape, own.dtype),
        in_specs=[pl.BlockSpec(memory_space=pl.ANY)],
        out_specs=pl.BlockSpec(memory_space=pl.ANY),
        scratch_shapes=[
            pltpu.SemaphoreType.DMA,
            pltpu.SemaphoreType.DMA((len(parts), len(bits))),
            pltpu.SemaphoreType.DMA((len(parts), len(bits))),
        ],
        compiler_params=pltpu.CompilerParams(collective_id=2, has_side_effects=True),
    )(own)
    return out.reshape(-1, own.shape[-1])


def scatter_kernel(bits, parts, shares, out, held, near_in, came, load_sem, send_sem, recv_sem):
    count = len(bits)
    partners = [partner_of(bit) for bit in bits]
    near = count - 1
    meet(partners)

    def codes(free):
        out = [()]
        for i in range(near):
            out = [code + (bit,) for code in out for bit in ((0, 1) if i in free else (0,))]
        return out

    def add(target, left, right):
        rows = target.shape[0]

        @pl.loop(0, rows // 32)
        def _(i):
            at = pl.ds(pl.multiple_of(i * 32, 32), 32)
            total = left[at, :].astype(jnp.float32) + right[at, :].astype(jnp.float32)
            target[at, :] = total.astype(target.dtype)

    pending = [None] * len(parts)
    loads = [None] * len(parts)
    for p, (start, width, order) in enumerate(parts):
        columns = pl.ds(start, width)
        every = list(range(near))
        pending[p] = pltpu.make_async_remote_copy(
            src_ref=shares.at[within(every, count, near, 1, columns)],
            dst_ref=near_in[p],
            send_sem=send_sem.at[p, 0],
            recv_sem=recv_sem.at[p, 0],
            device_id=partners[near],
            device_id_type=MESH,
        )
        pending[p].start()
        loads[p] = pltpu.make_async_copy(
            shares.at[within(every, count, near, 0, columns)], held[p], load_sem.at[p]
        )
        loads[p].start()
    for step in range(near):
        for p, (start, width, order) in enumerate(parts):
            turns = order[:-1][::-1]
            bit = turns[step]
            free = turns[step:]
            left = turns[step + 1 :]
            if step == 0:
                loads[p].wait()
            pending[p].wait()
            arrived = near_in[p] if step == 0 else came[p][step - 1]

            def merge(code):
                other = code if step == 0 else tuple(code[i] for i in sorted(free))
                add(held[p].at[code], held[p].at[code], arrived.at[other])

            for code in codes(free):
                if code[bit] == 1:
                    merge(code)
            lead = tuple(pl.ds(0, 2) if i in left else int(i == bit) for i in range(near))
            pending[p] = pltpu.make_async_remote_copy(
                src_ref=held[p].at[lead],
                dst_ref=came[p][step],
                send_sem=send_sem.at[p, step + 1],
                recv_sem=recv_sem.at[p, step + 1],
                device_id=partners[bit],
                device_id_type=MESH,
            )
            pending[p].start()
            for code in codes(free):
                if code[bit] == 0:
                    merge(code)
    for p, (start, width, order) in enumerate(parts):
        pending[p].wait()
        mine = (0,) * near
        out[:, pl.ds(start, width)] = held[p][mine].astype(jnp.float32) + came[p][near - 1][
            ...
        ].astype(jnp.float32)


def scatter_states(shares):
    bits = code_bits()
    parts = exchange_parts(bits)
    count = len(bits)
    low = jnp.bfloat16
    held = [pltpu.VMEM((2,) * (count - 1) + (TGT_LEN, width), low) for _, width, _ in parts]
    came = [
        [
            pltpu.VMEM((2,) * (count - 2 - step) + (TGT_LEN, width), low)
            for step in range(count - 1)
        ]
        for _, width, _ in parts
    ]
    return pl.pallas_call(
        functools.partial(scatter_kernel, bits, parts),
        out_shape=jax.ShapeDtypeStruct((TGT_LEN, D), jnp.float32),
        in_specs=[pl.BlockSpec(memory_space=pl.ANY)],
        out_specs=pl.BlockSpec(memory_space=pltpu.VMEM),
        scratch_shapes=[
            held,
            held,
            came,
            pltpu.SemaphoreType.DMA((len(parts),)),
            pltpu.SemaphoreType.DMA((len(parts), count)),
            pltpu.SemaphoreType.DMA((len(parts), count)),
        ],
        compiler_params=pltpu.CompilerParams(
            collective_id=3, has_side_effects=True, vmem_limit_bytes=56 << 20
        ),
    )(shares.reshape((2,) * count + (TGT_LEN, D)))


def merge_kernel(bits, stats, out, came, sent, send_sem, recv_sem):
    partners = [partner_of(bit) for bit in bits]
    meet(partners)
    count = len(bits)
    size = 1 << count
    out[...] = stats[...]
    position = lax.broadcasted_iota(jnp.int32, (size, TGT_LEN), 0)
    for step in range(count):
        mask = 1 << (count - 1 - step)
        sent[step] = out[...]
        copy = pltpu.make_async_remote_copy(
            src_ref=sent.at[step],
            dst_ref=came.at[step],
            send_sem=send_sem.at[step],
            recv_sem=recv_sem.at[step],
            device_id=partners[step],
            device_id_type=MESH,
        )
        copy.start()
        copy.wait()
        lower = (position // mask) % 2 == 0
        other = [
            jnp.where(
                lower,
                pltpu.roll(came[step, i], size - mask, 0),
                pltpu.roll(came[step, i], mask, 0),
            )
            for i in range(3)
        ]
        top = jnp.maximum(out[0], other[0])
        out[1] = out[1] * jnp.exp(out[0] - top) + other[1] * jnp.exp(other[0] - top)
        out[0] = top
        out[2] = out[2] + other[2]


def merge_stats(stats):
    bits = code_bits()
    shape = stats.shape
    return pl.pallas_call(
        functools.partial(merge_kernel, bits),
        out_shape=jax.ShapeDtypeStruct(shape, jnp.float32),
        in_specs=[pl.BlockSpec(memory_space=pltpu.VMEM)],
        out_specs=pl.BlockSpec(memory_space=pltpu.VMEM),
        scratch_shapes=[
            pltpu.VMEM((len(bits),) + shape, jnp.float32),
            pltpu.VMEM((len(bits),) + shape, jnp.float32),
            pltpu.SemaphoreType.DMA((len(bits),)),
            pltpu.SemaphoreType.DMA((len(bits),)),
        ],
        compiler_params=pltpu.CompilerParams(collective_id=4, has_side_effects=True),
    )(stats)


def weights_kernel(slots, groups, shards, vector, fact, fulls, vectors, facts, sems):
    holds, local_sem, send_sem, recv_sem, small_local, small_send, small_recv = sems
    slot, pb = lax.axis_index("slot"), lax.axis_index("pb")
    core, far = xor(pb, 1), xor(pb, 2)
    to_core, to_far = (slot, core), (slot, far)
    across = [(xor(slot, mask), pb) for mask in masks_below(slots)]
    meet([to_core, to_far] + across)

    jobs = []
    for shard, full in zip(shards, fulls):
        if len(shard.shape) == 3:
            for half in range(2):
                lead = pl.ds(half * (shard.shape[0] // 2), shard.shape[0] // 2)
                view = lambda ref, at, size, lead=lead: ref.at[lead, pl.ds(at, size)]
                jobs.append((shard, full, shard.shape[1], shard.shape[1], 0, view))
        elif shard.shape[1] > D:
            for half in range(2):
                lanes = pl.ds(half * (shard.shape[1] // 2), shard.shape[1] // 2)
                view = lambda ref, at, size, lanes=lanes: ref.at[pl.ds(at, size), lanes]
                jobs.append((shard, full, shard.shape[0], shard.shape[0], 0, view))
        else:
            for half in range(2):
                rows = shard.shape[0] // 2
                view = lambda ref, at, size: ref.at[pl.ds(at, size)]
                jobs.append((shard, full, shard.shape[0], rows, half * rows, view))

    def remote(source, target, job, kind, partner):
        return pltpu.make_async_remote_copy(
            src_ref=source,
            dst_ref=target,
            send_sem=send_sem.at[job, kind],
            recv_sem=recv_sem.at[job, kind],
            device_id=partner,
            device_id_type=MESH,
        )

    def describe(job):
        shard, full, block, rows, base, view = jobs[job]
        turn = job % 2
        first, second = (slot // (1 << turn)) % 2, (slot // (2 >> turn)) % 2
        to_first, to_second = across[turn], across[1 - turn]
        quarter, half = 3 * rows // 16, rows // 8
        split = base + 3 * rows // 4
        mine = pl.multiple_of(base + (second * 2 + first) * quarter, 16)
        pair = pl.multiple_of(base + second * 2 * quarter, 16)
        side = pl.multiple_of(split + second * half, 16)

        def there(owner, at):
            return pl.multiple_of(owner * block + at, 16)

        def send(kind, partner, owner, at, size, source=None):
            target = view(full, there(owner, at), size)
            return remote(target if source is None else source, target, job, kind, partner)

        own = view(shard, base, rows)
        stages = [
            [
                send(0, to_far, pb, mine, quarter, view(shard, mine, quarter)),
                send(1, to_far, pb, side, half, view(shard, side, half)),
                send(2, to_core, pb, base, rows, own),
            ],
            [
                send(3, to_first, far, mine, quarter),
                send(4, to_second, far, side, half),
            ],
            [send(5, to_second, far, pair, 2 * quarter)],
            [send(6, to_core, far, base, rows)],
        ]
        held = holds[job]
        into = pltpu.make_async_copy(own, held, local_sem.at[job, 0])
        onto = pltpu.make_async_copy(held, view(full, there(pb, base), rows), local_sem.at[job, 1])
        return stages, (into, onto)

    bits = [("pb", mask) for mask in masks_below(groups)] + [
        ("slot", mask) for mask in masks_below(slots)
    ]

    def small_copy(kind, source, target, partner):
        return pltpu.make_async_remote_copy(
            src_ref=source,
            dst_ref=target,
            send_sem=small_send.at[kind],
            recv_sem=small_recv.at[kind],
            device_id=partner,
            device_id_type=MESH,
        )

    def fact_copy(step):
        name, mask = bits[step]
        partner = (slot, xor(pb, mask)) if name == "pb" else (xor(slot, mask), pb)
        count = 1 << step
        source = fact if step == 0 else facts.at[pl.ds(0, count)]
        return small_copy(step, source, facts.at[pl.ds(count, count)], partner)

    near = len(bits)
    vector_copies = [
        small_copy(near, vector, vectors.at[pb], to_core),
        small_copy(near + 1, vector, vectors.at[pb], to_far),
    ]
    vector_last = small_copy(near + 2, vectors.at[far], vectors.at[far], to_core)
    small_own = [
        pltpu.make_async_copy(fact.at[0], facts.at[0], small_local.at[0]),
        pltpu.make_async_copy(vector, vectors.at[pb], small_local.at[1]),
    ]
    for copy in small_own + vector_copies:
        copy.start()
    plans = [describe(job) for job in range(len(jobs))]
    for step in range(max(len(jobs) + 4, len(bits) + 1)):
        for stage in range(5):
            job = step - stage
            if not 0 <= job < len(jobs):
                continue
            stages, (into, onto) = plans[job]
            if stage == 0:
                into.start()
            else:
                for copy in stages[stage - 1]:
                    copy.wait()
            if stage < 4:
                for copy in stages[stage]:
                    copy.start()
                if stage == 1:
                    into.wait()
                    onto.start()
            else:
                onto.wait()
        if step == 0:
            for copy in small_own:
                copy.wait()
        if step == 1:
            for copy in vector_copies:
                copy.wait()
            vector_last.start()
        if step == 2:
            vector_last.wait()
        if 0 < step <= len(bits):
            fact_copy(step - 1).wait()
        if step < len(bits):
            fact_copy(step).start()


def gather_weights(shards, vector, fact):
    slots, groups = lax.axis_size("slot"), lax.axis_size("pb")
    bits = (slots * groups).bit_length() - 1

    def widened(shard):
        axis = 1 if shard.ndim == 3 else 0
        shape = list(shard.shape)
        shape[axis] *= groups
        return jax.ShapeDtypeStruct(tuple(shape), shard.dtype)

    used = len(shards)

    def kernel(*refs):
        ins, outs, sems = refs[: used + 2], refs[used + 2 : 2 * used + 4], refs[2 * used + 4 :]
        weights_kernel(
            slots, groups, ins[:used], ins[used], ins[used + 1], outs[:used], outs[used],
            outs[used + 1], sems,
        )

    jobs = 2 * used
    holds = []
    for shard in shards:
        axis = 1 if shard.ndim == 2 and shard.shape[1] > D else 0
        shape = list(shard.shape)
        shape[axis] //= 2
        holds += [pltpu.VMEM(tuple(shape), shard.dtype)] * 2
    return pl.pallas_call(
        kernel,
        out_shape=[widened(shard) for shard in shards]
        + [
            jax.ShapeDtypeStruct((groups,) + vector.shape, vector.dtype),
            jax.ShapeDtypeStruct((slots * groups,) + fact.shape[1:], fact.dtype),
        ],
        in_specs=[pl.BlockSpec(memory_space=pl.ANY)] * (used + 2),
        out_specs=[pl.BlockSpec(memory_space=pl.ANY)] * (used + 2),
        scratch_shapes=[
            holds,
            pltpu.SemaphoreType.DMA((jobs, 2)),
            pltpu.SemaphoreType.DMA((jobs, 7)),
            pltpu.SemaphoreType.DMA((jobs, 7)),
            pltpu.SemaphoreType.DMA((2,)),
            pltpu.SemaphoreType.DMA((bits + 3,)),
            pltpu.SemaphoreType.DMA((bits + 3,)),
        ],
        compiler_params=pltpu.CompilerParams(
            collective_id=5, has_side_effects=True, vmem_limit_bytes=32 << 20
        ),
    )(*shards, vector, fact)


def own_facts(targets, owner, doc_scores):
    serving = jnp.arange(targets.shape[1]) == owner[0, 0]
    own = jnp.sum(jnp.where(serving[:, None], targets[0], 0), axis=0)
    half = (TGT_LEN // 2,)
    facts = [
        own.astype(jnp.float32),
        jnp.broadcast_to(owner[0, 0].astype(jnp.float32), half),
        jnp.broadcast_to(doc_scores[0, 0], half),
    ]
    return jnp.pad(jnp.concatenate(facts).reshape(1, 2, TGT_LEN), ((0, 0), (0, 6), (0, 0)))


def logit_kernel(states, embed, facts, logits_out, stats):
    logits = matmul_nt(states[...], embed[...])
    logits_out[...] = logits
    target = facts[...].T[:, 0:1]
    entry = lax.broadcasted_iota(jnp.int32, logits.shape, 1).astype(jnp.float32)
    top = jnp.max(logits, axis=1, keepdims=True)
    total = jnp.sum(jnp.exp(logits - top), axis=1, keepdims=True)
    pick = jnp.sum(jnp.where(entry == target, logits, 0.0), axis=1, keepdims=True)
    lane = lax.broadcasted_iota(jnp.int32, (logits.shape[0], 128), 1)
    stats[...] = jnp.where(lane == 0, top, jnp.where(lane == 1, total, pick)).T[:8]


def delta_kernel(logits, embed, facts, delta_out, grad_state):
    columns = facts[...].T
    target, weight, log_total = columns[:, 0:1], columns[:, 1:2], columns[:, 2:3]
    entry = lax.broadcasted_iota(jnp.int32, logits.shape, 1).astype(jnp.float32)
    onehot = jnp.where(entry == target, 1.0, 0.0)
    delta = to_low(weight * (onehot - jnp.exp(logits[...] - log_total)))
    delta_out[...] = delta
    grad_state[...] = to_low(matmul(delta, embed[...]))


def token_tiles(kernel, left, embed, facts, outs):
    tokens, tile = left.shape[0], 512
    tall = lambda width: pl.BlockSpec((tile, width), lambda i: (i, 0))
    wide = pl.BlockSpec((8, tile), lambda i: (0, i))
    return pl.pallas_call(
        kernel,
        grid=(tokens // tile,),
        out_shape=outs,
        in_specs=[tall(left.shape[1]), pl.BlockSpec(embed.shape, lambda i: (0, 0)), wide],
        out_specs=[wide if out.shape[0] == 8 else tall(out.shape[1]) for out in outs],
        compiler_params=pltpu.CompilerParams(vmem_limit_bytes=48 << 20),
    )(left, embed, facts)


def vocabulary_head(state_low, facts, questions, embed):
    slots, groups = lax.axis_size("slot"), lax.axis_size("pb")
    me = lax.axis_index("slot") * groups + lax.axis_index("pb")
    entries = embed.shape[0]
    tokens = slots * groups * TGT_LEN
    target_ids = (facts[:, 0] - (me * entries).astype(jnp.float32)).reshape(1, tokens)
    owners = facts[:, 1, 0].astype(jnp.int32).reshape(slots, groups)
    scores = facts[:, 1, TGT_LEN // 2].reshape(slots, groups)
    states = gather_states(state_low)
    logits, stats = token_tiles(
        logit_kernel,
        states,
        embed,
        jnp.pad(target_ids, ((0, 7), (0, 0))),
        [
            jax.ShapeDtypeStruct((tokens, entries), jnp.float32),
            jax.ShapeDtypeStruct((8, tokens), jnp.float32),
        ],
    )
    merged = merge_stats(stats[:3].reshape(3, -1, TGT_LEN))
    log_total = (merged[0] + jnp.log(merged[1])).reshape(tokens)
    picked = merged[2].reshape(slots, groups, TGT_LEN) - log_total.reshape(slots, groups, TGT_LEN)
    serving = owners[:, :, None] == jnp.arange(questions)
    score_terms = jnp.where(serving, scores[:, :, None], BIG_NEGATIVE)
    token_terms = jnp.where(
        serving[..., None], (scores[:, :, None] + picked)[:, :, None, :], BIG_NEGATIVE
    )
    score_top, token_top = jnp.max(score_terms, axis=0), jnp.max(token_terms, axis=0)
    score_norm = score_top + jnp.log(jnp.sum(jnp.exp(score_terms - score_top), axis=0))
    token_mix = token_top + jnp.log(jnp.sum(jnp.exp(token_terms - token_top), axis=0))
    group_tokens = questions * TGT_LEN
    count = groups * group_tokens
    losses = -jnp.sum(token_mix - score_norm[:, :, None], axis=(1, 2)) / group_tokens
    own_mix = jnp.sum(jnp.where(serving[..., None], token_mix[None], 0.0), axis=2)
    own_norm = jnp.sum(jnp.where(serving, score_norm[None], 0.0), axis=2)
    posterior = jnp.exp(scores[:, :, None] + picked - own_mix)
    prior = jnp.exp(scores - own_norm)
    token_grad = (-posterior / count).reshape(1, tokens)
    score_grads = -jnp.sum(posterior - prior[:, :, None], axis=2) / count
    known = jnp.concatenate([target_ids, token_grad, log_total.reshape(1, tokens)])
    delta, share = token_tiles(
        delta_kernel,
        logits,
        embed,
        jnp.pad(known, ((0, 5), (0, 0))),
        [
            jax.ShapeDtypeStruct((tokens, entries), jnp.bfloat16),
            jax.ShapeDtypeStruct((tokens, D), jnp.bfloat16),
        ],
    )
    grad_state = scatter_states(share)
    return (losses[:1], score_grads[:1, :1], grad_state, delta, states)


def local(
    enc_input,
    dec_input,
    doc_scores,
    owner,
    targets,
    enc_attn,
    enc_up,
    enc_down,
    enc_up_bias,
    enc_bias,
    enc_gain,
    dec_self,
    dec_cross,
    dec_up,
    dec_down,
    dec_up_bias,
    dec_bias,
    dec_gain,
    embed,
):
    pb_size = lax.axis_size("pb")
    width = D // pb_size
    vectors = (enc_up_bias, enc_bias, enc_gain, dec_up_bias, dec_bias, dec_gain)
    rows = [v.size // width for v in vectors]
    starts = [sum(rows[:i]) for i in range(len(rows) + 1)]
    passage_low = enc_input[0, 0]
    passage = passage_low.astype(jnp.float32)
    question_low = dec_input[0, 0]
    question = question_low.astype(jnp.float32)

    own_vectors = jnp.concatenate([v.reshape(-1, width) for v in vectors])
    (
        encoder_attn,
        encoder_up,
        encoder_down,
        decoder_self,
        decoder_cross,
        decoder_down,
        packed,
        facts,
    ) = gather_weights(
        (enc_attn, enc_up, enc_down, dec_self, dec_cross, dec_down),
        jnp.pad(own_vectors, ((0, -starts[-1] % 32), (0, 0))),
        own_facts(targets, owner, doc_scores),
    )
    packed, dec_up = lax.optimization_barrier((packed, dec_up))
    decoder_up = lax.all_gather(dec_up, "pb", axis=0, tiled=True)
    packed = packed.astype(jnp.float32)
    unpacked = [packed[:, starts[i] : starts[i + 1], :] for i in range(len(rows))]
    encoder_upbias = unpacked[0].reshape(-1)
    encoder_bias = unpacked[1].transpose(1, 0, 2).reshape(-1, D)
    encoder_gain = unpacked[2].transpose(1, 0, 2).reshape(-1, D)
    decoder_upbias = unpacked[3].reshape(-1)
    decoder_bias = unpacked[4].transpose(1, 0, 2).reshape(-1, D)
    decoder_gain = unpacked[5].transpose(1, 0, 2).reshape(-1, D)
    attn_out, enc_saved = attend_forward(
        passage_low,
        passage_low,
        encoder_attn,
        encoder_bias[0],
        encoder_bias[1],
        encoder_bias[2],
        False,
    )
    enc_first, enc_norm_one = norm_forward(passage + attn_out, encoder_gain[0], encoder_bias[3])
    enc_first_low = to_low(enc_first)
    enc_hidden, enc_slope = gelu_with_slope(matmul(enc_first_low, encoder_up) + encoder_upbias)
    enc_hidden_low = to_low(enc_hidden)
    ffn_out = matmul(enc_hidden_low, encoder_down) + encoder_bias[4]
    encoded, enc_norm_two = norm_forward(enc_first + ffn_out, encoder_gain[1], encoder_bias[5])
    memory_low = to_low(encoded)
    self_out, self_saved = attend_forward(
        question_low,
        question_low,
        decoder_self,
        decoder_bias[0],
        decoder_bias[1],
        decoder_bias[2],
        True,
    )
    dec_first, dec_norm_one = norm_forward(question + self_out, decoder_gain[0], decoder_bias[3])
    dec_first_low = to_low(dec_first)
    cross_out, cross_saved = attend_forward(
        dec_first_low,
        memory_low,
        decoder_cross,
        decoder_bias[4],
        decoder_bias[5],
        decoder_bias[6],
        False,
    )
    dec_second, dec_norm_two = norm_forward(dec_first + cross_out, decoder_gain[1], decoder_bias[7])
    dec_second_low = to_low(dec_second)
    dec_hidden, dec_slope = gelu_with_slope(matmul(dec_second_low, decoder_up) + decoder_upbias)
    dec_hidden_low = to_low(dec_hidden)
    dec_ffn_out = matmul(dec_hidden_low, decoder_down) + decoder_bias[8]
    state, dec_norm_three = norm_forward(dec_second + dec_ffn_out, decoder_gain[2], decoder_bias[9])
    state_low = to_low(state)

    loss, score_grad, grad_state_sum, delta, states = vocabulary_head(
        state_low, facts, targets.shape[1], embed
    )

    grad_third, gain_third, shift_third = norm_backward(
        grad_state_sum, dec_norm_three, decoder_gain[2]
    )
    dec_downbias_grad = jnp.sum(grad_third, axis=0)
    third_low = to_low(grad_third)
    grad_before = matmul_nt(third_low, decoder_down) * dec_slope
    dec_upbias_grad = jnp.sum(grad_before, axis=0)
    before_low = to_low(grad_before)
    grad_second, gain_second, shift_second = norm_backward(
        grad_third + matmul_nt(before_low, decoder_up), dec_norm_two, decoder_gain[1]
    )
    cross_query, grad_memory, dec_cross_pairs, cross_biases = attend_backward(
        grad_second, dec_first_low, memory_low, decoder_cross, cross_saved, False
    )
    grad_first, gain_first, shift_first = norm_backward(
        grad_second + cross_query, dec_norm_one, decoder_gain[0]
    )
    self_query, self_memory, dec_self_pairs, self_biases = attend_backward(
        grad_first, question_low, question_low, decoder_self, self_saved, True
    )
    question_grad = grad_first + self_query + self_memory
    enc_grad_two, enc_gain_two, enc_shift_two = norm_backward(
        grad_memory, enc_norm_two, encoder_gain[1]
    )
    enc_downbias_grad = jnp.sum(enc_grad_two, axis=0)
    enc_two_low = to_low(enc_grad_two)
    enc_grad_before = matmul_nt(enc_two_low, encoder_down) * enc_slope
    enc_upbias_grad = jnp.sum(enc_grad_before, axis=0)
    enc_before_low = to_low(enc_grad_before)
    enc_grad_one, enc_gain_one, enc_shift_one = norm_backward(
        enc_grad_two + matmul_nt(enc_before_low, encoder_up), enc_norm_one, encoder_gain[0]
    )
    enc_query, enc_memory, enc_attn_pairs, enc_biases = attend_backward(
        enc_grad_one, passage_low, passage_low, encoder_attn, enc_saved, False
    )
    passage_grad = enc_grad_one + enc_query + enc_memory
    operands, plan = [], []

    def share(left, right, tall=False):
        where = []
        for operand in (left, right):
            known = [i for i, other in enumerate(operands) if other is operand]
            where.append(known[0] if known else len(operands))
            if not known:
                operands.append(operand)
        for i in range(left.shape[1] * right.shape[1] // (D * D)):
            plan.append((where[0], where[1], i, tall))

    for left, right in enc_attn_pairs:
        share(left, right)
    share(enc_first_low, enc_before_low)
    share(enc_hidden_low, enc_two_low, tall=True)
    for left, right in dec_self_pairs + dec_cross_pairs:
        share(left, right)
    share(dec_second_low, before_low)
    share(dec_hidden_low, third_low, tall=True)
    enc_bias_grad = jnp.stack(
        [
            enc_biases[0],
            enc_biases[1],
            enc_biases[2],
            enc_shift_one,
            enc_downbias_grad,
            enc_shift_two,
        ]
    )
    enc_gain_grad = jnp.stack([enc_gain_one, enc_gain_two])
    dec_bias_grad = jnp.stack(
        [
            self_biases[0],
            self_biases[1],
            self_biases[2],
            shift_first,
            cross_biases[0],
            cross_biases[1],
            cross_biases[2],
            shift_second,
            dec_downbias_grad,
            shift_third,
        ]
    )
    dec_gain_grad = jnp.stack([gain_first, gain_second, gain_third])
    vector_grads = jnp.concatenate(
        [
            enc_upbias_grad.reshape(pb_size, -1, width),
            enc_bias_grad.reshape(-1, pb_size, width).transpose(1, 0, 2),
            enc_gain_grad.reshape(-1, pb_size, width).transpose(1, 0, 2),
            dec_upbias_grad.reshape(pb_size, -1, width),
            dec_bias_grad.reshape(-1, pb_size, width).transpose(1, 0, 2),
            dec_gain_grad.reshape(-1, pb_size, width).transpose(1, 0, 2),
        ],
        axis=1,
    )
    spare = -starts[-1] % 32
    small = jnp.pad(vector_grads, ((0, 0), (0, spare), (0, 0))).reshape(pb_size, -1, D)
    if lax.axis_size("slot") * 16 <= UNIT:
        summed_parts, small_sum, embed_grad = sync_gradients(
            plan, operands, small, (delta, states)
        )
    else:
        embed_grad = matmul_tn(delta, states)
        summed_parts, small_sum = sync_gradients(plan, operands, small)
    units = summed_parts.reshape(-1, width, D)
    square = lambda at: units[at : at + 4].astype(jnp.float32)
    wide = lambda at: jnp.concatenate([units[at + i].astype(jnp.float32) for i in range(4)], axis=1)
    tall = lambda at: square(at).reshape(-1, D)
    vector_sum = small_sum.reshape(-1, width)
    vector_out = [
        vector_sum[starts[i] : starts[i + 1]].reshape(v.shape) for i, v in enumerate(vectors)
    ]
    summed = (
        (square(0), wide(4), tall(8))
        + tuple(vector_out[:3])
        + (square(12), square(16), wide(20), tall(24))
        + tuple(vector_out[3:])
    )
    return (
        (
            loss,
            passage_grad.reshape(1, 1, SRC_LEN, D),
            question_grad.reshape(1, 1, TGT_LEN, D),
            score_grad,
        )
        + tuple(summed)
        + (embed_grad,)
    )


def solution(mesh):
    placed = (
        P("pb", "slot", None, None),
        P("pb", "slot", None, None),
        P("pb", "slot"),
        P("pb", "slot"),
        P("pb", None, None),
        P(None, "pb", None),
        P("pb", None),
        P("pb", None),
        P("pb"),
        P(None, "pb"),
        P(None, "pb"),
        P(None, "pb", None),
        P(None, "pb", None),
        P("pb", None),
        P("pb", None),
        P("pb"),
        P(None, "pb"),
        P(None, "pb"),
        P(("slot", "pb"), None),
    )
    return jax.shard_map(
        local,
        mesh=mesh,
        in_specs=placed,
        out_specs=(
            P("pb"),
            P("pb", "slot", None, None),
            P("pb", "slot", None, None),
            P("pb", "slot"),
            P(None, "pb", None),
            P("pb", None),
            P("pb", None),
            P("pb"),
            P(None, "pb"),
            P(None, "pb"),
            P(None, "pb", None),
            P(None, "pb", None),
            P("pb", None),
            P("pb", None),
            P("pb"),
            P(None, "pb"),
            P(None, "pb"),
            P(("slot", "pb"), None),
        ),
        check_vma=False,
    )
```

```python
import functools
import math

import jax
import jax.numpy as jnp
from jax import lax
from jax.experimental import pallas as pl
from jax.experimental.pallas import tpu as pltpu
from jax.sharding import PartitionSpec as P

D = 1024
HEADS = 16
HEAD_DIM = 64
SRC_LEN = 384
TGT_LEN = 128
MESH = pl.DeviceIdType.MESH
UNIT = 256
RING = 8
SIDE_STEPS = 16


BIG_NEGATIVE = -1e30
MASK_FILL = -1000000000.0


def matmul(left, right):
    return jnp.dot(left, right, preferred_element_type=jnp.float32)


def matmul_nt(left, right):
    return lax.dot_general(
        left, right, (((1,), (1,)), ((), ())), preferred_element_type=jnp.float32
    )


def matmul_tn(left, right):
    return lax.dot_general(
        left, right, (((0,), (0,)), ((), ())), preferred_element_type=jnp.float32
    )


def to_low(value):
    return value.astype(jnp.bfloat16)


def norm_forward(total, gain, shift):
    centered = total - jnp.mean(total, axis=-1, keepdims=True)
    inverse = lax.rsqrt(jnp.mean(centered * centered, axis=-1, keepdims=True) + 1e-05)
    normed = centered * inverse
    return (normed * gain + shift, (normed, inverse))


def norm_backward(upstream, saved, gain):
    normed, inverse = saved
    scaled = upstream * gain
    inner = (
        scaled
        - jnp.mean(scaled, axis=-1, keepdims=True)
        - normed * jnp.mean(scaled * normed, axis=-1, keepdims=True)
    )
    return (inverse * inner, jnp.sum(upstream * normed, axis=0), jnp.sum(upstream, axis=0))


def head_mask(which):
    return lax.broadcasted_iota(jnp.int32, (1, 2 * HEAD_DIM), 1) // HEAD_DIM == which


def only_head(pair, which):
    return jnp.where(head_mask(which), pair.astype(jnp.float32), 0.0).astype(pair.dtype)


def both_heads(first, second):
    return jnp.where(head_mask(0), first, second)


def attention_weights(queries, keys, causal):
    scores = matmul_nt(queries, keys) * HEAD_DIM ** (-0.5)
    if causal:
        rows = lax.broadcasted_iota(jnp.int32, scores.shape, 0)
        columns = lax.broadcasted_iota(jnp.int32, scores.shape, 1)
        scores = jnp.where(rows >= columns, scores, MASK_FILL)
    shifted = jnp.exp(scores - jnp.max(scores, axis=-1, keepdims=True))
    return shifted / jnp.sum(shifted, axis=-1, keepdims=True)


def attend_kernel(causal, queries, keys, values, out):
    parts = []
    for which in range(2):
        probs = attention_weights(only_head(queries[...], which), keys[...], causal)
        parts.append(matmul(to_low(probs), values[...]))
    out[...] = to_low(both_heads(*parts))


def attend_grad_kernel(
    causal, queries, keys, values, upstream, grad_q, grad_k, grad_v, sum_q, sum_v
):
    parts = []
    for which in range(2):
        probs = attention_weights(only_head(queries[...], which), keys[...], causal)
        grad_probs = matmul_nt(only_head(upstream[...], which), values[...])
        inner = jnp.sum(grad_probs * probs, axis=-1, keepdims=True)
        grad_scores = to_low(probs * (grad_probs - inner))
        parts.append(
            (
                matmul(grad_scores, keys[...]),
                matmul_tn(grad_scores, queries[...]),
                matmul_tn(to_low(probs), upstream[...]),
            )
        )
    scale = HEAD_DIM ** (-0.5)
    query, key, value = [both_heads(*pair) for pair in zip(*parts)]
    query = query * scale
    grad_q[...] = to_low(query)
    grad_k[...] = to_low(key * scale)
    grad_v[...] = to_low(value)
    sum_q[...] = jnp.broadcast_to(jnp.sum(query, axis=0, keepdims=True), sum_q.shape)
    sum_v[...] = jnp.broadcast_to(jnp.sum(value, axis=0, keepdims=True), sum_v.shape)


def head_pairs(rows):
    return pl.BlockSpec((rows, 2 * HEAD_DIM), lambda pair: (0, pair))


def attention_cost(rows, columns, products):
    return pl.CostEstimate(
        flops=2 * products * rows * columns * D,
        bytes_accessed=4 * (rows + columns) * D * products,
        transcendentals=HEADS * rows * columns,
    )


def attend_forward(query_low, memory_low, matrices, bias_query, bias_value, bias_out, causal):
    rows, columns = query_low.shape[0], memory_low.shape[0]
    queries = to_low(matmul(query_low, matrices[0]) + bias_query)
    keys = to_low(matmul(memory_low, matrices[1]))
    values = to_low(matmul(memory_low, matrices[2]) + bias_value)
    context = pl.pallas_call(
        functools.partial(attend_kernel, causal),
        grid=(HEADS // 2,),
        out_shape=jax.ShapeDtypeStruct((rows, D), jnp.bfloat16),
        in_specs=[head_pairs(rows), head_pairs(columns), head_pairs(columns)],
        out_specs=head_pairs(rows),
        cost_estimate=attention_cost(rows, columns, 2),
        compiler_params=pltpu.CompilerParams(vmem_limit_bytes=24 << 20),
    )(queries, keys, values)
    output = matmul(context, matrices[3]) + bias_out
    return (output, (queries, keys, values, context))


def attend_backward(upstream, query_low, memory_low, matrices, saved, causal):
    queries, keys, values, context = saved
    rows, columns = query_low.shape[0], memory_low.shape[0]
    upstream_low = to_low(upstream)
    grad_context = to_low(matmul_nt(upstream_low, matrices[3]))
    low, sums = jnp.bfloat16, jax.ShapeDtypeStruct((8, D), jnp.float32)
    queries_low, keys_low, values_low, query_sum, value_sum = pl.pallas_call(
        functools.partial(attend_grad_kernel, causal),
        grid=(HEADS // 2,),
        out_shape=(
            jax.ShapeDtypeStruct((rows, D), low),
            jax.ShapeDtypeStruct((columns, D), low),
            jax.ShapeDtypeStruct((columns, D), low),
            sums,
            sums,
        ),
        in_specs=[head_pairs(n) for n in (rows, columns, columns, rows)],
        out_specs=tuple(head_pairs(n) for n in (rows, columns, columns, 8, 8)),
        cost_estimate=attention_cost(rows, columns, 5),
        compiler_params=pltpu.CompilerParams(vmem_limit_bytes=24 << 20),
    )(queries, keys, values, grad_context)
    grad_query_input = matmul_nt(queries_low, matrices[0])
    grad_memory_input = matmul_nt(keys_low, matrices[1]) + matmul_nt(values_low, matrices[2])
    grad_pairs = [
        (query_low, queries_low),
        (memory_low, keys_low),
        (memory_low, values_low),
        (context, upstream_low),
    ]
    bias_grads = (query_sum[0], value_sum[0], jnp.sum(upstream, axis=0))
    return (grad_query_input, grad_memory_input, grad_pairs, bias_grads)


def gelu_with_slope(value):
    share = 0.5 * (1.0 + lax.erf(value * 0.5**0.5))
    density = jnp.exp(-0.5 * value * value) * (2.0 * math.pi) ** -0.5
    return value * share, share + value * density


def masks_below(size):
    return [1 << i for i in range(size.bit_length() - 1)]


def xor(value, mask):
    return jnp.where((value // mask) % 2 == 0, value + mask, value - mask)


def sync_kernel(slots, count, plan, operands, small, side, out, small_out, side_out, scratch):
    left_buffer, right_buffer, parts, core_in, far_out, far_keep, far_in = scratch[:7]
    half_out, half_keep, half_in, full = scratch[7:11]
    small_core, small_far, small_in, small_out_far, small_out_slot = scratch[11:16]
    load_sem, store_sem, send_sem, recv_sem, small_send, small_recv = scratch[16:22]
    if side:
        side_left, side_right, side_total, side_sem, side_store = scratch[22:]
    masks = masks_below(slots)
    levels = len(masks)
    rows = full.shape[1]
    slot, pb = lax.axis_index("slot"), lax.axis_index("pb")
    core, far = xor(pb, 1), xor(pb, 2)
    far_core = xor(core, 2)
    partners = [(slot, core), (slot, far)] + [(xor(slot, mask), pb) for mask in masks]
    bits = [(slot // mask) % 2 for mask in masks]

    barrier = pltpu.get_barrier_semaphore()
    for partner in partners:
        pl.semaphore_signal(barrier, inc=1, device_id=partner, device_id_type=MESH)
    pl.semaphore_wait(barrier, len(partners))

    def remote(source, target, stage, at, partner):
        return pltpu.make_async_remote_copy(
            src_ref=source,
            dst_ref=target,
            send_sem=send_sem.at[stage, at],
            recv_sem=recv_sem.at[stage, at],
            device_id=partner,
            device_id_type=MESH,
        )

    def core_copies(c):
        at = lax.rem(c, RING)
        ring = lax.rem(c, 4)
        pair = lax.rem(c, 2)
        return (
            remote(parts.at[pair, core], core_in.at[ring, 0], 0, at, partners[0]),
            remote(parts.at[pair, far_core], core_in.at[ring, 1], 1, at, partners[0]),
        )

    def load(unit):
        pair = lax.rem(unit, 2)
        for at, (left, right, k, tall) in enumerate(plan):

            @pl.when(unit == at)
            def _():
                tokens = operands[left].shape[0]
                rows_at = pl.ds(0, tokens)
                if tall:
                    for p in range(4):
                        pltpu.make_async_copy(
                            operands[left].at[:, pl.ds((4 * p + k) * UNIT, UNIT)],
                            left_buffer.at[pair, rows_at, pl.ds(p * UNIT, UNIT)],
                            load_sem.at[0, pair],
                        ).start()
                else:
                    pltpu.make_async_copy(
                        operands[left], left_buffer.at[pair, rows_at], load_sem.at[0, pair]
                    ).start()
                column = 0 if tall else k * D
                pltpu.make_async_copy(
                    operands[right].at[:, pl.ds(column, D)],
                    right_buffer.at[pair, rows_at],
                    load_sem.at[1, pair],
                ).start()

    def product(unit, chunk, offset):
        pair = lax.rem(unit, 2)
        lengths = [operands[left].shape[0] for left, _, _, _ in plan]
        for tokens in sorted(set(lengths)):
            among = functools.reduce(
                jnp.logical_or, [unit == at for at, n in enumerate(lengths) if n == tokens]
            )

            @pl.when(among)
            def _():
                rows_at = pl.ds(0, tokens)
                for i, buffer in enumerate((left_buffer, right_buffer)):
                    whole = buffer.at[pair, rows_at]
                    pltpu.make_async_copy(whole, whole, load_sem.at[i, pair]).wait()

                @pl.loop(0, 4)
                def _(p):
                    columns = pl.ds(pl.multiple_of(p * UNIT, UNIT), UNIT)
                    total = lax.dot_general(
                        left_buffer[pair, rows_at, columns],
                        right_buffer[pair, rows_at, :],
                        (((0,), (0,)), ((), ())),
                        preferred_element_type=jnp.float32,
                    )
                    parts[lax.rem(chunk, 2), p, pl.ds(offset, UNIT), :] = total.astype(
                        parts.dtype
                    )

    def far_copy(c):
        ring = lax.rem(c, 4)
        return remote(far_out.at[ring], far_in.at[ring], 2, lax.rem(c, RING), partners[1])

    def halve_copy(level, c):
        ring = lax.rem(c, 4)
        return remote(
            half_out[level].at[ring],
            half_in[level].at[ring],
            3 + level,
            lax.rem(c, RING),
            partners[2 + level],
        )

    def join_copy(level, c):
        at = lax.rem(c, RING)
        size = rows >> (level + 1)
        offset = sum(bits[i] * (rows >> (i + 1)) for i in range(level + 1))
        where = pl.ds(pl.multiple_of(offset, size), size)
        return remote(
            full.at[at, where], full.at[at, where], 3 + levels + level, at, partners[2 + level]
        )

    def store(c):
        at = lax.rem(c, RING)
        return pltpu.make_async_copy(full.at[at], out.at[c], store_sem.at[at])

    def add(target, left, right, size):
        tile = min(size, 32)

        @pl.loop(0, size // tile)
        def _(i):
            at = pl.ds(pl.multiple_of(i * tile, tile), tile)
            total = left[at, :].astype(jnp.float32) + right[at, :].astype(jnp.float32)
            target[at, :] = total.astype(target.dtype)

    def small_core_copies():
        return [
            pltpu.make_async_remote_copy(
                src_ref=small.at[source],
                dst_ref=small_core.at[i],
                send_sem=small_send.at[i],
                recv_sem=small_recv.at[i],
                device_id=partners[0],
                device_id_type=MESH,
            )
            for i, source in ((0, core), (1, far_core))
        ]

    def small_far_copy():
        return pltpu.make_async_remote_copy(
            src_ref=small_out_far,
            dst_ref=small_far,
            send_sem=small_send.at[2],
            recv_sem=small_recv.at[2],
            device_id=partners[1],
            device_id_type=MESH,
        )

    def small_slot_copy(level):
        return pltpu.make_async_remote_copy(
            src_ref=small_out_slot.at[level],
            dst_ref=small_in.at[level],
            send_sem=small_send.at[3 + level],
            recv_sem=small_recv.at[3 + level],
            device_id=partners[2 + level],
            device_id_type=MESH,
        )

    def small_stage(step):
        if step == 0:
            for copy in small_core_copies():
                copy.start()
        elif step == 1:
            for copy in small_core_copies():
                copy.wait()
            small_out_far[...] = small[far] + small_core[1]
            small_out[...] = small[pb] + small_core[0]
            small_far_copy().start()
        elif step == 2:
            small_far_copy().wait()
            small_out[...] = small_out[...] + small_far[...]
            small_out_slot[0] = small_out[...]
            small_slot_copy(0).start()
        else:
            level = step - 3
            small_slot_copy(level).wait()
            small_out[...] = small_out[...] + small_in[level]
            if level + 1 < levels:
                small_out_slot[level + 1] = small_out[...]
                small_slot_copy(level + 1).start()

    def stage(step, c):
        ring = lax.rem(c, 4)
        pair = lax.rem(c, 2)
        at = lax.rem(c, RING)
        if step == 0:
            for copy in core_copies(c):
                copy.start()
        elif step == 1:
            for copy in core_copies(c):
                copy.wait()
            add(far_out.at[ring], parts.at[pair, far], core_in.at[ring, 1], rows)
            far_copy(c).start()
            add(far_keep.at[ring], parts.at[pair, pb], core_in.at[ring, 0], rows)
        elif step < 2 + levels:
            level = step - 2
            size = rows >> (level + 1)
            if level == 0:
                far_copy(c).wait()
                left, right = far_keep.at[ring], far_in.at[ring]
            else:
                halve_copy(level - 1, c).wait()
                left, right = half_keep[level - 1].at[ring], half_in[level - 1].at[ring]
            mine = pl.ds(pl.multiple_of(bits[level] * size, size), size)
            other = pl.ds(pl.multiple_of((1 - bits[level]) * size, size), size)
            add(half_out[level].at[ring], left.at[other], right.at[other], size)
            halve_copy(level, c).start()
            add(half_keep[level].at[ring], left.at[mine], right.at[mine], size)
        elif step == 2 + levels:
            level = levels - 1
            size = rows >> levels
            halve_copy(level, c).wait()
            offset = sum(bits[i] * (rows >> (i + 1)) for i in range(levels))
            where = pl.ds(pl.multiple_of(offset, size), size)
            add(full.at[at, where], half_keep[level].at[ring], half_in[level].at[ring], size)
            join_copy(level, c).start()
        elif step < 2 + 2 * levels:
            level = levels - 1 - (step - 3 - levels)
            join_copy(level, c).wait()
            join_copy(level - 1, c).start()
        elif step == 2 + 2 * levels:
            join_copy(0, c).wait()
            store(c).start()
        else:
            store(c).wait()

    stages = 4 + 2 * levels

    def side_loads(step):
        pair = lax.rem(step, 2)
        tokens = side_right.shape[1]
        at = pl.ds(pl.multiple_of(step * tokens, tokens), tokens)
        return (
            pltpu.make_async_copy(side[0].at[at], side_left.at[pair], side_sem.at[0, pair]),
            pltpu.make_async_copy(side[1].at[at], side_right.at[pair], side_sem.at[1, pair]),
        )

    def side_product(step):
        pair = lax.rem(step, 2)
        for copy in side_loads(step):
            copy.wait()

        @pl.loop(0, side_total.shape[0] // UNIT)
        def _(i):
            at = pl.ds(pl.multiple_of(i * UNIT, UNIT), UNIT)
            side_total[at, :] += matmul_tn(side_left[pair, :, at], side_right[pair])

    per = rows // UNIT
    load(jnp.int32(0))
    if side:
        side_total[...] = jnp.zeros_like(side_total)
        side_copy = pltpu.make_async_copy(side_total, side_out, side_store)
        for copy in side_loads(jnp.int32(0)):
            copy.start()

    @pl.loop(0, count + stages)
    def _(it):
        for step in range(3 + levels):

            @pl.when(it == step)
            def _():
                small_stage(step)

        for step in range(stages):
            c = it - 1 - step

            @pl.when(jnp.logical_and(c >= 0, c < count))
            def _():
                stage(step, c)

        for i in range(per):

            @pl.when(it < count)
            def _():
                unit = it * per + i
                load(unit + 1)
                product(unit, it, i * UNIT)

        if side:

            @pl.when(it < SIDE_STEPS - 1)
            def _():
                for copy in side_loads(it + 1):
                    copy.start()

            @pl.when(it < SIDE_STEPS)
            def _():
                side_product(it)

            @pl.when(it == SIDE_STEPS)
            def _():
                side_copy.start()

    if side:
        side_copy.wait()


def sync_gradients(plan, operands, small, side=()):
    slots = lax.axis_size("slot")
    rows, columns = max(UNIT, 16 * slots), D
    count = len(plan) * UNIT // rows
    levels = slots.bit_length() - 1
    small_rows = small.shape[1:]
    low = jnp.bfloat16
    longest = max(operand.shape[0] for operand in operands)
    block = lambda *lead: pltpu.VMEM(lead + (columns,), low)
    halves = [block(4, rows >> (i + 1)) for i in range(levels)]
    used, more = len(operands), len(side)
    outs = 3 if side else 2
    shapes = [
        jax.ShapeDtypeStruct((count, rows, columns), low),
        jax.ShapeDtypeStruct(small_rows, jnp.float32),
    ]
    places = [pl.BlockSpec(memory_space=pl.ANY), pl.BlockSpec(memory_space=pltpu.VMEM)]
    side_scratch = []
    if side:
        tokens, entries = side[0].shape
        shapes.append(jax.ShapeDtypeStruct((entries, columns), jnp.float32))
        places.append(pl.BlockSpec(memory_space=pl.ANY))
        side_scratch = [
            pltpu.VMEM((2, tokens // SIDE_STEPS, entries), low),
            pltpu.VMEM((2, tokens // SIDE_STEPS, columns), low),
            pltpu.VMEM((entries, columns), jnp.float32),
            pltpu.SemaphoreType.DMA((2, 2)),
            pltpu.SemaphoreType.DMA,
        ]

    def kernel(*refs):
        ins, results = refs[: used + 1 + more], refs[used + 1 + more :]
        sync_kernel(
            slots,
            count,
            plan,
            ins[:used],
            ins[used],
            ins[used + 1 :],
            results[0],
            results[1],
            results[2] if side else None,
            results[outs:],
        )

    return pl.pallas_call(
        kernel,
        out_shape=shapes,
        in_specs=[pl.BlockSpec(memory_space=pl.ANY)] * used
        + [pl.BlockSpec(memory_space=pltpu.VMEM)]
        + [pl.BlockSpec(memory_space=pl.ANY)] * more,
        out_specs=places,
        scratch_shapes=[
            block(2, longest),
            block(2, longest),
            block(2, 4, rows),
            block(4, 2, rows),
            block(4, rows),
            block(4, rows),
            block(4, rows),
            halves,
            halves,
            halves,
            block(RING, rows),
            pltpu.VMEM((2,) + small_rows, jnp.float32),
            pltpu.VMEM(small_rows, jnp.float32),
            pltpu.VMEM((levels,) + small_rows, jnp.float32),
            pltpu.VMEM(small_rows, jnp.float32),
            pltpu.VMEM((levels,) + small_rows, jnp.float32),
            pltpu.SemaphoreType.DMA((2, 2)),
            pltpu.SemaphoreType.DMA((RING,)),
            pltpu.SemaphoreType.DMA((3 + 2 * levels, RING)),
            pltpu.SemaphoreType.DMA((3 + 2 * levels, RING)),
            pltpu.SemaphoreType.DMA((3 + levels,)),
            pltpu.SemaphoreType.DMA((3 + levels,)),
        ]
        + side_scratch,
        compiler_params=pltpu.CompilerParams(
            collective_id=1, has_side_effects=True, vmem_limit_bytes=56 << 20
        ),
    )(*operands, small, *side)


def code_bits():
    return [("slot", mask) for mask in masks_below(lax.axis_size("slot"))[::-1]] + [
        ("pb", mask) for mask in masks_below(lax.axis_size("pb"))[::-1]
    ]


def exchange_parts(bits):
    slot_bits = [i for i, (name, mask) in enumerate(bits) if name == "slot"]
    pb_bits = [i for i, (name, mask) in enumerate(bits) if name == "pb"]
    high, low, far, near = slot_bits[:-1], slot_bits[-1:], pb_bits[:-1], pb_bits[-1:]
    first, second = high + low + far + near, far + high + low + near
    return [
        (0, 256, first),
        (256, 256, second),
        (512, 256, first),
        (768, 128, second),
        (896, 128, low + far + high + near),
    ]


def partner_of(bit):
    name, mask = bit
    slot, pb = lax.axis_index("slot"), lax.axis_index("pb")
    return (xor(slot, mask), pb) if name == "slot" else (slot, xor(pb, mask))


def meet(partners):
    barrier = pltpu.get_barrier_semaphore()
    for partner in partners:
        pl.semaphore_signal(barrier, inc=1, device_id=partner, device_id_type=MESH)
    pl.semaphore_wait(barrier, len(partners))


def within(held, count, fixed, value, columns):
    lead = [pl.ds(0, 2) if i in held else 0 for i in range(count)]
    if fixed is not None:
        lead[fixed] = value
    return tuple(lead) + (slice(None), columns)


def gather_kernel(bits, parts, own, out, local_sem, send_sem, recv_sem):
    count = len(bits)
    partners = [partner_of(bit) for bit in bits]
    meet(partners)
    local = pltpu.make_async_copy(
        own, out.at[within([], count, None, 0, slice(None))], local_sem
    )
    local.start()
    pending = [None] * len(parts)
    for step in range(count):
        for p, (start, width, order) in enumerate(parts):
            columns = pl.ds(start, width)
            if step > 0:
                pending[p].wait()
            if step == 1 and p == 0:
                local.wait()
            bit = order[step]
            held = order[:step]
            source = (
                own.at[:, columns] if step == 0 else out.at[within(held, count, None, 0, columns)]
            )
            pending[p] = pltpu.make_async_remote_copy(
                src_ref=source,
                dst_ref=out.at[within(held, count, bit, 1, columns)],
                send_sem=send_sem.at[p, step],
                recv_sem=recv_sem.at[p, step],
                device_id=partners[bit],
                device_id_type=MESH,
            )
            pending[p].start()
    for copy in pending:
        copy.wait()


def gather_states(own):
    bits = code_bits()
    parts = exchange_parts(bits)
    out = pl.pallas_call(
        functools.partial(gather_kernel, bits, parts),
        out_shape=jax.ShapeDtypeStruct((2,) * len(bits) + own.shape, own.dtype),
        in_specs=[pl.BlockSpec(memory_space=pl.ANY)],
        out_specs=pl.BlockSpec(memory_space=pl.ANY),
        scratch_shapes=[
            pltpu.SemaphoreType.DMA,
            pltpu.SemaphoreType.DMA((len(parts), len(bits))),
            pltpu.SemaphoreType.DMA((len(parts), len(bits))),
        ],
        compiler_params=pltpu.CompilerParams(collective_id=2, has_side_effects=True),
    )(own)
    return out.reshape(-1, own.shape[-1])


def scatter_kernel(bits, parts, shares, out, held, near_in, came, load_sem, send_sem, recv_sem):
    count = len(bits)
    partners = [partner_of(bit) for bit in bits]
    near = count - 1
    meet(partners)

    def codes(free):
        out = [()]
        for i in range(near):
            out = [code + (bit,) for code in out for bit in ((0, 1) if i in free else (0,))]
        return out

    def add(target, left, right):
        rows = target.shape[0]

        @pl.loop(0, rows // 32)
        def _(i):
            at = pl.ds(pl.multiple_of(i * 32, 32), 32)
            total = left[at, :].astype(jnp.float32) + right[at, :].astype(jnp.float32)
            target[at, :] = total.astype(target.dtype)

    pending = [None] * len(parts)
    loads = [None] * len(parts)
    for p, (start, width, order) in enumerate(parts):
        columns = pl.ds(start, width)
        every = list(range(near))
        pending[p] = pltpu.make_async_remote_copy(
            src_ref=shares.at[within(every, count, near, 1, columns)],
            dst_ref=near_in[p],
            send_sem=send_sem.at[p, 0],
            recv_sem=recv_sem.at[p, 0],
            device_id=partners[near],
            device_id_type=MESH,
        )
        pending[p].start()
        loads[p] = pltpu.make_async_copy(
            shares.at[within(every, count, near, 0, columns)], held[p], load_sem.at[p]
        )
        loads[p].start()
    for step in range(near):
        for p, (start, width, order) in enumerate(parts):
            turns = order[:-1][::-1]
            bit = turns[step]
            free = turns[step:]
            left = turns[step + 1 :]
            if step == 0:
                loads[p].wait()
            pending[p].wait()
            arrived = near_in[p] if step == 0 else came[p][step - 1]

            def merge(code):
                other = code if step == 0 else tuple(code[i] for i in sorted(free))
                add(held[p].at[code], held[p].at[code], arrived.at[other])

            for code in codes(free):
                if code[bit] == 1:
                    merge(code)
            lead = tuple(pl.ds(0, 2) if i in left else int(i == bit) for i in range(near))
            pending[p] = pltpu.make_async_remote_copy(
                src_ref=held[p].at[lead],
                dst_ref=came[p][step],
                send_sem=send_sem.at[p, step + 1],
                recv_sem=recv_sem.at[p, step + 1],
                device_id=partners[bit],
                device_id_type=MESH,
            )
            pending[p].start()
            for code in codes(free):
                if code[bit] == 0:
                    merge(code)
    for p, (start, width, order) in enumerate(parts):
        pending[p].wait()
        mine = (0,) * near
        out[:, pl.ds(start, width)] = held[p][mine].astype(jnp.float32) + came[p][near - 1][
            ...
        ].astype(jnp.float32)


def scatter_states(shares):
    bits = code_bits()
    parts = exchange_parts(bits)
    count = len(bits)
    low = jnp.bfloat16
    held = [pltpu.VMEM((2,) * (count - 1) + (TGT_LEN, width), low) for _, width, _ in parts]
    came = [
        [
            pltpu.VMEM((2,) * (count - 2 - step) + (TGT_LEN, width), low)
            for step in range(count - 1)
        ]
        for _, width, _ in parts
    ]
    return pl.pallas_call(
        functools.partial(scatter_kernel, bits, parts),
        out_shape=jax.ShapeDtypeStruct((TGT_LEN, D), jnp.float32),
        in_specs=[pl.BlockSpec(memory_space=pl.ANY)],
        out_specs=pl.BlockSpec(memory_space=pltpu.VMEM),
        scratch_shapes=[
            held,
            held,
            came,
            pltpu.SemaphoreType.DMA((len(parts),)),
            pltpu.SemaphoreType.DMA((len(parts), count)),
            pltpu.SemaphoreType.DMA((len(parts), count)),
        ],
        compiler_params=pltpu.CompilerParams(
            collective_id=3, has_side_effects=True, vmem_limit_bytes=56 << 20
        ),
    )(shares.reshape((2,) * count + (TGT_LEN, D)))


def merge_kernel(bits, stats, out, came, sent, send_sem, recv_sem):
    partners = [partner_of(bit) for bit in bits]
    meet(partners)
    count = len(bits)
    size = 1 << count
    out[...] = stats[...]
    position = lax.broadcasted_iota(jnp.int32, (size, TGT_LEN), 0)
    for step in range(count):
        mask = 1 << (count - 1 - step)
        sent[step] = out[...]
        copy = pltpu.make_async_remote_copy(
            src_ref=sent.at[step],
            dst_ref=came.at[step],
            send_sem=send_sem.at[step],
            recv_sem=recv_sem.at[step],
            device_id=partners[step],
            device_id_type=MESH,
        )
        copy.start()
        copy.wait()
        lower = (position // mask) % 2 == 0
        other = [
            jnp.where(
                lower,
                pltpu.roll(came[step, i], size - mask, 0),
                pltpu.roll(came[step, i], mask, 0),
            )
            for i in range(3)
        ]
        top = jnp.maximum(out[0], other[0])
        out[1] = out[1] * jnp.exp(out[0] - top) + other[1] * jnp.exp(other[0] - top)
        out[0] = top
        out[2] = out[2] + other[2]


def merge_stats(stats):
    bits = code_bits()
    shape = stats.shape
    return pl.pallas_call(
        functools.partial(merge_kernel, bits),
        out_shape=jax.ShapeDtypeStruct(shape, jnp.float32),
        in_specs=[pl.BlockSpec(memory_space=pltpu.VMEM)],
        out_specs=pl.BlockSpec(memory_space=pltpu.VMEM),
        scratch_shapes=[
            pltpu.VMEM((len(bits),) + shape, jnp.float32),
            pltpu.VMEM((len(bits),) + shape, jnp.float32),
            pltpu.SemaphoreType.DMA((len(bits),)),
            pltpu.SemaphoreType.DMA((len(bits),)),
        ],
        compiler_params=pltpu.CompilerParams(collective_id=4, has_side_effects=True),
    )(stats)


def weights_kernel(slots, groups, shards, vector, fact, fulls, vectors, facts, sems):
    holds, local_sem, send_sem, recv_sem, small_local, small_send, small_recv = sems
    slot, pb = lax.axis_index("slot"), lax.axis_index("pb")
    core, far = xor(pb, 1), xor(pb, 2)
    to_core, to_far = (slot, core), (slot, far)
    across = [(xor(slot, mask), pb) for mask in masks_below(slots)]
    meet([to_core, to_far] + across)

    jobs = []
    for shard, full in zip(shards, fulls):
        if len(shard.shape) == 3:
            for half in range(2):
                lead = pl.ds(half * (shard.shape[0] // 2), shard.shape[0] // 2)
                view = lambda ref, at, size, lead=lead: ref.at[lead, pl.ds(at, size)]
                jobs.append((shard, full, shard.shape[1], shard.shape[1], 0, view))
        elif shard.shape[1] > D:
            for half in range(2):
                lanes = pl.ds(half * (shard.shape[1] // 2), shard.shape[1] // 2)
                view = lambda ref, at, size, lanes=lanes: ref.at[pl.ds(at, size), lanes]
                jobs.append((shard, full, shard.shape[0], shard.shape[0], 0, view))
        else:
            for half in range(2):
                rows = shard.shape[0] // 2
                view = lambda ref, at, size: ref.at[pl.ds(at, size)]
                jobs.append((shard, full, shard.shape[0], rows, half * rows, view))

    def remote(source, target, job, kind, partner):
        return pltpu.make_async_remote_copy(
            src_ref=source,
            dst_ref=target,
            send_sem=send_sem.at[job, kind],
            recv_sem=recv_sem.at[job, kind],
            device_id=partner,
            device_id_type=MESH,
        )

    def describe(job):
        shard, full, block, rows, base, view = jobs[job]
        turn = job % 2
        first, second = (slot // (1 << turn)) % 2, (slot // (2 >> turn)) % 2
        to_first, to_second = across[turn], across[1 - turn]
        quarter, half = 3 * rows // 16, rows // 8
        split = base + 3 * rows // 4
        mine = pl.multiple_of(base + (second * 2 + first) * quarter, 16)
        pair = pl.multiple_of(base + second * 2 * quarter, 16)
        side = pl.multiple_of(split + second * half, 16)

        def there(owner, at):
            return pl.multiple_of(owner * block + at, 16)

        def send(kind, partner, owner, at, size, source=None):
            target = view(full, there(owner, at), size)
            return remote(target if source is None else source, target, job, kind, partner)

        own = view(shard, base, rows)
        stages = [
            [
                send(0, to_far, pb, mine, quarter, view(shard, mine, quarter)),
                send(1, to_far, pb, side, half, view(shard, side, half)),
                send(2, to_core, pb, base, rows, own),
            ],
            [
                send(3, to_first, far, mine, quarter),
                send(4, to_second, far, side, half),
            ],
            [send(5, to_second, far, pair, 2 * quarter)],
            [send(6, to_core, far, base, rows)],
        ]
        held = holds[job]
        into = pltpu.make_async_copy(own, held, local_sem.at[job, 0])
        onto = pltpu.make_async_copy(held, view(full, there(pb, base), rows), local_sem.at[job, 1])
        return stages, (into, onto)

    bits = [("pb", mask) for mask in masks_below(groups)] + [
        ("slot", mask) for mask in masks_below(slots)
    ]

    def small_copy(kind, source, target, partner):
        return pltpu.make_async_remote_copy(
            src_ref=source,
            dst_ref=target,
            send_sem=small_send.at[kind],
            recv_sem=small_recv.at[kind],
            device_id=partner,
            device_id_type=MESH,
        )

    def fact_copy(step):
        name, mask = bits[step]
        partner = (slot, xor(pb, mask)) if name == "pb" else (xor(slot, mask), pb)
        count = 1 << step
        source = fact if step == 0 else facts.at[pl.ds(0, count)]
        return small_copy(step, source, facts.at[pl.ds(count, count)], partner)

    near = len(bits)
    vector_copies = [
        small_copy(near, vector, vectors.at[pb], to_core),
        small_copy(near + 1, vector, vectors.at[pb], to_far),
    ]
    vector_last = small_copy(near + 2, vectors.at[far], vectors.at[far], to_core)
    small_own = [
        pltpu.make_async_copy(fact.at[0], facts.at[0], small_local.at[0]),
        pltpu.make_async_copy(vector, vectors.at[pb], small_local.at[1]),
    ]
    for copy in small_own + vector_copies:
        copy.start()
    plans = [describe(job) for job in range(len(jobs))]
    for step in range(max(len(jobs) + 4, len(bits) + 1)):
        for stage in range(5):
            job = step - stage
            if not 0 <= job < len(jobs):
                continue
            stages, (into, onto) = plans[job]
            if stage == 0:
                into.start()
            else:
                for copy in stages[stage - 1]:
                    copy.wait()
            if stage < 4:
                for copy in stages[stage]:
                    copy.start()
                if stage == 1:
                    into.wait()
                    onto.start()
            else:
                onto.wait()
        if step == 0:
            for copy in small_own:
                copy.wait()
        if step == 1:
            for copy in vector_copies:
                copy.wait()
            vector_last.start()
        if step == 2:
            vector_last.wait()
        if 0 < step <= len(bits):
            fact_copy(step - 1).wait()
        if step < len(bits):
            fact_copy(step).start()


def gather_weights(shards, vector, fact):
    slots, groups = lax.axis_size("slot"), lax.axis_size("pb")
    bits = (slots * groups).bit_length() - 1

    def widened(shard):
        axis = 1 if shard.ndim == 3 else 0
        shape = list(shard.shape)
        shape[axis] *= groups
        return jax.ShapeDtypeStruct(tuple(shape), shard.dtype)

    used = len(shards)

    def kernel(*refs):
        ins, outs, sems = refs[: used + 2], refs[used + 2 : 2 * used + 4], refs[2 * used + 4 :]
        weights_kernel(
            slots, groups, ins[:used], ins[used], ins[used + 1], outs[:used], outs[used],
            outs[used + 1], sems,
        )

    jobs = 2 * used
    holds = []
    for shard in shards:
        axis = 1 if shard.ndim == 2 and shard.shape[1] > D else 0
        shape = list(shard.shape)
        shape[axis] //= 2
        holds += [pltpu.VMEM(tuple(shape), shard.dtype)] * 2
    return pl.pallas_call(
        kernel,
        out_shape=[widened(shard) for shard in shards]
        + [
            jax.ShapeDtypeStruct((groups,) + vector.shape, vector.dtype),
            jax.ShapeDtypeStruct((slots * groups,) + fact.shape[1:], fact.dtype),
        ],
        in_specs=[pl.BlockSpec(memory_space=pl.ANY)] * (used + 2),
        out_specs=[pl.BlockSpec(memory_space=pl.ANY)] * (used + 2),
        scratch_shapes=[
            holds,
            pltpu.SemaphoreType.DMA((jobs, 2)),
            pltpu.SemaphoreType.DMA((jobs, 7)),
            pltpu.SemaphoreType.DMA((jobs, 7)),
            pltpu.SemaphoreType.DMA((2,)),
            pltpu.SemaphoreType.DMA((bits + 3,)),
            pltpu.SemaphoreType.DMA((bits + 3,)),
        ],
        compiler_params=pltpu.CompilerParams(
            collective_id=5, has_side_effects=True, vmem_limit_bytes=58 << 20
        ),
    )(*shards, vector, fact)


def own_facts(targets, owner, doc_scores):
    serving = jnp.arange(targets.shape[1]) == owner[0, 0]
    own = jnp.sum(jnp.where(serving[:, None], targets[0], 0), axis=0)
    half = (TGT_LEN // 2,)
    facts = [
        own.astype(jnp.float32),
        jnp.broadcast_to(owner[0, 0].astype(jnp.float32), half),
        jnp.broadcast_to(doc_scores[0, 0], half),
    ]
    return jnp.pad(jnp.concatenate(facts).reshape(1, 2, TGT_LEN), ((0, 0), (0, 6), (0, 0)))


def logit_kernel(states, embed, facts, logits_out, stats):
    logits = matmul_nt(states[...], embed[...])
    logits_out[...] = logits
    target = facts[...].T[:, 0:1]
    entry = lax.broadcasted_iota(jnp.int32, logits.shape, 1).astype(jnp.float32)
    top = jnp.max(logits, axis=1, keepdims=True)
    total = jnp.sum(jnp.exp(logits - top), axis=1, keepdims=True)
    pick = jnp.sum(jnp.where(entry == target, logits, 0.0), axis=1, keepdims=True)
    lane = lax.broadcasted_iota(jnp.int32, (logits.shape[0], 128), 1)
    stats[...] = jnp.where(lane == 0, top, jnp.where(lane == 1, total, pick)).T[:8]


def delta_kernel(logits, embed, facts, delta_out, grad_state):
    columns = facts[...].T
    target, weight, log_total = columns[:, 0:1], columns[:, 1:2], columns[:, 2:3]
    entry = lax.broadcasted_iota(jnp.int32, logits.shape, 1).astype(jnp.float32)
    onehot = jnp.where(entry == target, 1.0, 0.0)
    delta = to_low(weight * (onehot - jnp.exp(logits[...] - log_total)))
    delta_out[...] = delta
    grad_state[...] = to_low(matmul(delta, embed[...]))


def token_tiles(kernel, left, embed, facts, outs):
    tokens, tile = left.shape[0], 512
    tall = lambda width: pl.BlockSpec((tile, width), lambda i: (i, 0))
    wide = pl.BlockSpec((8, tile), lambda i: (0, i))
    return pl.pallas_call(
        kernel,
        grid=(tokens // tile,),
        out_shape=outs,
        in_specs=[tall(left.shape[1]), pl.BlockSpec(embed.shape, lambda i: (0, 0)), wide],
        out_specs=[wide if out.shape[0] == 8 else tall(out.shape[1]) for out in outs],
        compiler_params=pltpu.CompilerParams(vmem_limit_bytes=48 << 20),
    )(left, embed, facts)


def vocabulary_head(state_low, facts, questions, embed):
    slots, groups = lax.axis_size("slot"), lax.axis_size("pb")
    me = lax.axis_index("slot") * groups + lax.axis_index("pb")
    entries = embed.shape[0]
    tokens = slots * groups * TGT_LEN
    target_ids = (facts[:, 0] - (me * entries).astype(jnp.float32)).reshape(1, tokens)
    owners = facts[:, 1, 0].astype(jnp.int32).reshape(slots, groups)
    scores = facts[:, 1, TGT_LEN // 2].reshape(slots, groups)
    states = gather_states(state_low)
    logits, stats = token_tiles(
        logit_kernel,
        states,
        embed,
        jnp.pad(target_ids, ((0, 7), (0, 0))),
        [
            jax.ShapeDtypeStruct((tokens, entries), jnp.float32),
            jax.ShapeDtypeStruct((8, tokens), jnp.float32),
        ],
    )
    merged = merge_stats(stats[:3].reshape(3, -1, TGT_LEN))
    log_total = (merged[0] + jnp.log(merged[1])).reshape(tokens)
    picked = merged[2].reshape(slots, groups, TGT_LEN) - log_total.reshape(slots, groups, TGT_LEN)
    serving = owners[:, :, None] == jnp.arange(questions)
    score_terms = jnp.where(serving, scores[:, :, None], BIG_NEGATIVE)
    token_terms = jnp.where(
        serving[..., None], (scores[:, :, None] + picked)[:, :, None, :], BIG_NEGATIVE
    )
    score_top, token_top = jnp.max(score_terms, axis=0), jnp.max(token_terms, axis=0)
    score_norm = score_top + jnp.log(jnp.sum(jnp.exp(score_terms - score_top), axis=0))
    token_mix = token_top + jnp.log(jnp.sum(jnp.exp(token_terms - token_top), axis=0))
    group_tokens = questions * TGT_LEN
    count = groups * group_tokens
    losses = -jnp.sum(token_mix - score_norm[:, :, None], axis=(1, 2)) / group_tokens
    own_mix = jnp.sum(jnp.where(serving[..., None], token_mix[None], 0.0), axis=2)
    own_norm = jnp.sum(jnp.where(serving, score_norm[None], 0.0), axis=2)
    posterior = jnp.exp(scores[:, :, None] + picked - own_mix)
    prior = jnp.exp(scores - own_norm)
    token_grad = (-posterior / count).reshape(1, tokens)
    score_grads = -jnp.sum(posterior - prior[:, :, None], axis=2) / count
    known = jnp.concatenate([target_ids, token_grad, log_total.reshape(1, tokens)])
    delta, share = token_tiles(
        delta_kernel,
        logits,
        embed,
        jnp.pad(known, ((0, 5), (0, 0))),
        [
            jax.ShapeDtypeStruct((tokens, entries), jnp.bfloat16),
            jax.ShapeDtypeStruct((tokens, D), jnp.bfloat16),
        ],
    )
    grad_state = scatter_states(share)
    return (losses[:1], score_grads[:1, :1], grad_state, delta, states)


def local(
    enc_input,
    dec_input,
    doc_scores,
    owner,
    targets,
    enc_attn,
    enc_up,
    enc_down,
    enc_up_bias,
    enc_bias,
    enc_gain,
    dec_self,
    dec_cross,
    dec_up,
    dec_down,
    dec_up_bias,
    dec_bias,
    dec_gain,
    embed,
):
    pb_size = lax.axis_size("pb")
    width = D // pb_size
    vectors = (enc_up_bias, enc_bias, enc_gain, dec_up_bias, dec_bias, dec_gain)
    rows = [v.size // width for v in vectors]
    starts = [sum(rows[:i]) for i in range(len(rows) + 1)]
    passage_low = enc_input[0, 0]
    passage = passage_low.astype(jnp.float32)
    question_low = dec_input[0, 0]
    question = question_low.astype(jnp.float32)

    own_vectors = jnp.concatenate([v.reshape(-1, width) for v in vectors])
    (
        encoder_attn,
        encoder_up,
        encoder_down,
        decoder_self,
        decoder_cross,
        decoder_down,
        packed,
        facts,
    ) = gather_weights(
        (enc_attn, enc_up, enc_down, dec_self, dec_cross, dec_down),
        jnp.pad(own_vectors, ((0, -starts[-1] % 32), (0, 0))),
        own_facts(targets, owner, doc_scores),
    )
    packed, dec_up = lax.optimization_barrier((packed, dec_up))
    decoder_up = lax.all_gather(dec_up, "pb", axis=0, tiled=True)
    packed = packed.astype(jnp.float32)
    unpacked = [packed[:, starts[i] : starts[i + 1], :] for i in range(len(rows))]
    encoder_upbias = unpacked[0].reshape(-1)
    encoder_bias = unpacked[1].transpose(1, 0, 2).reshape(-1, D)
    encoder_gain = unpacked[2].transpose(1, 0, 2).reshape(-1, D)
    decoder_upbias = unpacked[3].reshape(-1)
    decoder_bias = unpacked[4].transpose(1, 0, 2).reshape(-1, D)
    decoder_gain = unpacked[5].transpose(1, 0, 2).reshape(-1, D)
    attn_out, enc_saved = attend_forward(
        passage_low,
        passage_low,
        encoder_attn,
        encoder_bias[0],
        encoder_bias[1],
        encoder_bias[2],
        False,
    )
    enc_first, enc_norm_one = norm_forward(passage + attn_out, encoder_gain[0], encoder_bias[3])
    enc_first_low = to_low(enc_first)
    enc_hidden, enc_slope = gelu_with_slope(matmul(enc_first_low, encoder_up) + encoder_upbias)
    enc_hidden_low = to_low(enc_hidden)
    ffn_out = matmul(enc_hidden_low, encoder_down) + encoder_bias[4]
    encoded, enc_norm_two = norm_forward(enc_first + ffn_out, encoder_gain[1], encoder_bias[5])
    memory_low = to_low(encoded)
    self_out, self_saved = attend_forward(
        question_low,
        question_low,
        decoder_self,
        decoder_bias[0],
        decoder_bias[1],
        decoder_bias[2],
        True,
    )
    dec_first, dec_norm_one = norm_forward(question + self_out, decoder_gain[0], decoder_bias[3])
    dec_first_low = to_low(dec_first)
    cross_out, cross_saved = attend_forward(
        dec_first_low,
        memory_low,
        decoder_cross,
        decoder_bias[4],
        decoder_bias[5],
        decoder_bias[6],
        False,
    )
    dec_second, dec_norm_two = norm_forward(dec_first + cross_out, decoder_gain[1], decoder_bias[7])
    dec_second_low = to_low(dec_second)
    dec_hidden, dec_slope = gelu_with_slope(matmul(dec_second_low, decoder_up) + decoder_upbias)
    dec_hidden_low = to_low(dec_hidden)
    dec_ffn_out = matmul(dec_hidden_low, decoder_down) + decoder_bias[8]
    state, dec_norm_three = norm_forward(dec_second + dec_ffn_out, decoder_gain[2], decoder_bias[9])
    state_low = to_low(state)

    loss, score_grad, grad_state_sum, delta, states = vocabulary_head(
        state_low, facts, targets.shape[1], embed
    )

    grad_third, gain_third, shift_third = norm_backward(
        grad_state_sum, dec_norm_three, decoder_gain[2]
    )
    dec_downbias_grad = jnp.sum(grad_third, axis=0)
    third_low = to_low(grad_third)
    grad_before = matmul_nt(third_low, decoder_down) * dec_slope
    dec_upbias_grad = jnp.sum(grad_before, axis=0)
    before_low = to_low(grad_before)
    grad_second, gain_second, shift_second = norm_backward(
        grad_third + matmul_nt(before_low, decoder_up), dec_norm_two, decoder_gain[1]
    )
    cross_query, grad_memory, dec_cross_pairs, cross_biases = attend_backward(
        grad_second, dec_first_low, memory_low, decoder_cross, cross_saved, False
    )
    grad_first, gain_first, shift_first = norm_backward(
        grad_second + cross_query, dec_norm_one, decoder_gain[0]
    )
    self_query, self_memory, dec_self_pairs, self_biases = attend_backward(
        grad_first, question_low, question_low, decoder_self, self_saved, True
    )
    question_grad = grad_first + self_query + self_memory
    enc_grad_two, enc_gain_two, enc_shift_two = norm_backward(
        grad_memory, enc_norm_two, encoder_gain[1]
    )
    enc_downbias_grad = jnp.sum(enc_grad_two, axis=0)
    enc_two_low = to_low(enc_grad_two)
    enc_grad_before = matmul_nt(enc_two_low, encoder_down) * enc_slope
    enc_upbias_grad = jnp.sum(enc_grad_before, axis=0)
    enc_before_low = to_low(enc_grad_before)
    enc_grad_one, enc_gain_one, enc_shift_one = norm_backward(
        enc_grad_two + matmul_nt(enc_before_low, encoder_up), enc_norm_one, encoder_gain[0]
    )
    enc_query, enc_memory, enc_attn_pairs, enc_biases = attend_backward(
        enc_grad_one, passage_low, passage_low, encoder_attn, enc_saved, False
    )
    passage_grad = enc_grad_one + enc_query + enc_memory
    operands, plan = [], []

    def share(left, right, tall=False):
        where = []
        for operand in (left, right):
            known = [i for i, other in enumerate(operands) if other is operand]
            where.append(known[0] if known else len(operands))
            if not known:
                operands.append(operand)
        for i in range(left.shape[1] * right.shape[1] // (D * D)):
            plan.append((where[0], where[1], i, tall))

    for left, right in enc_attn_pairs:
        share(left, right)
    share(enc_first_low, enc_before_low)
    share(enc_hidden_low, enc_two_low, tall=True)
    for left, right in dec_self_pairs + dec_cross_pairs:
        share(left, right)
    share(dec_second_low, before_low)
    share(dec_hidden_low, third_low, tall=True)
    enc_bias_grad = jnp.stack(
        [
            enc_biases[0],
            enc_biases[1],
            enc_biases[2],
            enc_shift_one,
            enc_downbias_grad,
            enc_shift_two,
        ]
    )
    enc_gain_grad = jnp.stack([enc_gain_one, enc_gain_two])
    dec_bias_grad = jnp.stack(
        [
            self_biases[0],
            self_biases[1],
            self_biases[2],
            shift_first,
            cross_biases[0],
            cross_biases[1],
            cross_biases[2],
            shift_second,
            dec_downbias_grad,
            shift_third,
        ]
    )
    dec_gain_grad = jnp.stack([gain_first, gain_second, gain_third])
    vector_grads = jnp.concatenate(
        [
            enc_upbias_grad.reshape(pb_size, -1, width),
            enc_bias_grad.reshape(-1, pb_size, width).transpose(1, 0, 2),
            enc_gain_grad.reshape(-1, pb_size, width).transpose(1, 0, 2),
            dec_upbias_grad.reshape(pb_size, -1, width),
            dec_bias_grad.reshape(-1, pb_size, width).transpose(1, 0, 2),
            dec_gain_grad.reshape(-1, pb_size, width).transpose(1, 0, 2),
        ],
        axis=1,
    )
    spare = -starts[-1] % 32
    small = jnp.pad(vector_grads, ((0, 0), (0, spare), (0, 0))).reshape(pb_size, -1, D)
    if lax.axis_size("slot") * 16 <= UNIT:
        summed_parts, small_sum, embed_grad = sync_gradients(
            plan, operands, small, (delta, states)
        )
    else:
        embed_grad = matmul_tn(delta, states)
        summed_parts, small_sum = sync_gradients(plan, operands, small)
    units = summed_parts.reshape(-1, width, D)
    square = lambda at: units[at : at + 4].astype(jnp.float32)
    wide = lambda at: jnp.concatenate([units[at + i].astype(jnp.float32) for i in range(4)], axis=1)
    tall = lambda at: square(at).reshape(-1, D)
    vector_sum = small_sum.reshape(-1, width)
    vector_out = [
        vector_sum[starts[i] : starts[i + 1]].reshape(v.shape) for i, v in enumerate(vectors)
    ]
    summed = (
        (square(0), wide(4), tall(8))
        + tuple(vector_out[:3])
        + (square(12), square(16), wide(20), tall(24))
        + tuple(vector_out[3:])
    )
    return (
        (
            loss,
            passage_grad.reshape(1, 1, SRC_LEN, D),
            question_grad.reshape(1, 1, TGT_LEN, D),
            score_grad,
        )
        + tuple(summed)
        + (embed_grad,)
    )


def solution(mesh):
    placed = (
        P("pb", "slot", None, None),
        P("pb", "slot", None, None),
        P("pb", "slot"),
        P("pb", "slot"),
        P("pb", None, None),
        P(None, "pb", None),
        P("pb", None),
        P("pb", None),
        P("pb"),
        P(None, "pb"),
        P(None, "pb"),
        P(None, "pb", None),
        P(None, "pb", None),
        P("pb", None),
        P("pb", None),
        P("pb"),
        P(None, "pb"),
        P(None, "pb"),
        P(("slot", "pb"), None),
    )
    return jax.shard_map(
        local,
        mesh=mesh,
        in_specs=placed,
        out_specs=(
            P("pb"),
            P("pb", "slot", None, None),
            P("pb", "slot", None, None),
            P("pb", "slot"),
            P(None, "pb", None),
            P("pb", None),
            P("pb", None),
            P("pb"),
            P(None, "pb"),
            P(None, "pb"),
            P(None, "pb", None),
            P(None, "pb", None),
            P("pb", None),
            P("pb", None),
            P("pb"),
            P(None, "pb"),
            P(None, "pb"),
            P(("slot", "pb"), None),
        ),
        check_vma=False,
    )
```
